512 devices in a mesh: dp: 128 (over z_hi, x, y, core), width: 4 (over z_lo).
Axes of the slice: x: 4, y: 4, z: 16 (z_hi: 4, z_lo: 4; z = z_hi * 4 + z_lo), core: 2. Of those that a mesh axis runs over, the one named last changes fastest.
Arguments:
- image: bfloat16 [16384, 1152], P('dp', 'width'), may hold values from -4 to 4
- text: bfloat16 [16384, 1152], P('dp', 'width'), may hold values from -8 to 8
- log_temp: float32 [], replicated, may hold values from 2.7 to 2.9
- bias: float32 [], replicated, may hold values from -8 to -7
Outputs:
- loss: float32 [], replicated
- grad_image: bfloat16 [16384, 1152], P('dp', 'width')
- grad_text: bfloat16 [16384, 1152], P('dp', 'width')
- grad_log_temp: float32 [], replicated
- grad_bias: float32 [], replicated
The draws below stay inside these ranges and needn't reach their ends.
All inputs are finite; a program needn't handle non-finite values.
Results may differ from the reference program's by a relative error of at most 0.0052.
Values may be sent and summed in bfloat16 or wider, within the bound.
No kernel may reach another device: no remote copies, remote signals or barrier semaphores. Data moves between devices by JAX's collectives and lax.ppermute only.
A program may use at most 64 MiB of HBM per device.

```python
import math
import jax
import jax.numpy as jnp
from jax import lax

D = 1152
BATCH = 16384


def group_centres(key, groups):
    centre_key, member_key = jax.random.split(key, 2)
    centres = jnp.clip(jax.random.normal(centre_key, (groups, D), jnp.float32), -6.0, 6.0)
    members = jax.random.randint(member_key, (BATCH,), 0, groups)
    return jnp.take(centres, members, axis=0)


def shared_parts(key):
    base_key, tight_key, middle_key, loose_key = jax.random.split(key, 4)
    base = jnp.clip(jax.random.normal(base_key, (BATCH, D), jnp.float32), -6.0, 6.0)
    tight = group_centres(tight_key, max(BATCH // 4, 2))
    middle = group_centres(middle_key, max(BATCH // 32, 2))
    loose = group_centres(loose_key, max(BATCH // 512, 2))
    return (base, (tight, middle, loose))


def row_lengths(key, low, high):
    return jnp.exp(jax.random.uniform(key, (BATCH, 1), jnp.float32, jnp.log(low), jnp.log(high)))


def row_position():
    return jnp.arange(BATCH, dtype=jnp.float32)[:, None]


def blend_rows(key, own, centres, limits):
    share_keys = jax.random.split(key, 3)
    mixed = jnp.zeros((BATCH, D), jnp.float32)
    remain = jnp.ones((BATCH, 1), jnp.float32)
    for index in range(3):
        share = jax.random.uniform(share_keys[index], (BATCH, 1), jnp.float32, limits[index][0], limits[index][1])
        mixed = mixed + jnp.sqrt(share) * centres[index]
        remain = remain - share
    return mixed + jnp.sqrt(remain) * own


def draw_image(key, part):
    base, centres = shared_parts(key)
    key = jax.random.fold_in(key, 11)
    blend_key, length_key = jax.random.split(key, 2)
    mixed = blend_rows(blend_key, base, centres, ((0.2, 0.45), (0.1, 0.22), (0.03, 0.08)))
    lengths = row_lengths(length_key, 0.3, 3.0)
    return (mixed * lengths / jnp.sqrt(jnp.float32(D))).astype(jnp.bfloat16)


def draw_text(key, part):
    base, centres = shared_parts(key)
    key = jax.random.fold_in(key, 23)
    noise_key = jax.random.fold_in(key, 0)
    length_key = jax.random.fold_in(key, 1)
    blend_key = jax.random.fold_in(key, 3)
    mixing = 0.15 + 0.8 * row_position() / max(BATCH - 1, 1)
    noise = jnp.clip(jax.random.normal(noise_key, (BATCH, D), jnp.float32), -6.0, 6.0)
    own = mixing * base + jnp.sqrt(1.0 - mixing * mixing) * noise
    mixed = blend_rows(blend_key, own, centres, ((0.2, 0.45), (0.1, 0.22), (0.03, 0.08)))
    lengths = row_lengths(length_key, 0.3, 3.0)
    return (mixed * lengths / jnp.sqrt(jnp.float32(D))).astype(jnp.bfloat16)


def setup_inputs(seed: int = 0) -> dict:
    keys = jax.random.split(jax.random.key(seed), 5)
    return {
        "image": draw_image(jax.random.fold_in(keys[4], 71), 0),
        "text": draw_text(jax.random.fold_in(keys[4], 71), 0),
        "log_temp": jnp.clip(jax.random.uniform(keys[2], (), jnp.float32, 2.7, 2.9), 2.7, 2.9),
        "bias": jnp.clip(jax.random.uniform(keys[3], (), jnp.float32, -8.0, -7.0), -8.0, -7.0),
    }


epsilon = 1e-06

def unit_rows(rows_in):
    values = rows_in.astype(jnp.float32)
    inverse = lax.rsqrt(lax.optimization_barrier(jnp.sum(values * values, axis=1, keepdims=True)) + epsilon)
    return (values * inverse, inverse)

def block_terms(left, right, first_left, first_right, scale, bias):
    product = lax.dot_general(left, right, (((1,), (1,)), ((), ())), preferred_element_type=jnp.float32)
    logits = scale * product + bias
    left_ids = first_left + lax.iota(jnp.int32, left.shape[0])
    right_ids = first_right + lax.iota(jnp.int32, right.shape[0])
    signs = jnp.where(left_ids[:, None] == right_ids[None, :], 1.0, -1.0).astype(jnp.float32)
    slope = -signs * jax.nn.sigmoid(-signs * logits)
    weights = (scale * slope).astype(jnp.bfloat16)
    sums = (jnp.sum(jax.nn.softplus(-signs * logits)), jnp.sum(slope * product) * scale, jnp.sum(slope))
    return (weights, sums)

def unit_back(grad, unit, inverse):
    return (grad - unit * lax.optimization_barrier(jnp.sum(unit * grad, axis=1, keepdims=True))) * inverse

def reference(image, text, log_temp, bias):
    image_unit, image_inverse = unit_rows(image)
    text_unit, text_inverse = unit_rows(text)
    image_half = image_unit.astype(jnp.bfloat16)
    text_half = text_unit.astype(jnp.bfloat16)
    scale = jnp.exp(log_temp)
    span = math.gcd(BATCH, 512)

    def step(carry, index):
        grad_text, loss_total, temp_total, bias_total = carry
        start = (index * span).astype(jnp.int32)
        rows_here = lax.dynamic_slice_in_dim(image_half, start, span, 0)
        weights, sums = block_terms(rows_here, text_half, start, jnp.int32(0), scale, bias)
        grad_rows = jnp.dot(weights, text_half, preferred_element_type=jnp.float32)
        grad_text = grad_text + jnp.dot(weights.T, rows_here, preferred_element_type=jnp.float32)
        return ((grad_text, loss_total + sums[0], temp_total + sums[1], bias_total + sums[2]), grad_rows)
    nothing = jnp.zeros((), jnp.float32)
    start_carry = (jnp.zeros((BATCH, D), jnp.float32), nothing, nothing, nothing)
    carry, grad_blocks = lax.scan(step, start_carry, jnp.arange(BATCH // span, dtype=jnp.int32))
    grad_text_unit, loss_total, temp_total, bias_total = carry
    grad_image_unit = grad_blocks.reshape(BATCH, D)
    grad_image = unit_back(grad_image_unit, image_unit, image_inverse).astype(jnp.bfloat16)
    grad_text = unit_back(grad_text_unit, text_unit, text_inverse).astype(jnp.bfloat16)
    return (loss_total / BATCH, grad_image, grad_text, temp_total / BATCH, bias_total / BATCH)
```

```python
import functools
import math

import jax
import jax.numpy as jnp
from jax import lax
from jax.experimental import pallas as pl
from jax.experimental.pallas import tpu as pltpu
from jax.sharding import Mesh, PartitionSpec as P

epsilon = 1e-06
log2e = 1.0 / math.log(2.0)


def unit_rows(rows_in):
    values = rows_in.astype(jnp.float32)
    inverse = lax.rsqrt(jnp.sum(values * values, axis=1, keepdims=True) + epsilon)
    return (values * inverse, inverse)


def unit_back(grad, unit, inverse):
    return (grad - unit * jnp.sum(unit * grad, axis=1, keepdims=True)) * inverse


def fold(values):
    rows, columns = values.shape
    part = jnp.sum(values.reshape(rows // 8, 8, columns), axis=0)
    return sum(part[:, c : c + 128] for c in range(0, columns, 128))


def pair_kernel(params, left_ids, right_ids, left, right, back, weights_out, sums_out):
    scale = params[0]
    bias = params[1]
    rows = left.shape[0]
    tile = 256
    loss_sum = jnp.zeros((8, 128), jnp.float32)
    temp_sum = jnp.zeros((8, 128), jnp.float32)
    bias_sum = jnp.zeros((8, 128), jnp.float32)
    for start in range(0, rows, tile):
        here = pl.ds(start, tile)
        product = lax.dot_general(
            left[here, :], right[...], (((1,), (1,)), ((), ())), preferred_element_type=jnp.float32
        )
        logits = scale * product + bias
        same = left_ids[here, :] == right_ids[...]
        turned = jnp.where(same, -logits, logits)
        grown = jnp.exp(turned)
        share = grown / (1.0 + grown)
        slope = jnp.where(same, -share, share)
        weights = (scale * slope).astype(jnp.bfloat16)
        weights_out[here, :] = weights
        back[here, :] = jnp.dot(
            weights, right[...], preferred_element_type=jnp.float32
        ).astype(jnp.bfloat16)
        quarter = tile // 4
        a, b, c, d = (grown[k * quarter : (k + 1) * quarter, :] for k in range(4))
        ab = a + (b + a * b)
        cd = c + (d + c * d)
        loss_sum += fold(jnp.log1p(ab + (cd + ab * cd)))
        temp_sum += fold(slope * product)
        bias_sum += fold(slope)
    sums_out[0:8, :] = loss_sum
    sums_out[8:16, :] = temp_sum
    sums_out[16:24, :] = bias_sum


def pair_block(params, left_ids, right_ids, left, right):
    rows, width = left.shape
    columns = right.shape[0]
    vmem = pl.BlockSpec(memory_space=pltpu.VMEM)
    return pl.pallas_call(
        pair_kernel,
        out_shape=(
            jax.ShapeDtypeStruct((rows, width), jnp.bfloat16),
            jax.ShapeDtypeStruct((rows, columns), jnp.bfloat16),
            jax.ShapeDtypeStruct((24, 128), jnp.float32),
        ),
        in_specs=[pl.BlockSpec(memory_space=pltpu.SMEM)] + [vmem] * 4,
        out_specs=(vmem, vmem, vmem),
        compiler_params=pltpu.CompilerParams(vmem_limit_bytes=48 * 1024 * 1024),
        cost_estimate=pl.CostEstimate(
            flops=4 * rows * columns * width,
            bytes_accessed=6 * rows * width,
            transcendentals=2 * rows * columns,
        ),
        name="pair_block",
    )(params, left_ids, right_ids, left, right)


def text_kernel(first_weights, second_weights, first, second, back):
    contract = (((0,), (0,)), ((), ()))
    total = lax.dot_general(
        first_weights[...], first[...], contract, preferred_element_type=jnp.float32
    ) + lax.dot_general(
        second_weights[...], second[...], contract, preferred_element_type=jnp.float32
    )
    back[...] = total.astype(jnp.bfloat16)


def text_block(first_weights, second_weights, first, second):
    rows, width = first.shape
    columns = first_weights.shape[1]
    vmem = pl.BlockSpec(memory_space=pltpu.VMEM)
    return pl.pallas_call(
        text_kernel,
        out_shape=jax.ShapeDtypeStruct((columns, width), jnp.bfloat16),
        in_specs=[vmem] * 4,
        out_specs=vmem,
        compiler_params=pltpu.CompilerParams(vmem_limit_bytes=48 * 1024 * 1024),
        cost_estimate=pl.CostEstimate(
            flops=4 * rows * columns * width,
            bytes_accessed=8 * rows * width,
            transcendentals=0,
        ),
        name="text_block",
    )(first_weights, second_weights, first, second)


def spread(rows, axis):
    count = lax.axis_size(axis)
    return lax.all_to_all(jnp.broadcast_to(rows[None], (count,) + rows.shape), axis, 0, 0)


def swap_core(value):
    return lax.ppermute(value, "core", [(0, 1), (1, 0)])


def total_over(value, axis):
    count = lax.axis_size(axis)
    parts = lax.all_to_all(jnp.broadcast_to(value[None], (count,) + value.shape), axis, 0, 0)
    return jnp.sum(parts, axis=0)


def shards(image, text, log_temp, bias):
    rows, strip = image.shape
    zl_count = lax.axis_size("zl")
    zh_count = lax.axis_size("zh")
    x_count = lax.axis_size("x")
    y_count = lax.axis_size("y")
    width = strip * zl_count
    piece = rows // zl_count
    zh, x, y, core, zl = (lax.axis_index(name) for name in ("zh", "x", "y", "core", "zl"))
    scale = jnp.exp(log_temp)

    packed = jnp.concatenate(
        [
            image.reshape(zl_count, piece, strip),
            jnp.broadcast_to(text[None], (zl_count, rows, strip)),
        ],
        axis=1,
    )
    arrived = lax.all_to_all(packed, "zl", 0, 0)
    image_own = arrived[:, :piece].transpose(1, 0, 2).reshape(piece, width)
    text_own = arrived[:, piece:].transpose(1, 0, 2).reshape(rows, width)
    image_unit, image_inverse = unit_rows(image_own)
    text_unit, text_inverse = unit_rows(text_own)

    image_rows = spread(image_unit.astype(jnp.bfloat16), "zh").reshape(zh_count * piece, width)
    text_rows = spread(text_unit.astype(jnp.bfloat16), "y").reshape(y_count * rows, width)
    image_rows = spread(image_rows, "x").reshape(x_count * zh_count * piece, width)
    other_rows = swap_core(image_rows)

    count = image_rows.shape[0]
    left_spot = lax.iota(jnp.int32, count) - (x * zh_count + zh) * piece
    left_ids = jnp.where((left_spot >= 0) & (left_spot < piece), left_spot, -1)[:, None]
    right_ids = (lax.iota(jnp.int32, y_count * rows) - (y * rows + zl * piece))[None, :]
    right_ids = jnp.where(right_ids >= 0, right_ids, -2)
    none_ids = jnp.full_like(left_ids, -1)
    params = jnp.stack([scale, bias])

    own_back, own_weights, own_sums = pair_block(params, left_ids, right_ids, image_rows, text_rows)
    other_back, other_weights, other_sums = pair_block(
        params, none_ids, right_ids, other_rows, text_rows
    )
    given_back = swap_core(other_back)
    text_back = text_block(own_weights, other_weights, image_rows, other_rows)

    sums = jnp.sum((own_sums + other_sums).reshape(3, 8, 128), axis=1)
    sums = total_over(sums, ("x", "y"))
    sums = total_over(sums, ("zh", "zl"))
    sums = jnp.sum(sums, axis=1)
    sums = sums + swap_core(sums)

    image_back = (own_back.astype(jnp.float32) + given_back.astype(jnp.float32)).astype(jnp.bfloat16)
    image_back = lax.all_to_all(image_back.reshape(x_count, zh_count * piece, width), "x", 0, 0)
    image_back = jnp.sum(image_back.astype(jnp.float32), axis=0).astype(jnp.bfloat16)
    image_back = lax.all_to_all(image_back.reshape(zh_count, piece, width), "zh", 0, 0)
    image_back = jnp.sum(image_back.astype(jnp.float32), axis=0)
    text_back = lax.all_to_all(text_back.reshape(y_count, rows, width), "y", 0, 0)
    text_back = jnp.sum(text_back.astype(jnp.float32), axis=0)

    image_final = unit_back(image_back, image_unit, image_inverse).astype(jnp.bfloat16)
    text_final = unit_back(text_back, text_unit, text_inverse).astype(jnp.bfloat16)
    packed = jnp.concatenate([image_final, text_final], axis=0)
    packed = packed.reshape(piece + rows, zl_count, strip).transpose(1, 0, 2)
    arrived = lax.all_to_all(packed, "zl", 0, 0)
    grad_image = arrived[:, :piece].reshape(rows, strip)
    grad_text = jnp.sum(arrived[:, piece:].astype(jnp.float32), axis=0).astype(jnp.bfloat16)

    pairs_count = rows * zh_count * x_count * y_count * 2
    return (
        sums[0] / pairs_count,
        grad_image,
        grad_text,
        scale * sums[1] / pairs_count,
        sums[2] / pairs_count,
    )


def solution(mesh):
    fine = Mesh(mesh.devices.reshape(4, 4, 4, 2, 4), ("zh", "x", "y", "core", "zl"))
    whole = P(("zh", "x", "y", "core"), "zl")
    return jax.shard_map(
        shards,
        mesh=fine,
        in_specs=(whole, whole, P(), P()),
        out_specs=(P(), whole, whole, P(), P()),
        check_vma=False,
    )
```

```python
import functools

import jax
import jax.numpy as jnp
from jax import lax
from jax.experimental import pallas as pl
from jax.experimental.pallas import tpu as pltpu
from jax.sharding import Mesh, PartitionSpec as P

epsilon = 1e-06
lanes = 128
piece = 32
strips = 4
rest = 32
packed_rows = 72
carry_rows = 80
tiles = 9
vmem = pl.BlockSpec(memory_space=pltpu.VMEM)
smem = pl.BlockSpec(memory_space=pltpu.SMEM)


def call(kernel, out_shape, name, flops=0, special=0, specs=None):
    def run(*operands):
        moved = sum(a.size * a.dtype.itemsize for a in operands)
        moved += sum(a.size * a.dtype.itemsize for a in jax.tree.leaves(out_shape))
        return pl.pallas_call(
            kernel,
            out_shape=out_shape,
            in_specs=specs or [vmem] * len(operands),
            out_specs=jax.tree.map(lambda _: vmem, out_shape),
            compiler_params=pltpu.CompilerParams(vmem_limit_bytes=40 * 1024 * 1024),
            cost_estimate=pl.CostEstimate(
                flops=flops, bytes_accessed=moved, transcendentals=special
            ),
            name=name,
        )(*operands)

    return run


def shape(dims, dtype=jnp.bfloat16):
    return jax.ShapeDtypeStruct(dims, dtype)


def lane_group():
    return lax.broadcasted_iota(jnp.int32, (8, lanes), 1) // rest


def pack_kernel(image, out):
    count = out.shape[0] // strips
    for k in range(strips):
        rows = image[k * piece : (k + 1) * piece, :].astype(jnp.float32)
        last = rows[:, 2 * lanes :]
        last = jnp.concatenate([last[8 * g : 8 * g + 8] for g in range(4)], axis=1)
        chunk = jnp.concatenate([rows[:, :lanes], rows[:, lanes : 2 * lanes], last], axis=0)
        chunk = chunk.astype(jnp.bfloat16)
        for d in range(count):
            out[d * strips + k] = chunk


def unpack_rows(chunks, group):
    found = []
    lasts = []
    for chunk in chunks:
        found += [chunk[:piece], chunk[piece : 2 * piece]]
        lasts.append(chunk[2 * piece : 2 * piece + 8])
    last = []
    for g in range(4):
        value = jnp.zeros((8, lanes), jnp.float32)
        for s in range(strips):
            turn = rest * (s - g) % lanes
            moved = pltpu.roll(lasts[s], turn, 1) if turn else lasts[s]
            value = jnp.where(group == s, moved, value)
        last.append(value)
    found.append(jnp.concatenate(last, axis=0))
    return found


def unit_tiles(chunks, group):
    found = unpack_rows(chunks, group)
    squares = functools.reduce(lambda a, b: a + b, [t * t for t in found])
    inverse = lax.rsqrt(jnp.sum(squares, axis=1, keepdims=True) + epsilon)
    return [t * inverse for t in found], inverse


def read_chunks(arrived, h):
    return [arrived[h * strips + s].astype(jnp.float32) for s in range(strips)]


def unit_kernel(arrived, out):
    group = lane_group()
    for h in range(arrived.shape[0] // strips):
        units, _ = unit_tiles(read_chunks(arrived, h), group)
        for t in range(tiles):
            value = units[t].astype(jnp.bfloat16)
            for k in range(out.shape[0]):
                out[k, h * piece : (h + 1) * piece, t * lanes : (t + 1) * lanes] = value


def fold(values):
    rows, columns = values.shape
    part = jnp.sum(values.reshape(rows // 8, 8, columns), axis=0)
    return sum(part[:, c : c + lanes] for c in range(0, columns, lanes))


def pair_kernel(own, scales, spots, left, t0, t1, t2, t3, *rest_refs):
    if own:
        back, weights_out, sums_out, right = rest_refs
    else:
        first_sums, back, weights_out, sums_out, right = rest_refs
    scale = scales[0]
    bias = scales[1]
    rows = left.shape[0]
    part = t0.shape[0]
    for k, ref in enumerate((t0, t1, t2, t3)):
        right[k * part : (k + 1) * part, :] = ref[...]
    columns = 4 * part
    tile = 256
    loss_sum = jnp.zeros((8, lanes), jnp.float32)
    temp_sum = jnp.zeros((8, lanes), jnp.float32)
    bias_sum = jnp.zeros((8, lanes), jnp.float32)
    for start in range(0, rows, tile):
        here = pl.ds(start, tile)
        product = lax.dot_general(
            left[here, :], right[...], (((1,), (1,)), ((), ())), preferred_element_type=jnp.float32
        )
        logits = scale * product + bias
        if own:
            row = lax.broadcasted_iota(jnp.int32, (tile, 1), 0) + (start - spots[0])
            row = jnp.where((row >= 0) & (row < piece), row, -1)
            column = lax.broadcasted_iota(jnp.int32, (1, columns), 1) - spots[1]
            column = jnp.where(column >= 0, column, -2)
            same = row == column
            grown = jnp.exp(jnp.where(same, -logits, logits))
            share = grown / (1.0 + grown)
            slope = jnp.where(same, -share, share)
        else:
            grown = jnp.exp(logits)
            slope = grown / (1.0 + grown)
        weights = (scale * slope).astype(jnp.bfloat16)
        weights_out[here, :] = weights
        back[here, :] = jnp.dot(
            weights, right[...], preferred_element_type=jnp.float32
        ).astype(jnp.bfloat16)
        quarter = tile // 4
        a, b, c, d = (grown[k * quarter : (k + 1) * quarter, :] for k in range(4))
        ab = a + (b + a * b)
        cd = c + (d + c * d)
        loss_sum += fold(jnp.log1p(ab + (cd + ab * cd)))
        temp_sum += fold(slope * product)
        bias_sum += fold(slope)
    if own:
        sums_out[0:8, :] = loss_sum
        sums_out[8:16, :] = temp_sum
        sums_out[16:24, :] = bias_sum
    else:
        sums = []
        for k, found in enumerate((loss_sum, temp_sum, bias_sum)):
            sums.append(jnp.sum(found + first_sums[8 * k : 8 * k + 8, :], axis=0, keepdims=True))
        row = lax.broadcasted_iota(jnp.int32, (8, lanes), 0)
        total = jnp.where(
            row == 0, sums[0], jnp.where(row == 1, sums[1], jnp.where(row == 2, sums[2], 0.0))
        )
        for k in range(sums_out.shape[0]):
            sums_out[k] = total


def pair_block(own, scales, spots, left, texts, first_sums=None, copies=0):
    rows, width = left.shape
    columns = 4 * texts[0].shape[0]
    sums = shape((24, lanes), jnp.float32) if own else shape((copies, 8, lanes), jnp.float32)
    operands = [scales, spots, left] + list(texts) + ([] if own else [first_sums])
    moved = sum(a.size * a.dtype.itemsize for a in operands) * 2
    return pl.pallas_call(
        functools.partial(pair_kernel, own),
        out_shape=(shape((rows, width)), shape((rows, columns)), sums),
        in_specs=[smem, smem] + [vmem] * (len(operands) - 2),
        out_specs=(vmem, vmem, vmem),
        scratch_shapes=[pltpu.VMEM((columns, width), jnp.bfloat16)],
        compiler_params=pltpu.CompilerParams(vmem_limit_bytes=40 * 1024 * 1024),
        cost_estimate=pl.CostEstimate(
            flops=4 * rows * columns * width,
            bytes_accessed=moved,
            transcendentals=2 * rows * columns,
        ),
        name="pair_own" if own else "pair_other",
    )(*operands)


def text_kernel(first_weights, second_weights, first, second, *backs):
    contract = (((0,), (0,)), ((), ()))
    part = backs[0].shape[0]
    total = lax.dot_general(
        first_weights[...], first[...], contract, preferred_element_type=jnp.float32
    ) + lax.dot_general(
        second_weights[...], second[...], contract, preferred_element_type=jnp.float32
    )
    for k, back in enumerate(backs):
        back[...] = total[k * part : (k + 1) * part].astype(jnp.bfloat16)


def three_parts(value):
    high = value.astype(jnp.bfloat16).astype(jnp.float32)
    middle = (value - high).astype(jnp.bfloat16).astype(jnp.float32)
    return high, middle, value - high - middle


def combine_kernel(own, given, sums, out):
    count, total_rows, _ = out.shape
    block = own.shape[0] // count
    value = functools.reduce(lambda a, b: a + b, [sums[k] for k in range(sums.shape[0])])
    carried = jnp.concatenate(
        list(three_parts(value)) + [jnp.zeros((8, lanes), jnp.float32)], axis=0
    ).astype(jnp.bfloat16)
    for k in range(count):
        for t in range(tiles):
            rows = pl.ds(k * block, block)
            columns = pl.ds(t * lanes, lanes)
            value = own[rows, columns].astype(jnp.float32) + given[rows, columns].astype(jnp.float32)
            out[k, t * block : (t + 1) * block, :] = value.astype(jnp.bfloat16)
        out[k, tiles * block : total_rows, :] = carried


def finish_kernel(arrived, backs, out):
    group = lane_group()
    count = backs.shape[0]
    heads = arrived.shape[0] // strips
    block = heads * piece
    tail = tiles * block
    add = lambda a, b: a + b
    carried = functools.reduce(
        add, [backs[k, tail : tail + piece, :].astype(jnp.float32) for k in range(count)]
    )
    value = jnp.sum(carried[0:8] + carried[8:16] + carried[16:24], axis=1, keepdims=True)
    parts = three_parts(value)
    lane = lax.broadcasted_iota(jnp.int32, (8, lanes), 1)
    carry = jnp.zeros((8, lanes), jnp.float32)
    for k in range(3):
        carry = jnp.where(lane == k, parts[k], carry)
    for h in range(heads):
        units, inverse = unit_tiles(read_chunks(arrived, h), group)
        grads = []
        for t in range(tiles):
            start = t * block + h * piece
            grads.append(
                functools.reduce(
                    add,
                    [backs[k, start : start + piece, :].astype(jnp.float32) for k in range(count)],
                )
            )
        along = jnp.sum(
            functools.reduce(add, [u * g for u, g in zip(units, grads)]), axis=1, keepdims=True
        )
        final = [(g - u * along) * inverse for u, g in zip(units, grads)]
        for s in range(strips):
            last = jnp.zeros((8, lanes), jnp.float32)
            for g in range(4):
                turn = rest * (g - s) % lanes
                rows = final[tiles - 1][8 * g : 8 * g + 8]
                moved = pltpu.roll(rows, turn, 1) if turn else rows
                last = jnp.where(group == g, moved, last)
            chunk = jnp.concatenate([final[2 * s], final[2 * s + 1], last, carry], axis=0)
            out[h * strips + s] = chunk.astype(jnp.bfloat16)


def last_kernel(arrived, out, sums_out):
    heads = arrived.shape[0] // strips
    sums = jnp.zeros((8, lanes), jnp.float32)
    for s in range(strips):
        chunk = functools.reduce(
            lambda a, b: a + b,
            [arrived[h * strips + s].astype(jnp.float32) for h in range(heads)],
        )
        rows = pl.ds(s * piece, piece)
        out[rows, 0:lanes] = chunk[:piece].astype(jnp.bfloat16)
        out[rows, lanes : 2 * lanes] = chunk[piece : 2 * piece].astype(jnp.bfloat16)
        last = chunk[2 * piece : 2 * piece + 8]
        groups = [last] + [pltpu.roll(last, lanes - rest * g, 1) for g in range(1, 4)]
        value = jnp.concatenate(groups, axis=0)[:, :rest]
        out[rows, 2 * lanes : 2 * lanes + rest] = value.astype(jnp.bfloat16)
        sums = sums + chunk[2 * piece + 8 :]
    sums_out[...] = jnp.broadcast_to(jnp.sum(sums, axis=1, keepdims=True), sums.shape)


def swap_core(value):
    return lax.ppermute(value, "core", [(0, 1), (1, 0)])


def shift(value, axis, k):
    count = lax.axis_size(axis)
    return lax.ppermute(value, axis, [(i, (i + k) % count) for i in range(count)])


def shards(image, text, log_temp, bias):
    rows, strip = image.shape
    zh_count, x_count, y_count = (lax.axis_size(name) for name in ("zh", "x", "y"))
    width = strip * strips
    z_count = zh_count * strips
    block = zh_count * piece
    zh, x, zl = (lax.axis_index(name) for name in ("zh", "x", "zl"))
    scale = jnp.exp(log_temp)
    scales = jnp.stack([scale, bias])
    spots = jnp.stack([(x * zh_count + zh) * piece, zl * piece]).astype(jnp.int32)

    packed = call(pack_kernel, shape((z_count, packed_rows, lanes)), "pack")(image)
    image_chunks = lax.all_to_all(packed, ("zh", "zl"), 0, 0)

    found = lax.all_gather(text, "zl", axis=0)
    text_own = jnp.concatenate(
        [found[s, :, : 2 * lanes] for s in range(strips)]
        + [found[s, :, 2 * lanes :] for s in range(strips)],
        axis=1,
    ).astype(jnp.float32)
    text_inverse = lax.rsqrt(jnp.sum(text_own * text_own, axis=1, keepdims=True) + epsilon)
    text_unit = text_own * text_inverse
    text_half = text_unit.astype(jnp.bfloat16)
    texts = [text_half] + [shift(text_half, "y", k) for k in range(1, y_count)]

    units = call(unit_kernel, shape((x_count, block, width)), "unit")(image_chunks)
    image_rows = lax.all_to_all(units, "x", 0, 0).reshape(x_count * block, width)
    other_rows = swap_core(image_rows)

    own_back, own_weights, own_sums = pair_block(True, scales, spots, image_rows, texts)
    other_back, other_weights, sums = pair_block(
        False, scales, spots, other_rows, texts, own_sums, y_count * 2
    )
    given_back = swap_core(other_back)
    sums = lax.all_to_all(sums, ("y", "core"), 0, 0)
    text_backs = call(
        text_kernel,
        tuple(shape((rows, width)) for _ in range(y_count)),
        "text_back",
        flops=4 * image_rows.size * own_weights.shape[1],
    )(own_weights, other_weights, image_rows, other_rows)

    combined = call(combine_kernel, shape((x_count, tiles * block + piece, lanes)), "combine")(
        own_back, given_back, sums
    )
    combined = lax.all_to_all(combined, "x", 0, 0)
    finished = call(finish_kernel, shape((z_count, carry_rows, lanes)), "finish")(
        image_chunks, combined
    )
    finished = lax.all_to_all(finished, ("zh", "zl"), 0, 0)
    grad_image, sums = call(
        last_kernel, (shape((rows, strip)), shape((8, lanes), jnp.float32)), "last"
    )(finished)

    text_back = text_backs[0].astype(jnp.float32)
    for k in range(1, y_count):
        text_back = text_back + shift(text_backs[k], "y", -k).astype(jnp.float32)
    along = jnp.sum(text_unit * text_back, axis=1, keepdims=True)
    text_final = (text_back - text_unit * along) * text_inverse
    text_final = text_final.astype(jnp.bfloat16)
    text_strips = jnp.stack(
        [
            jnp.concatenate(
                [
                    text_final[:, 2 * lanes * s : 2 * lanes * (s + 1)],
                    text_final[:, 8 * lanes + rest * s : 8 * lanes + rest * (s + 1)],
                ],
                axis=1,
            )
            for s in range(strips)
        ]
    )
    grad_text = lax.dynamic_index_in_dim(text_strips, zl, 0, False).astype(jnp.float32)
    for k in range(1, strips):
        given = lax.dynamic_index_in_dim(text_strips, (zl + k) % strips, 0, False)
        grad_text = grad_text + shift(given, "zl", k).astype(jnp.float32)
    grad_text = grad_text.astype(jnp.bfloat16)

    pairs_count = rows * zh_count * x_count * y_count * 2
    return (
        sums[0, 0] / pairs_count,
        grad_image,
        grad_text,
        scale * sums[1, 0] / pairs_count,
        sums[2, 0] / pairs_count,
    )


def solution(mesh):
    fine = Mesh(mesh.devices.reshape(4, 4, 4, 2, 4), ("zh", "x", "y", "core", "zl"))
    whole = P(("zh", "x", "y", "core"), "zl")
    return jax.shard_map(
        shards,
        mesh=fine,
        in_specs=(whole, whole, P(), P()),
        out_specs=(P(), whole, whole, P(), P()),
        check_vma=False,
    )
```

```python
import functools

import jax
import jax.numpy as jnp
from jax import lax
from jax.experimental import pallas as pl
from jax.experimental.pallas import tpu as pltpu
from jax.sharding import Mesh, PartitionSpec as P

epsilon = 1e-06
lanes = 128
piece = 32
half = 64
strips = 4
rest = 32
chunk_rows = 72
carry_rows = 16
tiles = 9
vmem = pl.BlockSpec(memory_space=pltpu.VMEM)
smem = pl.BlockSpec(memory_space=pltpu.SMEM)
anywhere = pl.BlockSpec(memory_space=pl.ANY)
limits = pltpu.CompilerParams(vmem_limit_bytes=40 * 1024 * 1024)


def shape(dims, dtype=jnp.bfloat16):
    return jax.ShapeDtypeStruct(tuple(dims), dtype)


def call(kernel, out_shape, name, operands, scalars=(), after=(), flops=0, special=0):
    out_shape = tuple(out_shape)
    scalars, operands, after = tuple(scalars), tuple(operands), tuple(after)
    inputs = len(scalars) + len(operands)
    moved = sum(a.size * a.dtype.itemsize for a in operands + out_shape)

    def body(*refs):
        kernel(*refs[:inputs], *refs[inputs + len(after) :])

    return pl.pallas_call(
        body,
        out_shape=out_shape,
        in_specs=[smem] * len(scalars) + [vmem] * len(operands) + [anywhere] * len(after),
        out_specs=(vmem,) * len(out_shape),
        compiler_params=limits,
        cost_estimate=pl.CostEstimate(flops=flops, bytes_accessed=moved, transcendentals=special),
        name=name,
    )(*scalars, *operands, *after)


def total(values):
    return functools.reduce(lambda a, b: a + b, values)


def wide(ref, *index):
    return ref[index].astype(jnp.float32)


def lane_group():
    return lax.broadcasted_iota(jnp.int32, (8, lanes), 1) // rest


def pack_kernel(image, text, out):
    chunks = []
    for ref in (image, text):
        found = []
        for k in range(4):
            rows = wide(ref, pl.ds(k * piece, piece), slice(None))
            last = rows[:, 2 * lanes :]
            last = jnp.concatenate([last[8 * g : 8 * g + 8] for g in range(4)], axis=1)
            found.append(jnp.concatenate([rows[:, :lanes], rows[:, lanes : 2 * lanes], last], axis=0))
        chunks.append(found)
    for d in range(strips):
        a, b = d // 2, d % 2
        parts = chunks[0][2 * a : 2 * a + 2] + chunks[1][2 * b : 2 * b + 2]
        out[d] = jnp.concatenate(parts, axis=0).astype(jnp.bfloat16)


def unpack_rows(chunks, group):
    found = []
    lasts = []
    for chunk in chunks:
        found += [chunk[:piece], chunk[piece : 2 * piece]]
        lasts.append(chunk[2 * piece :])
    last = []
    for g in range(4):
        value = jnp.zeros((8, lanes), jnp.float32)
        for s in range(strips):
            turn = rest * (s - g) % lanes
            moved = pltpu.roll(lasts[s], turn, 1) if turn else lasts[s]
            value = jnp.where(group == s, moved, value)
        last.append(value)
    found.append(jnp.concatenate(last, axis=0))
    return found


def unit_tiles(arrived, c, group):
    chunks = [arrived[s][c * chunk_rows : (c + 1) * chunk_rows] for s in range(strips)]
    found = unpack_rows(chunks, group)
    inverse = lax.rsqrt(jnp.sum(total([t * t for t in found]), axis=1, keepdims=True) + epsilon)
    return [t * inverse for t in found], inverse


def unit_kernel(arrived, image, text):
    group = lane_group()
    values = [wide(arrived, s) for s in range(strips)]
    for c in range(4):
        units, _ = unit_tiles(values, c, group)
        out = image if c < 2 else text
        for t in range(tiles):
            out[(c % 2) * piece : (c % 2 + 1) * piece, t * lanes : (t + 1) * lanes] = units[
                t
            ].astype(jnp.bfloat16)


def join_kernel(image_own, image_near, text_own, text_near, image, text):
    for k in range(image.shape[0]):
        image[k, :half, :] = image_own[...]
        image[k, half:, :] = image_near[...]
    text[:half, :] = text_own[...]
    text[half:, :] = text_near[...]


def fold(values):
    rows, columns = values.shape
    part = jnp.sum(values.reshape(rows // 8, 8, columns), axis=0)
    return total([part[:, c : c + lanes] for c in range(0, columns, lanes)])


def pair_terms(left, right, scale, bias, same=None):
    product = lax.dot_general(
        left, right, (((1,), (1,)), ((), ())), preferred_element_type=jnp.float32
    )
    logits = scale * product + bias
    if same is None:
        grown = jnp.exp(logits)
        slope = grown / (1.0 + grown)
    else:
        grown = jnp.exp(jnp.where(same, -logits, logits))
        share = grown / (1.0 + grown)
        slope = jnp.where(same, -share, share)
    quarter = left.shape[0] // 4
    a, b, c, d = (grown[k * quarter : (k + 1) * quarter, :] for k in range(4))
    ab = a + (b + a * b)
    cd = c + (d + c * d)
    sums = (fold(jnp.log1p(ab + (cd + ab * cd))), fold(slope * product), fold(slope))
    return (scale * slope).astype(jnp.bfloat16), sums


def write_sums(out, sums, before=None):
    for k in range(3):
        value = total([found[k] for found in sums])
        if before is not None:
            value = value + before[8 * k : 8 * k + 8, :]
        out[8 * k : 8 * k + 8, :] = value


tile = 256


def home_kernel(scales, spot, left, right, weights, sums_out):
    rows, columns = left.shape[0], right.shape[0]
    sums = []
    for start in range(0, rows, tile):
        here = pl.ds(start, tile)
        row = lax.broadcasted_iota(jnp.int32, (tile, 1), 0) + (start - spot[0])
        row = jnp.where((row >= 0) & (row < half), row, -1)
        same = row == lax.broadcasted_iota(jnp.int32, (1, columns), 1)
        weights[here, :], found = pair_terms(
            left[here, :], right[...], scales[0], scales[1], same
        )
        sums.append(found)
    write_sums(sums_out, sums)


def own_kernel(scales, left, t0, t1, t2, t3, home, home_sums, back, weights, right, sums_out):
    rows, part = left.shape[0], t0.shape[0]
    for k, ref in enumerate((t0, t1, t2, t3)):
        right[k * part : (k + 1) * part, :] = ref[...]
    sums = []
    for start in range(0, rows, tile):
        here = pl.ds(start, tile)
        value, found = pair_terms(left[here, :], right[part:, :], scales[0], scales[1])
        weights[here, :part] = home[here, :]
        weights[here, part:] = value
        back[here, :] = jnp.dot(
            weights[here, :], right[...], preferred_element_type=jnp.float32
        ).astype(jnp.bfloat16)
        sums.append(found)
    write_sums(sums_out, sums, home_sums)


def other_kernel(scales, left, right, own_sums, back, weights, sums_out):
    sums = []
    for start in range(0, left.shape[0], tile):
        here = pl.ds(start, tile)
        value, found = pair_terms(left[here, :], right[...], scales[0], scales[1])
        weights[here, :] = value
        back[here, :] = jnp.dot(
            value, right[...], preferred_element_type=jnp.float32
        ).astype(jnp.bfloat16)
        sums.append(found)
    row = lax.broadcasted_iota(jnp.int32, (8, lanes), 0)
    value = jnp.zeros((8, lanes), jnp.float32)
    for k in range(3):
        found = total([s[k] for s in sums]) + own_sums[8 * k : 8 * k + 8, :]
        value = jnp.where(row == k, jnp.sum(found, axis=0, keepdims=True), value)
    for k in range(sums_out.shape[0]):
        sums_out[k] = value


def text_kernel(first_weights, second_weights, first, second, *backs):
    contract = (((0,), (0,)), ((), ()))
    part = backs[0].shape[0]
    value = lax.dot_general(
        first_weights[...], first[...], contract, preferred_element_type=jnp.float32
    ) + lax.dot_general(
        second_weights[...], second[...], contract, preferred_element_type=jnp.float32
    )
    for k, back in enumerate(backs):
        back[...] = value[k * part : (k + 1) * part].astype(jnp.bfloat16)


def three_parts(value):
    high = value.astype(jnp.bfloat16).astype(jnp.float32)
    middle = (value - high).astype(jnp.bfloat16).astype(jnp.float32)
    return high, middle, value - high - middle


def carry_of(value):
    parts = three_parts(jnp.sum(value, axis=1, keepdims=True))
    lane = lax.broadcasted_iota(jnp.int32, (8, lanes), 1)
    carry = jnp.zeros((8, lanes), jnp.float32)
    for k in range(3):
        carry = jnp.where(lane == k, parts[k], carry)
    return jnp.concatenate([carry, jnp.zeros((8, lanes), jnp.float32)], axis=0)


def combine_kernel(own, given, sums, out):
    count, all_rows, _ = out.shape
    block = own.shape[0] // count
    carry = carry_of(total([sums[k] for k in range(sums.shape[0])])).astype(jnp.bfloat16)
    for k in range(count):
        rows = pl.ds(k * block, block)
        for t in range(tiles):
            columns = pl.ds(t * lanes, lanes)
            value = wide(own, rows, columns) + wide(given, rows, columns)
            out[k, t * block : (t + 1) * block, :] = value.astype(jnp.bfloat16)
        out[k, tiles * block : all_rows, :] = carry


def image_sum_kernel(backs, kept, sent, carry_out):
    count = backs.shape[0]
    block = 2 * half
    tail = tiles * block
    for t in range(tiles):
        rows = total([wide(backs, k, pl.ds(t * block, block), slice(None)) for k in range(count)])
        kept[t * half : (t + 1) * half, :] = rows[:half]
        sent[t * half : (t + 1) * half, :] = rows[half:].astype(jnp.bfloat16)
    carried = total([wide(backs, k, pl.ds(tail, carry_rows), slice(None)) for k in range(count)])
    carry = carry_of(carried[:8])
    sent[tiles * half :, :] = carry.astype(jnp.bfloat16)
    carry_out[...] = carry.astype(jnp.bfloat16)


def text_sum_kernel(b0, b1, b2, b3, carry, kept, sent):
    for t in range(tiles):
        columns = pl.ds(t * lanes, lanes)
        rows = total([wide(b, slice(None), columns) for b in (b0, b1, b2, b3)])
        kept[t * half : (t + 1) * half, :] = rows[:half]
        sent[t * half : (t + 1) * half, :] = rows[half:].astype(jnp.bfloat16)
    sent[tiles * half :, :] = carry[...]


def finish_kernel(arrived, image_kept, image_given, text_kept, text_given, carry, far, out):
    group = lane_group()
    tail = pl.ds(tiles * half, carry_rows)
    carried = total(
        [
            wide(carry, slice(None)),
            wide(far, slice(None)),
            wide(image_given, tail, slice(None)),
            wide(text_given, tail, slice(None)),
        ]
    )
    carry_now = carry_of(carried[:8]).astype(jnp.bfloat16)
    values = [wide(arrived, s) for s in range(strips)]
    for c in range(4):
        units, inverse = unit_tiles(values, c, group)
        kept, given = (image_kept, image_given) if c < 2 else (text_kept, text_given)
        grads = []
        for t in range(tiles):
            rows = pl.ds(t * half + (c % 2) * piece, piece)
            grads.append(kept[rows, :] + wide(given, rows, slice(None)))
        along = jnp.sum(total([u * g for u, g in zip(units, grads)]), axis=1, keepdims=True)
        final = [(g - u * along) * inverse for u, g in zip(units, grads)]
        if c % 2 == 0:
            chunks = [[] for _ in range(strips)]
        for s in range(strips):
            last = jnp.zeros((8, lanes), jnp.float32)
            for g in range(4):
                turn = rest * (g - s) % lanes
                rows = final[tiles - 1][8 * g : 8 * g + 8]
                moved = pltpu.roll(rows, turn, 1) if turn else rows
                last = jnp.where(group == g, moved, last)
            chunks[s] += [final[2 * s], final[2 * s + 1], last]
            if c % 2 == 1:
                start = (c // 2) * 2 * chunk_rows
                value = jnp.concatenate(chunks[s], axis=0).astype(jnp.bfloat16)
                out[s, start : start + 2 * chunk_rows, :] = value
    for s in range(strips):
        out[s, 4 * chunk_rows :, :] = carry_now


def last_kernel(arrived, image, text, sums_out):
    values = [wide(arrived, s) for s in range(strips)]
    for which, out in enumerate((image, text)):
        for k in range(4):
            c = 2 * which + k % 2
            h = k // 2
            sources = (2 * h, 2 * h + 1) if which == 0 else (h, 2 + h)
            chunk = total([values[s][c * chunk_rows : (c + 1) * chunk_rows] for s in sources])
            rows = pl.ds(k * piece, piece)
            out[rows, 0:lanes] = chunk[:piece].astype(jnp.bfloat16)
            out[rows, lanes : 2 * lanes] = chunk[piece : 2 * piece].astype(jnp.bfloat16)
            last = chunk[2 * piece :]
            groups = [last] + [pltpu.roll(last, lanes - rest * g, 1) for g in range(1, 4)]
            value = jnp.concatenate(groups, axis=0)[:, :rest]
            out[rows, 2 * lanes : 2 * lanes + rest] = value.astype(jnp.bfloat16)
    sums = total([v[4 * chunk_rows : 4 * chunk_rows + 8] for v in values])
    sums_out[...] = jnp.broadcast_to(jnp.sum(sums, axis=1, keepdims=True), sums.shape)


def swap_core(value):
    return lax.ppermute(value, "core", [(0, 1), (1, 0)])


def shift(value, axis, k):
    count = lax.axis_size(axis)
    return lax.ppermute(value, axis, [(i, (i + k) % count) for i in range(count)])


def swap_image(value):
    return lax.ppermute(value, "zh", [(0, 1), (1, 0), (2, 3), (3, 2)])


def swap_text(value):
    return lax.ppermute(value, "zh", [(0, 3), (3, 0), (1, 2), (2, 1)])


def shards(image, text, log_temp, bias):
    rows, strip = image.shape
    x_count, y_count = (lax.axis_size(name) for name in ("x", "y"))
    width = strip * strips
    block = 2 * half
    count = x_count * block
    x, zl = (lax.axis_index(name) for name in ("x", "zl"))
    scale = jnp.exp(log_temp)
    scales = jnp.stack([scale, bias])
    spot = jnp.where(zl // 2 == zl % 2, x * block, -count).astype(jnp.int32).reshape(1)
    f32 = jnp.float32

    (packed,) = call(pack_kernel, [shape((strips, 4 * chunk_rows, lanes))], "pack", [image, text])
    arrived = lax.all_to_all(packed, "zl", 0, 0)
    image_unit, text_unit = call(unit_kernel, [shape((half, width))] * 2, "unit", [arrived])
    image_near = swap_image(image_unit)
    text_near = swap_text(text_unit)
    joined, home_text = call(
        join_kernel,
        [shape((x_count, block, width)), shape((block, width))],
        "join",
        [image_unit, image_near, text_unit, text_near],
    )
    image_rows = lax.all_to_all(joined, "x", 0, 0).reshape(count, width)
    texts = [home_text] + [shift(home_text, "y", k) for k in range(1, y_count)]
    other_rows = swap_core(image_rows)

    columns = y_count * block
    area = count * columns
    home_weights, home_sums = call(
        home_kernel,
        [shape((count, block)), shape((24, lanes), f32)],
        "home",
        [image_rows, home_text],
        scalars=[scales, spot],
        flops=200 * count * block * width,
    )
    own_back, own_weights, right, own_sums = call(
        own_kernel,
        [
            shape((count, width)),
            shape((count, columns)),
            shape((columns, width)),
            shape((24, lanes), f32),
        ],
        "own",
        [image_rows] + texts + [home_weights, home_sums],
        scalars=[scales],
        flops=4 * area * width,
        special=2 * area,
    )
    other_back, other_weights, sums = call(
        other_kernel,
        [shape((count, width)), shape((count, columns)), shape((y_count * 2, 8, lanes), f32)],
        "other",
        [other_rows, right, own_sums],
        scalars=[scales],
        flops=4 * area * width,
        special=2 * area,
    )
    given_back = swap_core(other_back)
    sums = lax.all_to_all(sums, ("y", "core"), 0, 0)
    text_backs = call(
        text_kernel,
        [shape((block, width))] * y_count,
        "text_back",
        [own_weights, other_weights, image_rows, other_rows],
        flops=4 * area * width,
    )
    (combined,) = call(
        combine_kernel,
        [shape((x_count, tiles * block + carry_rows, lanes))],
        "combine",
        [own_back, given_back, sums],
    )
    combined = lax.all_to_all(combined, "x", 0, 0)
    part = [shape((tiles * half, lanes), f32), shape((tiles * half + carry_rows, lanes))]
    image_kept, image_sent, carry = call(
        image_sum_kernel, part + [shape((carry_rows, lanes))], "image_sum", [combined]
    )
    image_given = swap_image(image_sent)
    far = shift(carry, "zh", 2)
    moved = [text_backs[0]] + [shift(text_backs[k], "y", -k) for k in range(1, y_count)]
    text_kept, text_sent = call(text_sum_kernel, part, "text_sum", moved + [carry])
    text_given = swap_text(text_sent)
    (finished,) = call(
        finish_kernel,
        [shape((strips, 4 * chunk_rows + carry_rows, lanes))],
        "finish",
        [arrived, image_kept, image_given, text_kept, text_given, carry, far],
    )
    finished = lax.all_to_all(finished, "zl", 0, 0)
    grad_image, grad_text, sums = call(
        last_kernel, [shape((rows, strip))] * 2 + [shape((8, lanes), f32)], "last", [finished]
    )
    pairs_count = rows * 4 * x_count * y_count * 2
    return (
        sums[0, 0] / pairs_count,
        grad_image,
        grad_text,
        scale * sums[1, 0] / pairs_count,
        sums[2, 0] / pairs_count,
    )


def solution(mesh):
    fine = Mesh(mesh.devices.reshape(4, 4, 4, 2, 4), ("zh", "x", "y", "core", "zl"))
    whole = P(("zh", "x", "y", "core"), "zl")
    return jax.shard_map(
        shards,
        mesh=fine,
        in_specs=(whole, whole, P(), P()),
        out_specs=(P(), whole, whole, P(), P()),
        check_vma=False,
    )
```

```python
import functools

import jax
import jax.numpy as jnp
from jax import lax
from jax.experimental import pallas as pl
from jax.experimental.pallas import tpu as pltpu
from jax.sharding import Mesh, PartitionSpec as P

epsilon = 1e-06
lanes = 128
piece = 32
strips = 4
rest = 32
chunk_rows = 72
part_rows = 2 * chunk_rows
carry_rows = 16
tiles = 9
vmem = pl.BlockSpec(memory_space=pltpu.VMEM)
smem = pl.BlockSpec(memory_space=pltpu.SMEM)
anywhere = pl.BlockSpec(memory_space=pl.ANY)
limits = pltpu.CompilerParams(vmem_limit_bytes=40 * 1024 * 1024)


def shape(dims, dtype=jnp.bfloat16):
    return jax.ShapeDtypeStruct(tuple(dims), dtype)


def call(kernel, out_shape, name, operands, scalars=(), after=(), flops=0, special=0):
    out_shape = tuple(out_shape)
    scalars, operands, after = tuple(scalars), tuple(operands), tuple(after)
    inputs = len(scalars) + len(operands)
    moved = sum(a.size * a.dtype.itemsize for a in operands + out_shape)

    def body(*refs):
        kernel(*refs[:inputs], *refs[inputs + len(after) :])

    return pl.pallas_call(
        body,
        out_shape=out_shape,
        in_specs=[smem] * len(scalars) + [vmem] * len(operands) + [anywhere] * len(after),
        out_specs=(vmem,) * len(out_shape),
        compiler_params=limits,
        cost_estimate=pl.CostEstimate(flops=flops, bytes_accessed=moved, transcendentals=special),
        name=name,
    )(*scalars, *operands, *after)


def total(values):
    return functools.reduce(lambda a, b: a + b, values)


def wide(ref, *index):
    return ref[index].astype(jnp.float32)


def lane_group():
    return lax.broadcasted_iota(jnp.int32, (8, lanes), 1) // rest


def pack_kernel(image, text, out):
    chunks = []
    for ref in (image, text):
        found = []
        whole = wide(ref, slice(None)).T
        for k in range(4):
            rows = whole[k * piece : (k + 1) * piece]
            last = rows[:, 2 * lanes :]
            last = jnp.concatenate([last[8 * g : 8 * g + 8] for g in range(4)], axis=1)
            found.append(jnp.concatenate([rows[:, :lanes], rows[:, lanes : 2 * lanes], last], axis=0))
        chunks.append(found)
    for d in range(out.shape[0]):
        both = [chunks[0][d % strips], chunks[1][d // strips]]
        out[d] = jnp.concatenate(both, axis=0).astype(jnp.bfloat16)


def unpack_rows(chunks, group):
    found = []
    lasts = []
    for chunk in chunks:
        found += [chunk[:piece], chunk[piece : 2 * piece]]
        lasts.append(chunk[2 * piece :])
    last = []
    for g in range(4):
        value = jnp.zeros((8, lanes), jnp.float32)
        for s in range(strips):
            turn = rest * (s - g) % lanes
            moved = pltpu.roll(lasts[s], turn, 1) if turn else lasts[s]
            value = jnp.where(group == s, moved, value)
        last.append(value)
    found.append(jnp.concatenate(last, axis=0))
    return found


def unit_tiles(arrived, h, which, group):
    rows = pl.ds(which * chunk_rows, chunk_rows)
    found = unpack_rows([wide(arrived, h * strips + s, rows) for s in range(strips)], group)
    inverse = lax.rsqrt(jnp.sum(total([t * t for t in found]), axis=1, keepdims=True) + epsilon)
    return [t * inverse for t in found], inverse


def unit_kernel(arrived, image, text):
    group = lane_group()
    for h in range(arrived.shape[0] // strips):
        rows = pl.ds(h * piece, piece)
        for which in range(2):
            units, _ = unit_tiles(arrived, h, which, group)
            for t in range(tiles):
                columns = pl.ds(t * lanes, lanes)
                value = units[t].astype(jnp.bfloat16)
                if which:
                    text[rows, columns] = value
                else:
                    for k in range(image.shape[0]):
                        image[k, rows, columns] = value


def fold(values):
    rows, columns = values.shape
    part = jnp.sum(values.reshape(rows // 8, 8, columns), axis=0)
    return total([part[:, c : c + lanes] for c in range(0, columns, lanes)])


def pair_terms(left, right, scale, bias, same=None):
    product = lax.dot_general(
        left, right, (((1,), (1,)), ((), ())), preferred_element_type=jnp.float32
    )
    logits = scale * product + bias
    if same is None:
        grown = jnp.exp(logits)
        slope = grown / (1.0 + grown)
    else:
        grown = jnp.exp(jnp.where(same, -logits, logits))
        share = grown / (1.0 + grown)
        slope = jnp.where(same, -share, share)
    quarter = left.shape[0] // 4
    a, b, c, d = (grown[k * quarter : (k + 1) * quarter, :] for k in range(4))
    ab = a + (b + a * b)
    cd = c + (d + c * d)
    sums = (fold(jnp.log1p(ab + (cd + ab * cd))), fold(slope * product), fold(slope))
    return (scale * slope).astype(jnp.bfloat16), sums


def write_sums(out, sums, before=None):
    for k in range(3):
        value = total([found[k] for found in sums])
        if before is not None:
            value = value + before[8 * k : 8 * k + 8, :]
        out[8 * k : 8 * k + 8, :] = value


tile = 256


def home_kernel(scales, spot, left, right, weights, sums_out):
    rows, columns = left.shape[0], right.shape[0]
    sums = []
    for start in range(0, rows, tile):
        here = pl.ds(start, tile)
        row = lax.broadcasted_iota(jnp.int32, (tile, 1), 0) + (start - spot[0])
        row = jnp.where((row >= 0) & (row < columns), row, -1)
        same = row == lax.broadcasted_iota(jnp.int32, (1, columns), 1)
        weights[here, :], found = pair_terms(
            left[here, :], right[...], scales[0], scales[1], same
        )
        sums.append(found)
    write_sums(sums_out, sums)


def own_kernel(scales, left, t0, t1, t2, t3, home, home_sums, back, weights, right, sums_out):
    rows, part = left.shape[0], t0.shape[0]
    for k, ref in enumerate((t0, t1, t2, t3)):
        right[k * part : (k + 1) * part, :] = ref[...]
    sums = []
    for start in range(0, rows, tile):
        here = pl.ds(start, tile)
        value, found = pair_terms(left[here, :], right[part:, :], scales[0], scales[1])
        weights[here, :part] = home[here, :]
        weights[here, part:] = value
        back[here, :] = jnp.dot(
            weights[here, :], right[...], preferred_element_type=jnp.float32
        ).astype(jnp.bfloat16)
        sums.append(found)
    write_sums(sums_out, sums, home_sums)


def other_kernel(scales, left, right, own_sums, back, weights, sums_out):
    sums = []
    for start in range(0, left.shape[0], tile):
        here = pl.ds(start, tile)
        value, found = pair_terms(left[here, :], right[...], scales[0], scales[1])
        weights[here, :] = value
        back[here, :] = jnp.dot(
            value, right[...], preferred_element_type=jnp.float32
        ).astype(jnp.bfloat16)
        sums.append(found)
    row = lax.broadcasted_iota(jnp.int32, (8, lanes), 0)
    value = jnp.zeros((8, lanes), jnp.float32)
    for k in range(3):
        found = total([s[k] for s in sums]) + own_sums[8 * k : 8 * k + 8, :]
        value = jnp.where(row == k, jnp.sum(found, axis=0, keepdims=True), value)
    for k in range(sums_out.shape[0]):
        sums_out[k] = value


def text_kernel(first_weights, second_weights, first, second, *backs):
    contract = (((0,), (0,)), ((), ()))
    part = backs[0].shape[0]
    value = lax.dot_general(
        first_weights[...], first[...], contract, preferred_element_type=jnp.float32
    ) + lax.dot_general(
        second_weights[...], second[...], contract, preferred_element_type=jnp.float32
    )
    for k, back in enumerate(backs):
        back[...] = value[k * part : (k + 1) * part].astype(jnp.bfloat16)


def three_parts(value):
    high = value.astype(jnp.bfloat16).astype(jnp.float32)
    middle = (value - high).astype(jnp.bfloat16).astype(jnp.float32)
    return high, middle, value - high - middle


def carry_of(value):
    parts = three_parts(jnp.sum(value, axis=1, keepdims=True))
    lane = lax.broadcasted_iota(jnp.int32, (8, lanes), 1)
    carry = jnp.zeros((8, lanes), jnp.float32)
    for k in range(3):
        carry = jnp.where(lane == k, parts[k], carry)
    return jnp.concatenate([carry, jnp.zeros((8, lanes), jnp.float32)], axis=0)


def combine_kernel(own, given, sums, out):
    count, all_rows, _ = out.shape
    block = own.shape[0] // count
    carry = carry_of(total([sums[k] for k in range(sums.shape[0])])).astype(jnp.bfloat16)
    for k in range(count):
        rows = pl.ds(k * block, block)
        for t in range(tiles):
            columns = pl.ds(t * lanes, lanes)
            value = wide(own, rows, columns) + wide(given, rows, columns)
            out[k, t * block : (t + 1) * block, :] = value.astype(jnp.bfloat16)
        out[k, tiles * block : all_rows, :] = carry


def pack_grads(units, inverse, grads, group):
    along = jnp.sum(total([u * g for u, g in zip(units, grads)]), axis=1, keepdims=True)
    final = [(g - u * along) * inverse for u, g in zip(units, grads)]
    chunks = []
    for s in range(strips):
        last = jnp.zeros((8, lanes), jnp.float32)
        for g in range(4):
            turn = rest * (g - s) % lanes
            rows = final[tiles - 1][8 * g : 8 * g + 8]
            moved = pltpu.roll(rows, turn, 1) if turn else rows
            last = jnp.where(group == g, moved, last)
        chunks.append(jnp.concatenate([final[2 * s], final[2 * s + 1], last], axis=0))
    return chunks


def image_finish_kernel(arrived, backs, out):
    group = lane_group()
    count = backs.shape[0]
    heads = arrived.shape[0] // strips
    block = heads * piece
    tail = pl.ds(tiles * block, carry_rows)
    carry = carry_of(total([wide(backs, k, tail) for k in range(count)])[:8])
    for h in range(heads):
        units, inverse = unit_tiles(arrived, h, 0, group)
        grads = []
        for t in range(tiles):
            rows = pl.ds(t * block + h * piece, piece)
            grads.append(total([wide(backs, k, rows) for k in range(count)]))
        for s, chunk in enumerate(pack_grads(units, inverse, grads, group)):
            out[h * strips + s] = jnp.concatenate([carry, chunk], axis=0)


def text_finish_kernel(arrived, image, b0, b1, b2, b3, out):
    group = lane_group()
    for h in range(arrived.shape[0] // strips):
        units, inverse = unit_tiles(arrived, h, 1, group)
        grads = []
        for t in range(tiles):
            rows, columns = pl.ds(h * piece, piece), pl.ds(t * lanes, lanes)
            grads.append(total([wide(b, rows, columns) for b in (b0, b1, b2, b3)]))
        for s, chunk in enumerate(pack_grads(units, inverse, grads, group)):
            d = h * strips + s
            out[d] = jnp.concatenate([image[d], chunk], axis=0).astype(jnp.bfloat16)


def last_kernel(arrived, image, text, sums_out):
    values = [wide(arrived, d) for d in range(arrived.shape[0])]
    heads = len(values) // strips
    for which, out in enumerate((image, text)):
        start = carry_rows + which * chunk_rows
        found = []
        for k in range(4):
            if which:
                sources = [k * strips + s for s in range(strips)]
            else:
                sources = [h * strips + k for h in range(heads)]
            chunk = total([values[d][start : start + chunk_rows] for d in sources])
            last = chunk[2 * piece :]
            groups = [last] + [pltpu.roll(last, lanes - rest * g, 1) for g in range(1, 4)]
            last = jnp.concatenate(groups, axis=0)
            found.append((chunk[:piece], chunk[piece : 2 * piece], last))
        for t in range(3):
            rows = jnp.concatenate([f[t] for f in found], axis=0).T
            count = lanes if t < 2 else rest
            out[t * lanes : t * lanes + count, :] = rows[:count].astype(jnp.bfloat16)
    sums = total([v[:8] for v in values])
    sums_out[...] = jnp.broadcast_to(jnp.sum(sums, axis=1, keepdims=True), sums.shape)


def swap_core(value):
    return lax.ppermute(value, "core", [(0, 1), (1, 0)])


def shift(value, axis, k):
    count = lax.axis_size(axis)
    return lax.ppermute(value, axis, [(i, (i + k) % count) for i in range(count)])


def shards(image, text, log_temp, bias):
    rows, strip = image.shape
    x_count, y_count, zh_count = (lax.axis_size(name) for name in ("x", "y", "zh"))
    z_count = zh_count * strips
    width = strip * strips
    block = zh_count * piece
    count = x_count * block
    zh, x, zl = (lax.axis_index(name) for name in ("zh", "x", "zl"))
    scale = jnp.exp(log_temp)
    scales = jnp.stack([scale, bias])
    spot = jnp.where(zh == zl, x * block, -count).astype(jnp.int32).reshape(1)
    f32 = jnp.float32

    (packed,) = call(pack_kernel, [shape((z_count, part_rows, lanes))], "pack", [image.T, text.T])
    arrived = lax.all_to_all(packed, ("zh", "zl"), 0, 0)
    units, home_text = call(
        unit_kernel, [shape((x_count, block, width)), shape((block, width))], "unit", [arrived]
    )
    image_rows = lax.all_to_all(units, "x", 0, 0).reshape(count, width)
    texts = [home_text] + [shift(home_text, "y", k) for k in range(1, y_count)]
    other_rows = swap_core(image_rows)

    columns = y_count * block
    area = count * columns
    home_weights, home_sums = call(
        home_kernel,
        [shape((count, block)), shape((24, lanes), f32)],
        "home",
        [image_rows, home_text],
        scalars=[scales, spot],
        flops=200 * count * block * width,
    )
    own_back, own_weights, right, own_sums = call(
        own_kernel,
        [
            shape((count, width)),
            shape((count, columns)),
            shape((columns, width)),
            shape((24, lanes), f32),
        ],
        "own",
        [image_rows] + texts + [home_weights, home_sums],
        scalars=[scales],
        flops=4 * area * width,
        special=2 * area,
    )
    other_back, other_weights, sums = call(
        other_kernel,
        [shape((count, width)), shape((count, columns)), shape((y_count * 2, 8, lanes), f32)],
        "other",
        [other_rows, right, own_sums],
        scalars=[scales],
        flops=4 * area * width,
        special=2 * area,
    )
    given_back = swap_core(other_back)
    sums = lax.all_to_all(sums, ("y", "core"), 0, 0)
    text_backs = call(
        text_kernel,
        [shape((block, width))] * y_count,
        "text_back",
        [own_weights, other_weights, image_rows, other_rows],
        flops=4 * area * width,
    )
    (combined,) = call(
        combine_kernel,
        [shape((x_count, tiles * block + carry_rows, lanes))],
        "combine",
        [own_back, given_back, sums],
        after=text_backs[:1],
    )
    combined = lax.all_to_all(combined, "x", 0, 0)
    (finished,) = call(
        image_finish_kernel,
        [shape((z_count, carry_rows + chunk_rows, lanes), f32)],
        "image_finish",
        [arrived, combined],
        flops=200 * count * block * width,
    )
    moved = [text_backs[0]] + [shift(text_backs[k], "y", -k) for k in range(1, y_count)]
    (finished,) = call(
        text_finish_kernel,
        [shape((z_count, carry_rows + part_rows, lanes))],
        "text_finish",
        [arrived, finished] + moved,
    )
    finished = lax.all_to_all(finished, ("zh", "zl"), 0, 0)
    grad_image, grad_text, sums = call(
        last_kernel, [shape((strip, rows))] * 2 + [shape((8, lanes), f32)], "last", [finished]
    )
    pairs_count = rows * zh_count * x_count * y_count * 2
    return (
        sums[0, 0] / pairs_count,
        grad_image.T,
        grad_text.T,
        scale * sums[1, 0] / pairs_count,
        sums[2, 0] / pairs_count,
    )


def solution(mesh):
    fine = Mesh(mesh.devices.reshape(4, 4, 4, 2, 4), ("zh", "x", "y", "core", "zl"))
    whole = P(("zh", "x", "y", "core"), "zl")
    return jax.shard_map(
        shards,
        mesh=fine,
        in_specs=(whole, whole, P(), P()),
        out_specs=(P(), whole, whole, P(), P()),
        check_vma=False,
    )
```

```python
import functools

import jax
import jax.numpy as jnp
from jax import lax
from jax.experimental import pallas as pl
from jax.experimental.pallas import tpu as pltpu
from jax.sharding import Mesh, PartitionSpec as P

epsilon = 1e-06
lanes = 128
piece = 32
half = 64
strips = 4
rest = 32
chunk_rows = 72
carry_rows = 16
tiles = 9
vmem = pl.BlockSpec(memory_space=pltpu.VMEM)
smem = pl.BlockSpec(memory_space=pltpu.SMEM)
anywhere = pl.BlockSpec(memory_space=pl.ANY)
limits = pltpu.CompilerParams(vmem_limit_bytes=16 * 1024 * 1024)


def shape(dims, dtype=jnp.bfloat16):
    return jax.ShapeDtypeStruct(tuple(dims), dtype)


def call(kernel, out_shape, name, operands, scalars=(), after=(), flops=0, special=0, scratch=()):
    out_shape = tuple(out_shape)
    scalars, operands, after = tuple(scalars), tuple(operands), tuple(after)
    inputs = len(scalars) + len(operands)
    moved = sum(a.size * a.dtype.itemsize for a in operands + out_shape)

    def body(*refs):
        kernel(*refs[:inputs], *refs[inputs + len(after) :])

    return pl.pallas_call(
        body,
        out_shape=out_shape,
        in_specs=[smem] * len(scalars) + [vmem] * len(operands) + [anywhere] * len(after),
        out_specs=(vmem,) * len(out_shape),
        scratch_shapes=list(scratch),
        compiler_params=limits,
        cost_estimate=pl.CostEstimate(flops=flops, bytes_accessed=moved, transcendentals=special),
        name=name,
    )(*scalars, *operands, *after)


def total(values):
    return functools.reduce(lambda a, b: a + b, values)


def wide(ref, *index):
    return ref[index].astype(jnp.float32)


def lane_group():
    return lax.broadcasted_iota(jnp.int32, (8, lanes), 1) // rest


def pack_kernel(image, text, out):
    chunks = []
    for ref in (image, text):
        found = []
        whole = wide(ref, slice(None)).T
        for k in range(4):
            rows = whole[k * piece : (k + 1) * piece]
            last = rows[:, 2 * lanes :]
            last = jnp.concatenate([last[8 * g : 8 * g + 8] for g in range(4)], axis=1)
            found.append(jnp.concatenate([rows[:, :lanes], rows[:, lanes : 2 * lanes], last], axis=0))
        chunks.append(found)
    for d in range(strips):
        a, b = d // 2, d % 2
        parts = chunks[0][2 * a : 2 * a + 2] + chunks[1][2 * b : 2 * b + 2]
        out[d] = jnp.concatenate(parts, axis=0).astype(jnp.bfloat16)


def unpack_rows(chunks, group):
    found = []
    lasts = []
    for chunk in chunks:
        found += [chunk[:piece], chunk[piece : 2 * piece]]
        lasts.append(chunk[2 * piece :])
    last = []
    for g in range(4):
        value = jnp.zeros((8, lanes), jnp.float32)
        for s in range(strips):
            turn = rest * (s - g) % lanes
            moved = pltpu.roll(lasts[s], turn, 1) if turn else lasts[s]
            value = jnp.where(group == s, moved, value)
        last.append(value)
    found.append(jnp.concatenate(last, axis=0))
    return found


def unit_tiles(arrived, c, group):
    chunks = [arrived[s][c * chunk_rows : (c + 1) * chunk_rows] for s in range(strips)]
    found = unpack_rows(chunks, group)
    inverse = lax.rsqrt(jnp.sum(total([t * t for t in found]), axis=1, keepdims=True) + epsilon)
    return [t * inverse for t in found], inverse


def unit_kernel(arrived, image, text):
    group = lane_group()
    values = [wide(arrived, s) for s in range(strips)]
    for c in range(4):
        units, _ = unit_tiles(values, c, group)
        out = image if c < 2 else text
        for t in range(tiles):
            out[(c % 2) * piece : (c % 2 + 1) * piece, t * lanes : (t + 1) * lanes] = units[
                t
            ].astype(jnp.bfloat16)


def join_kernel(image_own, image_near, text_own, text_near, image, text):
    for k in range(image.shape[0]):
        image[k, :half, :] = image_own[...]
        image[k, half:, :] = image_near[...]
    text[:half, :] = text_own[...]
    text[half:, :] = text_near[...]


def fold(values):
    rows, columns = values.shape
    part = jnp.sum(values.reshape(rows // 8, 8, columns), axis=0)
    return total([part[:, c : c + lanes] for c in range(0, columns, lanes)])


def pair_terms(left, right, scale, bias, same=None):
    product = lax.dot_general(
        left, right, (((1,), (1,)), ((), ())), preferred_element_type=jnp.float32
    )
    logits = scale * product + bias
    if same is None:
        grown = jnp.exp(logits)
        slope = grown / (1.0 + grown)
    else:
        grown = jnp.exp(jnp.where(same, -logits, logits))
        share = grown / (1.0 + grown)
        slope = jnp.where(same, -share, share)
    quarter = left.shape[0] // 4
    a, b, c, d = (grown[k * quarter : (k + 1) * quarter, :] for k in range(4))
    ab = a + (b + a * b)
    cd = c + (d + c * d)
    sums = (fold(jnp.log1p(ab + (cd + ab * cd))), fold(slope * product), fold(slope))
    return (scale * slope).astype(jnp.bfloat16), sums


def write_sums(out, sums, before=None):
    for k in range(3):
        value = total([found[k] for found in sums])
        if before is not None:
            value = value + before[8 * k : 8 * k + 8, :]
        out[8 * k : 8 * k + 8, :] = value


tile = 256


def home_kernel(scales, spot, left, right, weights, sums_out, kept):
    kept[...] = right[...]
    rows, columns = left.shape[0], right.shape[0]
    sums = []
    for start in range(0, rows, tile):
        here = pl.ds(start, tile)
        row = lax.broadcasted_iota(jnp.int32, (tile, 1), 0) + (start - spot[0])
        row = jnp.where((row >= 0) & (row < half), row, -1)
        same = row == lax.broadcasted_iota(jnp.int32, (1, columns), 1)
        weights[here, :], found = pair_terms(
            left[here, :], right[...], scales[0], scales[1], same
        )
        sums.append(found)
    write_sums(sums_out, sums)


def own_kernel(scales, left, t0, t1, t2, t3, home, home_sums, back, weights, right, sums_out):
    rows, part = left.shape[0], t0.shape[0]
    for k, ref in enumerate((t0, t1, t2, t3)):
        right[k * part : (k + 1) * part, :] = ref[...]
    sums = []
    for start in range(0, rows, tile):
        here = pl.ds(start, tile)
        value, found = pair_terms(left[here, :], right[part:, :], scales[0], scales[1])
        weights[here, :part] = home[here, :]
        weights[here, part:] = value
        back[here, :] = jnp.dot(
            weights[here, :], right[...], preferred_element_type=jnp.float32
        ).astype(jnp.bfloat16)
        sums.append(found)
    write_sums(sums_out, sums, home_sums)


def other_kernel(
    scales, left, right, own_sums, own_weights, own_left, back, sums_out, b0, b1, b2, b3, weights
):
    sums = []
    for start in range(0, left.shape[0], tile):
        here = pl.ds(start, tile)
        value, found = pair_terms(left[here, :], right[...], scales[0], scales[1])
        weights[here, :] = value
        back[here, :] = jnp.dot(
            value, right[...], preferred_element_type=jnp.float32
        ).astype(jnp.bfloat16)
        sums.append(found)
    row = lax.broadcasted_iota(jnp.int32, (8, lanes), 0)
    value = jnp.zeros((8, lanes), jnp.float32)
    for k in range(3):
        found = total([s[k] for s in sums]) + own_sums[8 * k : 8 * k + 8, :]
        value = jnp.where(row == k, jnp.sum(found, axis=0, keepdims=True), value)
    for k in range(sums_out.shape[0]):
        sums_out[k] = value
    contract = (((0,), (0,)), ((), ()))
    part = b0.shape[0]
    value = lax.dot_general(
        own_weights[...], own_left[...], contract, preferred_element_type=jnp.float32
    ) + lax.dot_general(weights[...], left[...], contract, preferred_element_type=jnp.float32)
    for k, out in enumerate((b0, b1, b2, b3)):
        out[...] = value[k * part : (k + 1) * part].astype(jnp.bfloat16)


def three_parts(value):
    high = value.astype(jnp.bfloat16).astype(jnp.float32)
    middle = (value - high).astype(jnp.bfloat16).astype(jnp.float32)
    return high, middle, value - high - middle


def carry_of(value):
    parts = three_parts(jnp.sum(value, axis=1, keepdims=True))
    lane = lax.broadcasted_iota(jnp.int32, (8, lanes), 1)
    carry = jnp.zeros((8, lanes), jnp.float32)
    for k in range(3):
        carry = jnp.where(lane == k, parts[k], carry)
    return jnp.concatenate([carry, jnp.zeros((8, lanes), jnp.float32)], axis=0)


def combine_kernel(own, given, sums, out):
    count, all_rows, _ = out.shape
    block = own.shape[0] // count
    carry = carry_of(total([sums[k] for k in range(sums.shape[0])])).astype(jnp.bfloat16)
    for k in range(count):
        rows = pl.ds(k * block, block)
        for t in range(tiles):
            columns = pl.ds(t * lanes, lanes)
            value = wide(own, rows, columns) + wide(given, rows, columns)
            out[k, t * block : (t + 1) * block, :] = value.astype(jnp.bfloat16)
        out[k, tiles * block : all_rows, :] = carry


def image_sum_kernel(backs, kept, sent):
    count = backs.shape[0]
    block = 2 * half
    for t in range(tiles):
        rows = total([wide(backs, k, pl.ds(t * block, block), slice(None)) for k in range(count)])
        kept[t * half : (t + 1) * half, :] = rows[:half]
        sent[t * half : (t + 1) * half, :] = rows[half:].astype(jnp.bfloat16)
    tail = pl.ds(tiles * block, carry_rows)
    carry = carry_of(total([wide(backs, k, tail, slice(None)) for k in range(count)])[:8])
    kept[tiles * half :, :] = carry
    sent[tiles * half :, :] = carry.astype(jnp.bfloat16)


def text_sum_kernel(b0, b1, b2, b3, kept, sent):
    for t in range(tiles):
        columns = pl.ds(t * lanes, lanes)
        rows = total([wide(b, slice(None), columns) for b in (b0, b1, b2, b3)])
        kept[t * half : (t + 1) * half, :] = rows[:half]
        sent[t * half : (t + 1) * half, :] = rows[half:].astype(jnp.bfloat16)


def finish_kernel(arrived, image_kept, image_given, text_kept, text_given, out):
    group = lane_group()
    tail = pl.ds(tiles * half, carry_rows)
    carried = image_kept[tail, :] + wide(image_given, tail, slice(None))
    carry_now = carry_of(carried[:8]).astype(jnp.bfloat16)
    values = [wide(arrived, s) for s in range(strips)]
    for c in range(4):
        units, inverse = unit_tiles(values, c, group)
        kept, given = (image_kept, image_given) if c < 2 else (text_kept, text_given)
        grads = []
        for t in range(tiles):
            rows = pl.ds(t * half + (c % 2) * piece, piece)
            grads.append(kept[rows, :] + wide(given, rows, slice(None)))
        along = jnp.sum(total([u * g for u, g in zip(units, grads)]), axis=1, keepdims=True)
        final = [(g - u * along) * inverse for u, g in zip(units, grads)]
        if c % 2 == 0:
            chunks = [[] for _ in range(strips)]
        for s in range(strips):
            last = jnp.zeros((8, lanes), jnp.float32)
            for g in range(4):
                turn = rest * (g - s) % lanes
                rows = final[tiles - 1][8 * g : 8 * g + 8]
                moved = pltpu.roll(rows, turn, 1) if turn else rows
                last = jnp.where(group == g, moved, last)
            chunks[s] += [final[2 * s], final[2 * s + 1], last]
            if c % 2 == 1:
                start = (c // 2) * 2 * chunk_rows
                value = jnp.concatenate(chunks[s], axis=0).astype(jnp.bfloat16)
                out[s, start : start + 2 * chunk_rows, :] = value
    for s in range(strips):
        out[s, 4 * chunk_rows :, :] = carry_now


def last_kernel(arrived, image, text, sums_out):
    values = [wide(arrived, s) for s in range(strips)]
    for which, out in enumerate((image, text)):
        found = []
        for k in range(4):
            c = 2 * which + k % 2
            h = k // 2
            sources = (h, 2 + h) if which else (2 * h, 2 * h + 1)
            chunk = total([values[s][c * chunk_rows : (c + 1) * chunk_rows] for s in sources])
            last = chunk[2 * piece :]
            groups = [last] + [pltpu.roll(last, lanes - rest * g, 1) for g in range(1, 4)]
            last = jnp.concatenate(groups, axis=0)
            found.append((chunk[:piece], chunk[piece : 2 * piece], last))
        for t in range(3):
            rows = jnp.concatenate([f[t] for f in found], axis=0).T
            count = lanes if t < 2 else rest
            out[t * lanes : t * lanes + count, :] = rows[:count].astype(jnp.bfloat16)
    sums = total([v[4 * chunk_rows : 4 * chunk_rows + 8] for v in values])
    sums_out[...] = jnp.broadcast_to(jnp.sum(sums, axis=1, keepdims=True), sums.shape)


def swap_core(value):
    return lax.ppermute(value, "core", [(0, 1), (1, 0)])


def shift(value, axis, k):
    count = lax.axis_size(axis)
    return lax.ppermute(value, axis, [(i, (i + k) % count) for i in range(count)])


def swap_image(value):
    return lax.ppermute(value, ("zh1", "zh0"), [(0, 3), (3, 0), (1, 2), (2, 1)])


def swap_text(value):
    return lax.ppermute(value, ("zh1", "zh0"), [(0, 1), (1, 0), (2, 3), (3, 2)])


def shards(image, text, log_temp, bias):
    rows, strip = image.shape
    x_count, y_count = (lax.axis_size(name) for name in ("x", "y"))
    width = strip * strips
    block = 2 * half
    count = x_count * block
    x, zl = (lax.axis_index(name) for name in ("x", "zl"))
    scale = jnp.exp(log_temp)
    scales = jnp.stack([scale, bias])
    spot = jnp.where(zl // 2 == zl % 2, x * block, -count).astype(jnp.int32).reshape(1)
    f32 = jnp.float32

    (packed,) = call(pack_kernel, [shape((strips, 4 * chunk_rows, lanes))], "pack", [image.T, text.T])
    arrived = lax.all_to_all(packed, "zl", 0, 0)
    image_unit, text_unit = call(unit_kernel, [shape((half, width))] * 2, "unit", [arrived])
    image_near = swap_image(image_unit)
    text_near = swap_text(text_unit)
    joined, home_text = call(
        join_kernel,
        [shape((x_count, block, width)), shape((block, width))],
        "join",
        [image_unit, image_near, text_unit, text_near],
    )
    image_rows = lax.all_to_all(joined, "x", 0, 0).reshape(count, width)
    texts = [shift(home_text, "y", k) for k in range(1, y_count)]
    other_rows = swap_core(image_rows)

    columns = y_count * block
    area = count * columns
    home_weights, home_sums, home_text = call(
        home_kernel,
        [shape((count, block)), shape((24, lanes), f32), shape((block, width))],
        "home",
        [image_rows, home_text],
        scalars=[scales, spot],
        flops=200 * count * block * width,
    )
    own_back, own_weights, right, own_sums = call(
        own_kernel,
        [
            shape((count, width)),
            shape((count, columns)),
            shape((columns, width)),
            shape((24, lanes), f32),
        ],
        "own",
        [image_rows, home_text] + texts + [home_weights, home_sums],
        scalars=[scales],
        flops=4 * area * width,
        special=2 * area,
    )
    other_back, sums, *text_backs = call(
        other_kernel,
        [shape((count, width)), shape((y_count * 4, 8, lanes), f32)]
        + [shape((block, width))] * y_count,
        "other",
        [other_rows, right, own_sums, own_weights, image_rows],
        scalars=[scales],
        flops=8 * area * width,
        special=2 * area,
        scratch=[pltpu.VMEM((count, columns), jnp.bfloat16)],
    )
    given_back = swap_core(other_back)
    sums = lax.all_to_all(sums, ("zh0", "y", "core"), 0, 0)
    (combined,) = call(
        combine_kernel,
        [shape((x_count, tiles * block + carry_rows, lanes))],
        "combine",
        [own_back, given_back, sums],
    )
    combined = lax.all_to_all(combined, "x", 0, 0)
    sums_rows = tiles * half + carry_rows
    image_kept, image_sent = call(
        image_sum_kernel,
        [shape((sums_rows, lanes), f32), shape((sums_rows, lanes))],
        "image_sum",
        [combined],
    )
    image_given = swap_image(image_sent)
    moved = [text_backs[0]] + [shift(text_backs[k], "y", -k) for k in range(1, y_count)]
    text_kept, text_sent = call(
        text_sum_kernel,
        [shape((tiles * half, lanes), f32), shape((tiles * half, lanes))],
        "text_sum",
        moved,
    )
    text_given = swap_text(text_sent)
    (finished,) = call(
        finish_kernel,
        [shape((strips, 4 * chunk_rows + carry_rows, lanes))],
        "finish",
        [arrived, image_kept, image_given, text_kept, text_given],
    )
    finished = lax.all_to_all(finished, "zl", 0, 0)
    grad_image, grad_text, sums = call(
        last_kernel, [shape((strip, rows))] * 2 + [shape((8, lanes), f32)], "last", [finished]
    )
    pairs_count = rows * 4 * x_count * y_count * 2
    return (
        sums[0, 0] / pairs_count,
        grad_image.T,
        grad_text.T,
        scale * sums[1, 0] / pairs_count,
        sums[2, 0] / pairs_count,
    )


def solution(mesh):
    fine = Mesh(mesh.devices.reshape(2, 2, 4, 4, 2, 4), ("zh1", "zh0", "x", "y", "core", "zl"))
    whole = P(("zh1", "zh0", "x", "y", "core"), "zl")
    return jax.shard_map(
        shards,
        mesh=fine,
        in_specs=(whole, whole, P(), P()),
        out_specs=(P(), whole, whole, P(), P()),
        check_vma=False,
    )
```

```python
import functools

import jax
import jax.numpy as jnp
from jax import lax
from jax.experimental import pallas as pl
from jax.experimental.pallas import tpu as pltpu
from jax.sharding import Mesh, PartitionSpec as P

epsilon = 1e-06
lanes = 128
piece = 32
strips = 4
rest = 32
chunk_rows = 72
carry_rows = 16
sent_rows = 88
tiles = 9
vmem = pl.BlockSpec(memory_space=pltpu.VMEM)
smem = pl.BlockSpec(memory_space=pltpu.SMEM)
anywhere = pl.BlockSpec(memory_space=pl.ANY)
limits = pltpu.CompilerParams(vmem_limit_bytes=16 * 1024 * 1024)


def shape(dims, dtype=jnp.bfloat16):
    return jax.ShapeDtypeStruct(tuple(dims), dtype)


def call(kernel, out_shape, name, operands, scalars=(), after=(), flops=0, special=0, scratch=()):
    out_shape = tuple(out_shape)
    scalars, operands, after = tuple(scalars), tuple(operands), tuple(after)
    inputs = len(scalars) + len(operands)
    moved = sum(a.size * a.dtype.itemsize for a in operands + out_shape)

    def body(*refs):
        kernel(*refs[:inputs], *refs[inputs + len(after) :])

    return pl.pallas_call(
        body,
        out_shape=out_shape,
        in_specs=[smem] * len(scalars) + [vmem] * len(operands) + [anywhere] * len(after),
        out_specs=(vmem,) * len(out_shape),
        scratch_shapes=list(scratch),
        compiler_params=limits,
        cost_estimate=pl.CostEstimate(flops=flops, bytes_accessed=moved, transcendentals=special),
        name=name,
    )(*scalars, *operands, *after)


def hold(value, after):
    def body(*refs):
        del refs

    return pl.pallas_call(
        body,
        out_shape=shape(value.shape, value.dtype),
        in_specs=[anywhere] * (1 + len(after)),
        out_specs=anywhere,
        input_output_aliases={0: 0},
        compiler_params=limits,
        name="hold",
    )(value, *after)


def total(values):
    return functools.reduce(lambda a, b: a + b, values)


def wide(ref, *index):
    return ref[index].astype(jnp.float32)


def lane_group():
    return lax.broadcasted_iota(jnp.int32, (8, lanes), 1) // rest


def pack_kernel(image, out):
    whole = wide(image, slice(None)).T
    for k in range(4):
        rows = whole[k * piece : (k + 1) * piece]
        last = rows[:, 2 * lanes :]
        last = jnp.concatenate([last[8 * g : 8 * g + 8] for g in range(4)], axis=1)
        chunk = jnp.concatenate([rows[:, :lanes], rows[:, lanes : 2 * lanes], last], axis=0)
        chunk = chunk.astype(jnp.bfloat16)
        for h in range(out.shape[0] // strips):
            out[h * strips + k] = chunk


def unpack_rows(chunks, group):
    found = []
    lasts = []
    for chunk in chunks:
        found += [chunk[:piece], chunk[piece : 2 * piece]]
        lasts.append(chunk[2 * piece :])
    last = []
    for g in range(4):
        value = jnp.zeros((8, lanes), jnp.float32)
        for s in range(strips):
            turn = rest * (s - g) % lanes
            moved = pltpu.roll(lasts[s], turn, 1) if turn else lasts[s]
            value = jnp.where(group == s, moved, value)
        last.append(value)
    found.append(jnp.concatenate(last, axis=0))
    return found


def units_of(found):
    inverse = lax.rsqrt(jnp.sum(total([t * t for t in found]), axis=1, keepdims=True) + epsilon)
    return [t * inverse for t in found], inverse


def strip_at(place, k):
    return lax.rem(place[0] + (strips - k), strips)


def image_units(place, arrived, h, group):
    chunks = [wide(arrived, h * strips + strip_at(place, k)) for k in range(strips)]
    return units_of(unpack_rows(chunks, group))


def image_unit_kernel(place, arrived, out):
    group = lane_group()
    for h in range(arrived.shape[0] // strips):
        units, _ = image_units(place, arrived, h, group)
        for t in range(tiles):
            value = units[t].astype(jnp.bfloat16)
            for k in range(out.shape[0]):
                out[k, h * piece : (h + 1) * piece, t * lanes : (t + 1) * lanes] = value


def text_units(parts):
    rows = [wide(p, slice(None)).T for p in parts]
    found = []
    for r in rows:
        found += [r[:, :lanes], r[:, lanes : 2 * lanes]]
    found.append(jnp.concatenate([r[:, 2 * lanes :] for r in rows], axis=1))
    return units_of(found)


def text_unit_kernel(p0, p1, p2, p3, out):
    units, _ = text_units((p0, p1, p2, p3))
    for t in range(tiles):
        out[:, t * lanes : (t + 1) * lanes] = units[t].astype(jnp.bfloat16)


def fold(values):
    rows, columns = values.shape
    part = jnp.sum(values.reshape(rows // 8, 8, columns), axis=0)
    return total([part[:, c : c + lanes] for c in range(0, columns, lanes)])


def pair_terms(left, right, scale, bias, same=None):
    product = lax.dot_general(
        left, right, (((1,), (1,)), ((), ())), preferred_element_type=jnp.float32
    )
    logits = scale * product + bias
    if same is None:
        grown = jnp.exp(logits)
        slope = grown / (1.0 + grown)
    else:
        grown = jnp.exp(jnp.where(same, -logits, logits))
        share = grown / (1.0 + grown)
        slope = jnp.where(same, -share, share)
    quarter = left.shape[0] // 4
    a, b, c, d = (grown[k * quarter : (k + 1) * quarter, :] for k in range(4))
    ab = a + (b + a * b)
    cd = c + (d + c * d)
    sums = (fold(jnp.log1p(ab + (cd + ab * cd))), fold(slope * product), fold(slope))
    return (scale * slope).astype(jnp.bfloat16), sums


def write_sums(out, sums, before=None):
    for k in range(3):
        value = total([found[k] for found in sums])
        if before is not None:
            value = value + before[8 * k : 8 * k + 8, :]
        out[8 * k : 8 * k + 8, :] = value


tile = 256


def home_kernel(scales, spot, left, right, weights, sums_out, kept):
    kept[...] = right[...]
    rows, columns = left.shape[0], right.shape[0]
    sums = []
    for start in range(0, rows, tile):
        here = pl.ds(start, tile)
        row = lax.broadcasted_iota(jnp.int32, (tile, 1), 0) + (start - spot[0])
        row = jnp.where((row >= 0) & (row < piece), row, -1)
        column = lax.broadcasted_iota(jnp.int32, (1, columns), 1) - spot[1]
        same = row == jnp.where(column >= 0, column, -2)
        weights[here, :], found = pair_terms(
            left[here, :], right[...], scales[0], scales[1], same
        )
        sums.append(found)
    write_sums(sums_out, sums)


def own_kernel(scales, left, t0, t1, t2, t3, home, home_sums, back, weights, right, sums_out):
    rows, part = left.shape[0], t0.shape[0]
    for k, ref in enumerate((t0, t1, t2, t3)):
        right[k * part : (k + 1) * part, :] = ref[...]
    sums = []
    for start in range(0, rows, tile):
        here = pl.ds(start, tile)
        value, found = pair_terms(left[here, :], right[part:, :], scales[0], scales[1])
        weights[here, :part] = home[here, :]
        weights[here, part:] = value
        back[here, :] = jnp.dot(
            weights[here, :], right[...], preferred_element_type=jnp.float32
        ).astype(jnp.bfloat16)
        sums.append(found)
    write_sums(sums_out, sums, home_sums)


def other_kernel(
    scales, left, right, own_sums, own_weights, own_left, back, sums_out, b0, b1, b2, b3, weights
):
    sums = []
    for start in range(0, left.shape[0], tile):
        here = pl.ds(start, tile)
        value, found = pair_terms(left[here, :], right[...], scales[0], scales[1])
        weights[here, :] = value
        back[here, :] = jnp.dot(
            value, right[...], preferred_element_type=jnp.float32
        ).astype(jnp.bfloat16)
        sums.append(found)
    row = lax.broadcasted_iota(jnp.int32, (8, lanes), 0)
    value = jnp.zeros((8, lanes), jnp.float32)
    for k in range(3):
        found = total([s[k] for s in sums]) + own_sums[8 * k : 8 * k + 8, :]
        value = jnp.where(row == k, jnp.sum(found, axis=0, keepdims=True), value)
    for k in range(sums_out.shape[0]):
        sums_out[k] = value
    contract = (((0,), (0,)), ((), ()))
    part = b0.shape[0]
    value = lax.dot_general(
        own_weights[...], own_left[...], contract, preferred_element_type=jnp.float32
    ) + lax.dot_general(weights[...], left[...], contract, preferred_element_type=jnp.float32)
    for k, out in enumerate((b0, b1, b2, b3)):
        out[...] = value[k * part : (k + 1) * part].astype(jnp.bfloat16)


def three_parts(value):
    high = value.astype(jnp.bfloat16).astype(jnp.float32)
    middle = (value - high).astype(jnp.bfloat16).astype(jnp.float32)
    return high, middle, value - high - middle


def carry_of(value):
    parts = three_parts(jnp.sum(value, axis=1, keepdims=True))
    lane = lax.broadcasted_iota(jnp.int32, (8, lanes), 1)
    carry = jnp.zeros((8, lanes), jnp.float32)
    for k in range(3):
        carry = jnp.where(lane == k, parts[k], carry)
    return jnp.concatenate([carry, jnp.zeros((8, lanes), jnp.float32)], axis=0)


def combine_kernel(own, given, sums, out):
    count, all_rows, _ = out.shape
    block = own.shape[0] // count
    carry = carry_of(total([sums[k] for k in range(sums.shape[0])])).astype(jnp.bfloat16)
    for k in range(count):
        rows = pl.ds(k * block, block)
        for t in range(tiles):
            columns = pl.ds(t * lanes, lanes)
            value = wide(own, rows, columns) + wide(given, rows, columns)
            out[k, t * block : (t + 1) * block, :] = value.astype(jnp.bfloat16)
        out[k, tiles * block : all_rows, :] = carry


def grads_of(units, inverse, grads):
    along = jnp.sum(total([u * g for u, g in zip(units, grads)]), axis=1, keepdims=True)
    return [(g - u * along) * inverse for u, g in zip(units, grads)]


def image_finish_kernel(place, arrived, backs, out):
    group = lane_group()
    count = backs.shape[0]
    heads = arrived.shape[0] // strips
    block = heads * piece
    tail = pl.ds(tiles * block, carry_rows)
    carry = carry_of(total([wide(backs, k, tail, slice(None)) for k in range(count)])[:8])
    for h in range(heads):
        units, inverse = image_units(place, arrived, h, group)
        grads = []
        for t in range(tiles):
            rows = pl.ds(t * block + h * piece, piece)
            grads.append(total([wide(backs, k, rows, slice(None)) for k in range(count)]))
        final = grads_of(units, inverse, grads)
        for s in range(strips):
            last = jnp.zeros((8, lanes), jnp.float32)
            for g in range(4):
                turn = rest * (g - s) % lanes
                rows = final[tiles - 1][8 * g : 8 * g + 8]
                moved = pltpu.roll(rows, turn, 1) if turn else rows
                last = jnp.where(group == g, moved, last)
            chunk = jnp.concatenate([carry, final[2 * s], final[2 * s + 1], last], axis=0)
            out[h * strips + strip_at(place, s)] = chunk.astype(jnp.bfloat16)


def text_finish_kernel(p0, p1, p2, p3, b0, b1, b2, b3, *outs):
    units, inverse = text_units((p0, p1, p2, p3))
    grads = []
    for t in range(tiles):
        columns = pl.ds(t * lanes, lanes)
        grads.append(total([wide(b, slice(None), columns) for b in (b0, b1, b2, b3)]))
    final = grads_of(units, inverse, grads)
    last = final[tiles - 1].T.astype(jnp.bfloat16)
    for s, out in enumerate(outs):
        out[:lanes, :] = final[2 * s].T.astype(jnp.bfloat16)
        out[lanes : 2 * lanes, :] = final[2 * s + 1].T.astype(jnp.bfloat16)
        out[2 * lanes :, :] = last[s * rest : (s + 1) * rest]


def text_last_kernel(g0, g1, g2, g3, out):
    value = total([wide(g, slice(None)) for g in (g0, g1, g2, g3)])
    out[...] = value.astype(jnp.bfloat16)


def image_last_kernel(arrived, out, sums_out):
    values = [wide(arrived, d) for d in range(arrived.shape[0])]
    heads = len(values) // strips
    found = []
    for k in range(strips):
        chunk = total([values[h * strips + k][carry_rows:] for h in range(heads)])
        last = chunk[2 * piece :]
        groups = [last] + [pltpu.roll(last, lanes - rest * g, 1) for g in range(1, 4)]
        last = jnp.concatenate(groups, axis=0)
        found.append((chunk[:piece], chunk[piece : 2 * piece], last))
    for t in range(3):
        rows = jnp.concatenate([f[t] for f in found], axis=0).T
        count = lanes if t < 2 else rest
        out[t * lanes : t * lanes + count, :] = rows[:count].astype(jnp.bfloat16)
    sums = total([v[:8] for v in values])
    sums_out[...] = jnp.broadcast_to(jnp.sum(sums, axis=1, keepdims=True), sums.shape)


def swap_core(value):
    return lax.ppermute(value, "core", [(0, 1), (1, 0)])


def shift(value, axis, k):
    count = lax.axis_size(axis)
    return lax.ppermute(value, axis, [(i, (i + k) % count) for i in range(count)])


def shards(image, text, log_temp, bias):
    rows, strip = image.shape
    x_count, y_count, zh_count = (lax.axis_size(name) for name in ("x", "y", "zh"))
    z_count = zh_count * strips
    width = strip * strips
    block = zh_count * piece
    count = x_count * block
    zh, x, zl = (lax.axis_index(name).astype(jnp.int32) for name in ("zh", "x", "zl"))
    scale = jnp.exp(log_temp)
    scales = jnp.stack([scale, bias])
    place = zl.reshape(1)
    spot = jnp.stack([x * block + zh * piece, zl * piece])
    f32 = jnp.float32

    (packed,) = call(pack_kernel, [shape((z_count, chunk_rows, lanes))], "pack", [image.T])
    parts = [text.T] + [shift(text.T, "zl", k) for k in range(1, strips)]
    arrived = lax.all_to_all(hold(packed, parts[1:]), ("zh", "zl"), 0, 0)
    (home_text,) = call(text_unit_kernel, [shape((block, width))], "text_unit", parts)
    texts = [shift(home_text, "y", k) for k in range(1, y_count)]
    (units,) = call(
        image_unit_kernel,
        [shape((x_count, block, width))],
        "image_unit",
        [arrived],
        scalars=[place],
        after=texts,
    )
    image_rows = lax.all_to_all(units, "x", 0, 0).reshape(count, width)
    other_rows = swap_core(image_rows)

    columns = y_count * block
    area = count * columns
    home_weights, home_sums, home_text = call(
        home_kernel,
        [shape((count, block)), shape((24, lanes), f32), shape((block, width))],
        "home",
        [image_rows, home_text],
        scalars=[scales, spot],
        flops=200 * count * block * width,
    )
    own_back, own_weights, right, own_sums = call(
        own_kernel,
        [
            shape((count, width)),
            shape((count, columns)),
            shape((columns, width)),
            shape((24, lanes), f32),
        ],
        "own",
        [image_rows, home_text] + texts + [home_weights, home_sums],
        scalars=[scales],
        flops=4 * area * width,
        special=2 * area,
    )
    other_back, sums, *text_backs = call(
        other_kernel,
        [shape((count, width)), shape((y_count * 2, 8, lanes), f32)]
        + [shape((block, width))] * y_count,
        "other",
        [other_rows, right, own_sums, own_weights, image_rows],
        scalars=[scales],
        flops=8 * area * width,
        special=2 * area,
        scratch=[pltpu.VMEM((count, columns), jnp.bfloat16)],
    )
    given_back = swap_core(other_back)
    sums = lax.all_to_all(sums, ("y", "core"), 0, 0)
    (combined,) = call(
        combine_kernel,
        [shape((x_count, tiles * block + carry_rows, lanes))],
        "combine",
        [own_back, given_back, sums],
    )
    combined = lax.all_to_all(combined, "x", 0, 0)
    (finished,) = call(
        image_finish_kernel,
        [shape((z_count, sent_rows, lanes))],
        "image_finish",
        [arrived, combined],
        scalars=[place],
        flops=200 * count * block * width,
    )
    moved = [text_backs[0]] + [shift(text_backs[k], "y", -k) for k in range(1, y_count)]
    finished = hold(finished, moved[1:])
    finished = lax.all_to_all(finished, ("zh", "zl"), 0, 0)
    text_parts = call(
        text_finish_kernel, [shape((strip, rows))] * strips, "text_finish", parts + moved
    )
    given = [text_parts[0]] + [shift(text_parts[k], "zl", -k) for k in range(1, strips)]
    (grad_text,) = call(text_last_kernel, [shape((strip, rows))], "text_last", given)
    grad_image, sums = call(
        image_last_kernel, [shape((strip, rows)), shape((8, lanes), f32)], "image_last", [finished]
    )
    pairs_count = rows * 4 * x_count * y_count * 2
    return (
        sums[0, 0] / pairs_count,
        grad_image.T,
        grad_text.T,
        scale * sums[1, 0] / pairs_count,
        sums[2, 0] / pairs_count,
    )


def solution(mesh):
    fine = Mesh(mesh.devices.reshape(4, 4, 4, 2, 4), ("zh", "x", "y", "core", "zl"))
    whole = P(("zh", "x", "y", "core"), "zl")
    return jax.shard_map(
        shards,
        mesh=fine,
        in_specs=(whole, whole, P(), P()),
        out_specs=(P(), whole, whole, P(), P()),
        check_vma=False,
    )
```

```python
import functools

import jax
import jax.numpy as jnp
from jax import lax
from jax.experimental import pallas as pl
from jax.experimental.pallas import tpu as pltpu
from jax.sharding import Mesh, PartitionSpec as P

epsilon = 1e-06
lanes = 128
piece = 32
strips = 4
rest = 32
chunk_rows = 72
carry_rows = 16
in_rows = 368
out_rows = 384
tiles = 9
vmem = pl.BlockSpec(memory_space=pltpu.VMEM)
smem = pl.BlockSpec(memory_space=pltpu.SMEM)
anywhere = pl.BlockSpec(memory_space=pl.ANY)
limits = pltpu.CompilerParams(vmem_limit_bytes=24 * 1024 * 1024)


def shape(dims, dtype=jnp.bfloat16):
    return jax.ShapeDtypeStruct(tuple(dims), dtype)


def call(kernel, out_shape, name, operands, scalars=(), after=(), flops=0, special=0, scratch=()):
    out_shape = tuple(out_shape)
    scalars, operands, after = tuple(scalars), tuple(operands), tuple(after)
    inputs = len(scalars) + len(operands)
    moved = sum(a.size * a.dtype.itemsize for a in operands + out_shape)

    def body(*refs):
        kernel(*refs[:inputs], *refs[inputs + len(after) :])

    return pl.pallas_call(
        body,
        out_shape=out_shape,
        in_specs=[smem] * len(scalars) + [vmem] * len(operands) + [anywhere] * len(after),
        out_specs=(vmem,) * len(out_shape),
        scratch_shapes=list(scratch),
        compiler_params=limits,
        cost_estimate=pl.CostEstimate(flops=flops, bytes_accessed=moved, transcendentals=special),
        name=name,
    )(*scalars, *operands, *after)


def total(values):
    return functools.reduce(lambda a, b: a + b, values)


def wide(ref, *index):
    return ref[index].astype(jnp.float32)


def lane_group():
    return lax.broadcasted_iota(jnp.int32, (8, lanes), 1) // rest


def pack_kernel(image, text, out):
    chunks = []
    for ref in (image, text):
        found = []
        whole = wide(ref, slice(None)).T
        for k in range(4):
            rows = whole[k * piece : (k + 1) * piece]
            last = rows[:, 2 * lanes :]
            last = jnp.concatenate([last[8 * g : 8 * g + 8] for g in range(4)], axis=1)
            found.append(jnp.concatenate([rows[:, :lanes], rows[:, lanes : 2 * lanes], last], axis=0))
        chunks.append(found)
    spare = jnp.zeros((in_rows - 5 * chunk_rows, lanes), jnp.float32)
    for d in range(strips):
        parts = [chunks[0][d]] + chunks[1] + [spare]
        out[d] = jnp.concatenate(parts, axis=0).astype(jnp.bfloat16)


def unpack_rows(chunks, group):
    found = []
    lasts = []
    for chunk in chunks:
        found += [chunk[:piece], chunk[piece : 2 * piece]]
        lasts.append(chunk[2 * piece :])
    last = []
    for g in range(4):
        value = jnp.zeros((8, lanes), jnp.float32)
        for s in range(strips):
            turn = rest * (s - g) % lanes
            moved = pltpu.roll(lasts[s], turn, 1) if turn else lasts[s]
            value = jnp.where(group == s, moved, value)
        last.append(value)
    found.append(jnp.concatenate(last, axis=0))
    return found


def unit_tiles(arrived, c, group):
    chunks = [arrived[s][c * chunk_rows : (c + 1) * chunk_rows] for s in range(strips)]
    found = unpack_rows(chunks, group)
    inverse = lax.rsqrt(jnp.sum(total([t * t for t in found]), axis=1, keepdims=True) + epsilon)
    return [t * inverse for t in found], inverse


def unit_kernel(arrived, image, text):
    group = lane_group()
    values = [wide(arrived, s) for s in range(strips)]
    for c in range(5):
        units, _ = unit_tiles(values, c, group)
        for t in range(tiles):
            columns = pl.ds(t * lanes, lanes)
            if c == 0:
                image[:, columns] = units[t].astype(jnp.bfloat16)
            else:
                text[(c - 1) * piece : c * piece, columns] = units[t].astype(jnp.bfloat16)


def join_image_kernel(own, near, out):
    for k in range(out.shape[0]):
        out[k, :piece, :] = own[...]
        out[k, piece:, :] = near[...]


def join_text_kernel(own, near, out):
    rows = own.shape[0]
    out[:rows, :] = own[...]
    out[rows:, :] = near[...]


def fold(values):
    rows, columns = values.shape
    part = jnp.sum(values.reshape(rows // 8, 8, columns), axis=0)
    return total([part[:, c : c + lanes] for c in range(0, columns, lanes)])


tile = 256


def pair_kernel(scales, spot, left, first, second, out, weights_out, right):
    scale = scales[0]
    bias = scales[1]
    count, block, _ = left.shape
    part = first.shape[0]
    right[:part, :] = first[...]
    right[part:, :] = second[...]
    per_tile = tile // block
    sums = [jnp.zeros((8, lanes), jnp.float32) for _ in range(3)]
    for start in range(0, count, per_tile):
        rows = jnp.concatenate([left[start + k] for k in range(per_tile)], axis=0)
        product = lax.dot_general(
            rows, right[...], (((1,), (1,)), ((), ())), preferred_element_type=jnp.float32
        )
        logits = scale * product + bias
        row = lax.broadcasted_iota(jnp.int32, (tile, 1), 0) + (start * block - spot[0])
        row = jnp.where((row >= 0) & (row < piece), row, -1)
        column = lax.broadcasted_iota(jnp.int32, (1, lanes), 1) - spot[1]
        same = row == jnp.where(column >= 0, column, -2)
        home = logits[:, :lanes]
        grown = jnp.exp(jnp.concatenate([jnp.where(same, -home, home), logits[:, lanes:]], axis=1))
        slope = grown / (1.0 + grown)
        home = slope[:, :lanes]
        slope = jnp.concatenate([jnp.where(same, -home, home), slope[:, lanes:]], axis=1)
        weights = (scale * slope).astype(jnp.bfloat16)
        weights_out[start * block : start * block + tile, :] = weights
        back = jnp.dot(weights, right[...], preferred_element_type=jnp.float32)
        for k in range(per_tile):
            for t in range(tiles):
                out[start + k, t * block : (t + 1) * block, :] = back[
                    k * block : (k + 1) * block, t * lanes : (t + 1) * lanes
                ].astype(jnp.bfloat16)
        quarter = tile // 4
        a, b, c, d = (grown[k * quarter : (k + 1) * quarter, :] for k in range(4))
        ab = a + (b + a * b)
        cd = c + (d + c * d)
        sums[0] += fold(jnp.log1p(ab + (cd + ab * cd)))
        sums[1] += fold(slope * product)
        sums[2] += fold(slope)
    row = lax.broadcasted_iota(jnp.int32, (8, lanes), 0)
    value = jnp.zeros((8, lanes), jnp.float32)
    for k in range(3):
        value = jnp.where(row == k, jnp.sum(sums[k], axis=0, keepdims=True), value)
    carry = carry_of(value).astype(jnp.bfloat16)
    for k in range(count):
        out[k, tiles * block :, :] = carry


def text_kernel(weights, left, own, other):
    count, block, width = left.shape
    part = own.shape[0]
    contract = (((0,), (0,)), ((), ()))
    value = lax.dot_general(
        weights[...], left[...].reshape(count * block, width), contract,
        preferred_element_type=jnp.float32,
    )
    own[...] = value[:part]
    other[...] = value[part:].astype(jnp.bfloat16)


def text_sum_kernel(own, given, kept, sent):
    rows = kept.shape[0]
    kept[...] = own[:rows, :] + wide(given, pl.ds(0, rows), slice(None))
    value = own[rows:, :] + wide(given, pl.ds(rows, rows), slice(None))
    sent[...] = value.astype(jnp.bfloat16)


def three_parts(value):
    high = value.astype(jnp.bfloat16).astype(jnp.float32)
    middle = (value - high).astype(jnp.bfloat16).astype(jnp.float32)
    return high, middle, value - high - middle


def carry_of(value):
    parts = three_parts(jnp.sum(value, axis=1, keepdims=True))
    lane = lax.broadcasted_iota(jnp.int32, (8, lanes), 1)
    carry = jnp.zeros((8, lanes), jnp.float32)
    for k in range(3):
        carry = jnp.where(lane == k, parts[k], carry)
    return jnp.concatenate([carry, jnp.zeros((8, lanes), jnp.float32)], axis=0)


def pack_grads(units, inverse, grads, group):
    along = jnp.sum(total([u * g for u, g in zip(units, grads)]), axis=1, keepdims=True)
    final = [(g - u * along) * inverse for u, g in zip(units, grads)]
    chunks = []
    for s in range(strips):
        last = jnp.zeros((8, lanes), jnp.float32)
        for g in range(4):
            turn = rest * (g - s) % lanes
            rows = final[tiles - 1][8 * g : 8 * g + 8]
            moved = pltpu.roll(rows, turn, 1) if turn else rows
            last = jnp.where(group == g, moved, last)
        chunks.append(jnp.concatenate([final[2 * s], final[2 * s + 1], last], axis=0))
    return chunks


def image_sum_kernel(backs, kept, sent):
    count = backs.shape[0]
    block = 2 * piece
    for t in range(tiles):
        rows = total([wide(backs, k, pl.ds(t * block, block), slice(None)) for k in range(count)])
        kept[t * piece : (t + 1) * piece, :] = rows[:piece]
        sent[t * piece : (t + 1) * piece, :] = rows[piece:].astype(jnp.bfloat16)
    tail = pl.ds(tiles * block, carry_rows)
    carry = carry_of(total([wide(backs, k, tail, slice(None)) for k in range(count)])[:8])
    kept[tiles * piece :, :] = carry
    sent[tiles * piece :, :] = carry.astype(jnp.bfloat16)


def finish_kernel(arrived, image_kept, image_given, text_kept, text_given, near, far, out):
    group = lane_group()
    values = [wide(arrived, s) for s in range(strips)]
    tail = pl.ds(tiles * piece, carry_rows)
    carried = image_kept[tail, :] + wide(image_given, tail, slice(None))
    carry = carry_of((carried + wide(near, slice(None)) + wide(far, slice(None)))[:8])
    spare = jnp.zeros((out_rows - 5 * chunk_rows - carry_rows, lanes), jnp.float32)
    chunks = [[] for _ in range(strips)]
    for c in range(5):
        units, inverse = unit_tiles(values, c, group)
        grads = []
        for t in range(tiles):
            if c == 0:
                rows = pl.ds(t * piece, piece)
                grads.append(image_kept[rows, :] + wide(image_given, rows, slice(None)))
            else:
                rows, columns = pl.ds((c - 1) * piece, piece), pl.ds(t * lanes, lanes)
                grads.append(text_kept[rows, columns] + wide(text_given, rows, columns))
        for s, chunk in enumerate(pack_grads(units, inverse, grads, group)):
            chunks[s].append(chunk)
    for s in range(strips):
        out[s] = jnp.concatenate([carry] + chunks[s] + [spare], axis=0).astype(jnp.bfloat16)


def last_kernel(arrived, image, text, sums_out):
    values = [wide(arrived, s) for s in range(strips)]
    for which, out in enumerate((image, text)):
        found = []
        for k in range(4):
            if which:
                first = carry_rows + (1 + k) * chunk_rows
                chunk = total([v[first : first + chunk_rows] for v in values])
            else:
                chunk = values[k][carry_rows : carry_rows + chunk_rows]
            last = chunk[2 * piece :]
            groups = [last] + [pltpu.roll(last, lanes - rest * g, 1) for g in range(1, 4)]
            last = jnp.concatenate(groups, axis=0)
            found.append((chunk[:piece], chunk[piece : 2 * piece], last))
        for t in range(3):
            rows = jnp.concatenate([f[t] for f in found], axis=0).T
            size = lanes if t < 2 else rest
            out[t * lanes : t * lanes + size, :] = rows[:size].astype(jnp.bfloat16)
    sums = jnp.sum(total([v[:8] for v in values]), axis=1, keepdims=True)
    sums_out[...] = jnp.broadcast_to(sums, sums_out.shape)


def swap_core(value):
    return lax.ppermute(value, "core", [(0, 1), (1, 0)])


def shift(value, axis, k):
    count = lax.axis_size(axis)
    return lax.ppermute(value, axis, [(i, (i + k) % count) for i in range(count)])


def swap_image(value):
    return lax.ppermute(value, "zh", [(0, 3), (3, 0), (1, 2), (2, 1)])


def swap_text(value):
    return lax.ppermute(value, "zh", [(0, 1), (1, 0), (2, 3), (3, 2)])


def shards(image, text, log_temp, bias):
    rows, strip = image.shape
    x_count, y_count, zh_count = (lax.axis_size(name) for name in ("x", "y", "zh"))
    width = strip * strips
    block = 2 * piece
    blocks = x_count * y_count
    count = blocks * block
    columns = 4 * rows
    area = count * columns
    x, y, zl = (lax.axis_index(name).astype(jnp.int32) for name in ("x", "y", "zl"))
    scale = jnp.exp(log_temp)
    scales = jnp.stack([scale, bias])
    spot = jnp.stack([(x * y_count + y) * block, zl * piece])
    f32 = jnp.float32

    (packed,) = call(pack_kernel, [shape((strips, in_rows, lanes))], "pack", [image.T, text.T])
    arrived = lax.all_to_all(packed, "zl", 0, 0)
    image_own, text_own = call(
        unit_kernel, [shape((piece, width)), shape((rows, width))], "unit", [arrived]
    )
    image_near = swap_image(image_own)
    text_near = swap_text(text_own)
    (joined,) = call(
        join_image_kernel, [shape((blocks, block, width))], "join_image", [image_own, image_near]
    )
    image_rows = lax.all_to_all(joined, ("x", "y"), 0, 0)
    (text_rows,) = call(
        join_text_kernel, [shape((2 * rows, width))], "join_text", [text_own, text_near]
    )
    text_other = swap_core(text_rows)

    back, weights = call(
        pair_kernel,
        [shape((blocks, tiles * block + carry_rows, lanes)), shape((count, columns))],
        "pair",
        [image_rows, text_rows, text_other],
        scalars=[scales, spot],
        flops=4 * area * width,
        special=2 * area,
        scratch=[pltpu.VMEM((columns, width), jnp.bfloat16)],
    )
    back = lax.all_to_all(back, ("x", "y"), 0, 0)
    text_kept, text_sent = call(
        text_kernel,
        [shape((2 * rows, width), f32), shape((2 * rows, width))],
        "text_back",
        [weights, image_rows],
        flops=2 * area * width,
    )
    text_given = swap_core(text_sent)
    text_kept, text_sent = call(
        text_sum_kernel,
        [shape((rows, width), f32), shape((rows, width))],
        "text_sum",
        [text_kept, text_given],
    )
    text_given = swap_text(text_sent)
    sums_rows = tiles * piece + carry_rows
    image_kept, image_sent = call(
        image_sum_kernel,
        [shape((sums_rows, lanes), f32), shape((sums_rows, lanes))],
        "image_sum",
        [back],
    )
    image_given = swap_image(image_sent)
    carry = image_sent[tiles * piece :]
    near = swap_text(carry)
    far = shift(carry, "zh", 2)
    (finished,) = call(
        finish_kernel,
        [shape((strips, out_rows, lanes))],
        "finish",
        [arrived, image_kept, image_given, text_kept, text_given, near, far],
    )
    finished = lax.all_to_all(finished, "zl", 0, 0)
    grad_image, grad_text, sums = call(
        last_kernel, [shape((strip, rows))] * 2 + [shape((8, lanes), f32)], "last", [finished]
    )
    sums = (sums + swap_core(sums))[:, 0]
    pairs_count = rows * zh_count * blocks * 2
    return (
        sums[0] / pairs_count,
        grad_image.T,
        grad_text.T,
        scale * sums[1] / pairs_count,
        sums[2] / pairs_count,
    )


def solution(mesh):
    fine = Mesh(mesh.devices.reshape(4, 4, 4, 2, 4), ("zh", "x", "y", "core", "zl"))
    whole = P(("zh", "x", "y", "core"), "zl")
    return jax.shard_map(
        shards,
        mesh=fine,
        in_specs=(whole, whole, P(), P()),
        out_specs=(P(), whole, whole, P(), P()),
        check_vma=False,
    )
```

```python
import functools

import jax
import jax.numpy as jnp
from jax import lax
from jax.experimental import pallas as pl
from jax.experimental.pallas import tpu as pltpu
from jax.sharding import Mesh, PartitionSpec as P

epsilon = 1e-06
lanes = 128
piece = 32
strips = 4
rest = 32
chunk_rows = 72
carry_rows = 16
chunk_total = 368
strip_rows = 304
tiles = 9
vmem = pl.BlockSpec(memory_space=pltpu.VMEM)
smem = pl.BlockSpec(memory_space=pltpu.SMEM)
anywhere = pl.BlockSpec(memory_space=pl.ANY)
mebibyte = 1024 * 1024


def shape(dims, dtype=jnp.bfloat16):
    return jax.ShapeDtypeStruct(tuple(dims), dtype)


def call(
    kernel,
    out_shape,
    name,
    operands,
    scalars=(),
    after=(),
    flops=0,
    special=0,
    scratch=(),
    out_specs=None,
    limit=24,
):
    out_shape = tuple(out_shape)
    scalars, operands, after = tuple(scalars), tuple(operands), tuple(after)
    inputs = len(scalars) + len(operands)
    moved = sum(a.size * a.dtype.itemsize for a in operands + out_shape)

    def body(*refs):
        kernel(*refs[:inputs], *refs[inputs + len(after) :])

    return pl.pallas_call(
        body,
        out_shape=out_shape,
        in_specs=[smem] * len(scalars) + [vmem] * len(operands) + [anywhere] * len(after),
        out_specs=out_specs or (vmem,) * len(out_shape),
        scratch_shapes=list(scratch),
        compiler_params=pltpu.CompilerParams(vmem_limit_bytes=limit * mebibyte),
        cost_estimate=pl.CostEstimate(flops=flops, bytes_accessed=moved, transcendentals=special),
        name=name,
    )(*scalars, *operands, *after)


def total(values):
    return functools.reduce(lambda a, b: a + b, values)


def wide(ref, *index):
    return ref[index].astype(jnp.float32)


def lane_group():
    return lax.broadcasted_iota(jnp.int32, (8, lanes), 1) // rest


def pack_kernel(image, text, out):
    chunks = []
    for ref in (image, text):
        found = []
        whole = wide(ref, slice(None)).T
        for k in range(4):
            rows = whole[k * piece : (k + 1) * piece]
            last = rows[:, 2 * lanes :]
            last = jnp.concatenate([last[8 * g : 8 * g + 8] for g in range(4)], axis=1)
            found.append(jnp.concatenate([rows[:, :lanes], rows[:, lanes : 2 * lanes], last], axis=0))
        chunks.append(found)
    spare = jnp.zeros((chunk_total - 5 * chunk_rows, lanes), jnp.float32)
    for d in range(strips):
        parts = [chunks[0][d]] + chunks[1] + [spare]
        out[d] = jnp.concatenate(parts, axis=0).astype(jnp.bfloat16)


def unpack_rows(chunks, group):
    found = []
    lasts = []
    for chunk in chunks:
        found += [chunk[:piece], chunk[piece : 2 * piece]]
        lasts.append(chunk[2 * piece :])
    last = []
    for g in range(4):
        value = jnp.zeros((8, lanes), jnp.float32)
        for s in range(strips):
            turn = rest * (s - g) % lanes
            moved = pltpu.roll(lasts[s], turn, 1) if turn else lasts[s]
            value = jnp.where(group == s, moved, value)
        last.append(value)
    found.append(jnp.concatenate(last, axis=0))
    return found


def units_of(found):
    inverse = lax.rsqrt(jnp.sum(total([t * t for t in found]), axis=1, keepdims=True) + epsilon)
    return [t * inverse for t in found], inverse


def strip_at(place, k):
    return lax.rem(place[0] + (strips - k), strips)


def read_strips(place, arrived):
    return [wide(arrived, strip_at(place, k)) for k in range(strips)]


def unit_tiles(values, c, group):
    return units_of(unpack_rows([v[c * chunk_rows : (c + 1) * chunk_rows] for v in values], group))


def unit_kernel(place, arrived, image, text):
    group = lane_group()
    values = read_strips(place, arrived)
    for c in range(5):
        units, _ = unit_tiles(values, c, group)
        for t in range(tiles):
            columns = pl.ds(t * lanes, lanes)
            if c == 0:
                image[:, columns] = units[t].astype(jnp.bfloat16)
            else:
                text[(c - 1) * piece : c * piece, columns] = units[t].astype(jnp.bfloat16)


def text_units(parts):
    rows = [wide(p, slice(None)).T for p in parts]
    found = []
    for r in rows:
        found += [r[:, :lanes], r[:, lanes : 2 * lanes]]
    found.append(jnp.concatenate([r[:, 2 * lanes :] for r in rows], axis=1))
    return units_of(found)


def text_rows_kernel(own, p0, p1, p2, p3, out):
    rows = own.shape[0]
    out[:rows, :] = own[...]
    units, _ = text_units((p0, p1, p2, p3))
    for t in range(tiles):
        out[rows:, t * lanes : (t + 1) * lanes] = units[t].astype(jnp.bfloat16)


def join_image_kernel(own, near, out):
    for k in range(out.shape[0]):
        out[k, :piece, :] = own[...]
        out[k, piece:, :] = near[...]


def fold(values):
    rows, columns = values.shape
    part = jnp.sum(values.reshape(rows // 8, 8, columns), axis=0)
    return total([part[:, c : c + lanes] for c in range(0, columns, lanes)])


tile = 256


def pair_kernel(
    scales, spot, left, first, second, out, weights_out, sums_out, right, buffer, semaphores
):
    scale = scales[0]
    bias = scales[1]
    count, block, _ = left.shape
    part = first.shape[0]
    right[:part, :] = first[...]
    right[part:, :] = second[...]
    per_tile = tile // block
    copies = []
    sums = [jnp.zeros((8, lanes), jnp.float32) for _ in range(3)]
    for start in range(0, count, per_tile):
        rows = jnp.concatenate([left[start + k] for k in range(per_tile)], axis=0)
        product = lax.dot_general(
            rows, right[...], (((1,), (1,)), ((), ())), preferred_element_type=jnp.float32
        )
        logits = scale * product + bias
        row = lax.broadcasted_iota(jnp.int32, (tile, 1), 0) + (start * block - spot[0])
        row = jnp.where((row >= 0) & (row < piece), row, -1)
        column = lax.broadcasted_iota(jnp.int32, (1, lanes), 1) - spot[1]
        same = row == jnp.where(column >= 0, column, -2)
        home = logits[:, :lanes]
        grown = jnp.exp(jnp.concatenate([jnp.where(same, -home, home), logits[:, lanes:]], axis=1))
        slope = grown / (1.0 + grown)
        home = slope[:, :lanes]
        slope = jnp.concatenate([jnp.where(same, -home, home), slope[:, lanes:]], axis=1)
        weights = (scale * slope).astype(jnp.bfloat16)
        weights_out[start * block : start * block + tile, :] = weights
        back = jnp.dot(weights, right[...], preferred_element_type=jnp.float32)
        slot = len(copies) % 2
        if len(copies) > 1:
            copies[-2].wait()
        for k in range(per_tile):
            for t in range(tiles):
                buffer[slot, k, t * block : (t + 1) * block, :] = back[
                    k * block : (k + 1) * block, t * lanes : (t + 1) * lanes
                ].astype(jnp.bfloat16)
        copies.append(
            pltpu.make_async_copy(
                buffer.at[slot], out.at[pl.ds(start, per_tile)], semaphores.at[slot]
            )
        )
        copies[-1].start()
        quarter = tile // 4
        a, b, c, d = (grown[k * quarter : (k + 1) * quarter, :] for k in range(4))
        ab = a + (b + a * b)
        cd = c + (d + c * d)
        sums[0] += fold(jnp.log1p(ab + (cd + ab * cd)))
        sums[1] += fold(slope * product)
        sums[2] += fold(slope)
    row = lax.broadcasted_iota(jnp.int32, (8, lanes), 0)
    value = jnp.zeros((8, lanes), jnp.float32)
    for k in range(3):
        value = jnp.where(row == k, jnp.sum(sums[k], axis=0, keepdims=True), value)
    sums_out[...] = value
    for copy in copies[-2:]:
        copy.wait()


def text_kernel(weights, left, sums, sums_given, own, other, sums_out):
    count, block, width = left.shape
    part = own.shape[0]
    contract = (((0,), (0,)), ((), ()))
    value = lax.dot_general(
        weights[...],
        left[...].reshape(count * block, width),
        contract,
        preferred_element_type=jnp.float32,
    )
    own[...] = value[:part]
    other[:part, :] = value[part:].astype(jnp.bfloat16)
    sums_now = carry_of(sums[...] + sums_given[...])
    sums_out[...] = sums_now
    other[part:, :lanes] = sums_now.astype(jnp.bfloat16)
    other[part:, lanes:] = jnp.zeros((carry_rows, width - lanes), jnp.bfloat16)


def text_sum_kernel(own, given, sums, p0, p1, p2, p3, kept, *outs):
    rows = kept.shape[0]
    kept[...] = own[:rows, :] + wide(given, pl.ds(0, rows), slice(None))
    units, inverse = text_units((p0, p1, p2, p3))
    here = pl.ds(rows, rows)
    grads = []
    for t in range(tiles):
        columns = pl.ds(t * lanes, lanes)
        grads.append(own[here, columns] + wide(given, here, columns))
    final = grads_of(units, inverse, grads)
    carry = sums[...] + wide(given, pl.ds(2 * rows, carry_rows), pl.ds(0, lanes))
    carry = carry_of(carry[:8])
    last = final[tiles - 1].T
    for k, out in enumerate(outs):
        parts = [final[2 * k].T, final[2 * k + 1].T, last[k * rest : (k + 1) * rest], carry]
        out[...] = jnp.concatenate(parts, axis=0).astype(jnp.bfloat16)


def strip_sum_kernel(g0, g1, g2, g3, out):
    value = total([wide(g, slice(None)) for g in (g0, g1, g2, g3)])
    strip = strip_rows - carry_rows
    out[:strip, :] = value[:strip].astype(jnp.bfloat16)
    out[strip:, :] = carry_of(value[strip : strip + 8]).astype(jnp.bfloat16)


def sums_kernel(own, given, out):
    tail = pl.ds(strip_rows - carry_rows, carry_rows)
    value = (wide(own, tail, slice(None)) + wide(given, tail, slice(None)))[:8]
    for k in range(out.shape[0]):
        out[k] = value


def three_parts(value):
    high = value.astype(jnp.bfloat16).astype(jnp.float32)
    middle = (value - high).astype(jnp.bfloat16).astype(jnp.float32)
    return high, middle, value - high - middle


def carry_of(value):
    parts = three_parts(jnp.sum(value, axis=1, keepdims=True))
    lane = lax.broadcasted_iota(jnp.int32, (8, lanes), 1)
    carry = jnp.zeros((8, lanes), jnp.float32)
    for k in range(3):
        carry = jnp.where(lane == k, parts[k], carry)
    return jnp.concatenate([carry, jnp.zeros((8, lanes), jnp.float32)], axis=0)


def grads_of(units, inverse, grads):
    along = jnp.sum(total([u * g for u, g in zip(units, grads)]), axis=1, keepdims=True)
    return [(g - u * along) * inverse for u, g in zip(units, grads)]


def pack_grads(units, inverse, grads, group):
    final = grads_of(units, inverse, grads)
    chunks = []
    for s in range(strips):
        last = jnp.zeros((8, lanes), jnp.float32)
        for g in range(4):
            turn = rest * (g - s) % lanes
            rows = final[tiles - 1][8 * g : 8 * g + 8]
            moved = pltpu.roll(rows, turn, 1) if turn else rows
            last = jnp.where(group == g, moved, last)
        chunks.append(jnp.concatenate([final[2 * s], final[2 * s + 1], last], axis=0))
    return chunks


def image_sum_kernel(backs, kept, sent):
    count = backs.shape[0]
    block = 2 * piece
    for t in range(tiles):
        rows = total([wide(backs, k, pl.ds(t * block, block), slice(None)) for k in range(count)])
        kept[t * piece : (t + 1) * piece, :] = rows[:piece]
        sent[t * piece : (t + 1) * piece, :] = rows[piece:].astype(jnp.bfloat16)


def finish_kernel(place, arrived, image_kept, image_given, text_kept, out):
    group = lane_group()
    values = read_strips(place, arrived)
    spare = jnp.zeros((chunk_total - 5 * chunk_rows, lanes), jnp.float32)
    chunks = [[] for _ in range(strips)]
    for c in range(5):
        units, inverse = unit_tiles(values, c, group)
        grads = []
        for t in range(tiles):
            if c == 0:
                rows = pl.ds(t * piece, piece)
                grads.append(image_kept[rows, :] + wide(image_given, rows, slice(None)))
            else:
                rows, columns = pl.ds((c - 1) * piece, piece), pl.ds(t * lanes, lanes)
                grads.append(text_kept[rows, columns])
        for s, chunk in enumerate(pack_grads(units, inverse, grads, group)):
            chunks[s].append(chunk)
    for s in range(strips):
        value = jnp.concatenate(chunks[s] + [spare], axis=0)
        out[strip_at(place, s)] = value.astype(jnp.bfloat16)


def last_kernel(arrived, text_given, sums, image, text, sums_out):
    values = [wide(arrived, s) for s in range(strips)]
    for which, out in enumerate((image, text)):
        found = []
        for k in range(4):
            if which:
                first = (1 + k) * chunk_rows
                chunk = total([v[first : first + chunk_rows] for v in values])
            else:
                chunk = values[k][:chunk_rows]
            last = chunk[2 * piece :]
            groups = [last] + [pltpu.roll(last, lanes - rest * g, 1) for g in range(1, 4)]
            last = jnp.concatenate(groups, axis=0)
            found.append((chunk[:piece], chunk[piece : 2 * piece], last))
        for t in range(3):
            rows = jnp.concatenate([f[t] for f in found], axis=0).T
            here = pl.ds(t * lanes, lanes if t < 2 else rest)
            rows = rows[: here.size]
            if which:
                rows = rows + wide(text_given, here, slice(None))
            out[here, :] = rows.astype(jnp.bfloat16)
    value = total([sums[k] for k in range(sums.shape[0])])
    sums_out[...] = jnp.broadcast_to(jnp.sum(value, axis=1, keepdims=True), value.shape)


def swap_core(value):
    return lax.ppermute(value, "core", [(0, 1), (1, 0)])


def shift(value, axis, k):
    count = lax.axis_size(axis)
    return lax.ppermute(value, axis, [(i, (i + k) % count) for i in range(count)])


def swap_image(value):
    return lax.ppermute(value, "zh", [(0, 3), (3, 0), (1, 2), (2, 1)])


def swap_text(value):
    return lax.ppermute(value, "zh", [(0, 1), (1, 0), (2, 3), (3, 2)])


def shards(image, text, log_temp, bias):
    rows, strip = image.shape
    x_count, y_count, zh_count = (lax.axis_size(name) for name in ("x", "y", "zh"))
    width = strip * strips
    block = 2 * piece
    blocks = x_count * y_count
    count = blocks * block
    columns = 4 * rows
    area = count * columns
    place = lax.axis_index("zl").astype(jnp.int32).reshape(1)
    x, y, zl = (lax.axis_index(name).astype(jnp.int32) for name in ("x", "y", "zl"))
    scale = jnp.exp(log_temp)
    scales = jnp.stack([scale, bias])
    spot = jnp.stack([(x * y_count + y) * block, zl * piece])
    f32 = jnp.float32

    strip_near = swap_text(text.T)
    (packed,) = call(pack_kernel, [shape((strips, chunk_total, lanes))], "pack", [image.T, text.T])
    arrived = lax.all_to_all(packed, "zl", 0, 0)
    image_own, text_own = call(
        unit_kernel,
        [shape((piece, width)), shape((rows, width))],
        "unit",
        [arrived],
        scalars=[place],
        after=[strip_near],
    )
    image_near = swap_image(image_own)
    (joined,) = call(
        join_image_kernel, [shape((blocks, block, width))], "join_image", [image_own, image_near]
    )
    image_rows = lax.all_to_all(joined, ("x", "y"), 0, 0)
    parts = [strip_near] + [shift(strip_near, "zl", k) for k in range(1, strips)]
    (text_rows,) = call(
        text_rows_kernel, [shape((2 * rows, width))], "text_rows", [text_own] + parts
    )
    text_other = swap_core(text_rows)

    back, weights, sums = call(
        pair_kernel,
        [
            shape((blocks, tiles * block, lanes)),
            shape((count, columns)),
            shape((8, lanes), f32),
        ],
        "pair",
        [image_rows, text_rows, text_other],
        scalars=[scales, spot],
        flops=4 * area * width,
        special=2 * area,
        scratch=[
            pltpu.VMEM((columns, width), jnp.bfloat16),
            pltpu.VMEM((2, tile // block, tiles * block, lanes), jnp.bfloat16),
            pltpu.SemaphoreType.DMA((2,)),
        ],
        out_specs=(pl.BlockSpec(memory_space=pltpu.HBM), vmem, vmem),
        limit=58,
    )
    back = lax.all_to_all(back, ("x", "y"), 0, 0)
    sums_given = swap_image(sums)
    text_kept, text_sent, sums = call(
        text_kernel,
        [
            shape((2 * rows, width), f32),
            shape((2 * rows + carry_rows, width)),
            shape((carry_rows, lanes), f32),
        ],
        "text_back",
        [weights, image_rows, sums, sums_given],
        flops=2 * area * width,
    )
    text_given = swap_core(text_sent)
    text_kept, *near_strips = call(
        text_sum_kernel,
        [shape((rows, width), f32)] + [shape((strip_rows, lanes))] * strips,
        "text_sum",
        [text_kept, text_given, sums] + parts,
    )
    near_strips = [near_strips[0]] + [
        shift(near_strips[k], "zl", -k) for k in range(1, strips)
    ]
    (strip_sent,) = call(
        strip_sum_kernel, [shape((strip_rows, lanes))], "strip_sum", near_strips
    )
    strip_given = swap_text(strip_sent)
    image_kept, image_sent = call(
        image_sum_kernel,
        [shape((tiles * piece, lanes), f32), shape((tiles * piece, lanes))],
        "image_sum",
        [back],
    )
    image_given = swap_image(image_sent)
    (sums,) = call(
        sums_kernel,
        [shape((blocks, 8, lanes), f32)],
        "sums",
        [strip_sent, strip_given],
        after=[image_sent],
    )
    sums = lax.all_to_all(sums, ("x", "y"), 0, 0)
    (finished,) = call(
        finish_kernel,
        [shape((strips, chunk_total, lanes))],
        "finish",
        [arrived, image_kept, image_given, text_kept],
        scalars=[place],
        after=[sums],
    )
    finished = lax.all_to_all(finished, "zl", 0, 0)
    grad_image, grad_text, sums = call(
        last_kernel,
        [shape((strip, rows))] * 2 + [shape((8, lanes), f32)],
        "last",
        [finished, strip_given, sums],
    )
    sums = sums[:, 0]
    pairs_count = rows * zh_count * blocks * 2
    return (
        sums[0] / pairs_count,
        grad_image.T,
        grad_text.T,
        scale * sums[1] / pairs_count,
        sums[2] / pairs_count,
    )


def solution(mesh):
    fine = Mesh(mesh.devices.reshape(4, 4, 4, 2, 4), ("zh", "x", "y", "core", "zl"))
    whole = P(("zh", "x", "y", "core"), "zl")
    return jax.shard_map(
        shards,
        mesh=fine,
        in_specs=(whole, whole, P(), P()),
        out_specs=(P(), whole, whole, P(), P()),
        check_vma=False,
    )
```

```python
import functools

import jax
import jax.numpy as jnp
from jax import lax
from jax.experimental import pallas as pl
from jax.experimental.pallas import tpu as pltpu
from jax.sharding import Mesh, PartitionSpec as P

epsilon = 1e-06
lanes = 128
piece = 32
strips = 4
rest = 32
chunk_rows = 72
carry_rows = 16
sent_rows = 88
tiles = 9
vmem = pl.BlockSpec(memory_space=pltpu.VMEM)
smem = pl.BlockSpec(memory_space=pltpu.SMEM)
anywhere = pl.BlockSpec(memory_space=pl.ANY)
limits = pltpu.CompilerParams(vmem_limit_bytes=16 * 1024 * 1024)


def shape(dims, dtype=jnp.bfloat16):
    return jax.ShapeDtypeStruct(tuple(dims), dtype)


def call(kernel, out_shape, name, operands, scalars=(), after=(), flops=0, special=0, scratch=()):
    out_shape = tuple(out_shape)
    scalars, operands, after = tuple(scalars), tuple(operands), tuple(after)
    inputs = len(scalars) + len(operands)
    moved = sum(a.size * a.dtype.itemsize for a in operands + out_shape)

    def body(*refs):
        kernel(*refs[:inputs], *refs[inputs + len(after) :])

    return pl.pallas_call(
        body,
        out_shape=out_shape,
        in_specs=[smem] * len(scalars) + [vmem] * len(operands) + [anywhere] * len(after),
        out_specs=(vmem,) * len(out_shape),
        scratch_shapes=list(scratch),
        compiler_params=limits,
        cost_estimate=pl.CostEstimate(flops=flops, bytes_accessed=moved, transcendentals=special),
        name=name,
    )(*scalars, *operands, *after)


def hold(value, after):
    def body(*refs):
        del refs

    return pl.pallas_call(
        body,
        out_shape=shape(value.shape, value.dtype),
        in_specs=[anywhere] * (1 + len(after)),
        out_specs=anywhere,
        input_output_aliases={0: 0},
        compiler_params=limits,
        name="hold",
    )(value, *after)


def total(values):
    return functools.reduce(lambda a, b: a + b, values)


def wide(ref, *index):
    return ref[index].astype(jnp.float32)


def lane_group():
    return lax.broadcasted_iota(jnp.int32, (8, lanes), 1) // rest


def pack_kernel(image, out):
    whole = wide(image, slice(None)).T
    for k in range(4):
        rows = whole[k * piece : (k + 1) * piece]
        last = rows[:, 2 * lanes :]
        last = jnp.concatenate([last[8 * g : 8 * g + 8] for g in range(4)], axis=1)
        chunk = jnp.concatenate([rows[:, :lanes], rows[:, lanes : 2 * lanes], last], axis=0)
        chunk = chunk.astype(jnp.bfloat16)
        for h in range(out.shape[0] // strips):
            out[h * strips + k] = chunk


def unpack_rows(chunks, group):
    found = []
    lasts = []
    for chunk in chunks:
        found += [chunk[:piece], chunk[piece : 2 * piece]]
        lasts.append(chunk[2 * piece :])
    last = []
    for g in range(4):
        value = jnp.zeros((8, lanes), jnp.float32)
        for s in range(strips):
            turn = rest * (s - g) % lanes
            moved = pltpu.roll(lasts[s], turn, 1) if turn else lasts[s]
            value = jnp.where(group == s, moved, value)
        last.append(value)
    found.append(jnp.concatenate(last, axis=0))
    return found


def units_of(found):
    inverse = lax.rsqrt(jnp.sum(total([t * t for t in found]), axis=1, keepdims=True) + epsilon)
    return [t * inverse for t in found], inverse


def strip_at(place, k):
    return lax.rem(place[0] + (strips - k), strips)


def image_units(place, arrived, h, group):
    chunks = [wide(arrived, h * strips + strip_at(place, k)) for k in range(strips)]
    return units_of(unpack_rows(chunks, group))


def image_unit_kernel(place, arrived, out):
    group = lane_group()
    for h in range(arrived.shape[0] // strips):
        units, _ = image_units(place, arrived, h, group)
        for t in range(tiles):
            value = units[t].astype(jnp.bfloat16)
            for k in range(out.shape[0]):
                out[k, h * piece : (h + 1) * piece, t * lanes : (t + 1) * lanes] = value


def text_units(parts):
    rows = [wide(p, slice(None)).T for p in parts]
    found = []
    for r in rows:
        found += [r[:, :lanes], r[:, lanes : 2 * lanes]]
    found.append(jnp.concatenate([r[:, 2 * lanes :] for r in rows], axis=1))
    return units_of(found)


def text_unit_kernel(p0, p1, p2, p3, out):
    units, _ = text_units((p0, p1, p2, p3))
    for t in range(tiles):
        out[:, t * lanes : (t + 1) * lanes] = units[t].astype(jnp.bfloat16)


def fold(values):
    rows, columns = values.shape
    part = jnp.sum(values.reshape(rows // 8, 8, columns), axis=0)
    return total([part[:, c : c + lanes] for c in range(0, columns, lanes)])


def pair_terms(left, right, scale, bias, same=None):
    product = lax.dot_general(
        left, right, (((1,), (1,)), ((), ())), preferred_element_type=jnp.float32
    )
    logits = scale * product + bias
    if same is None:
        grown = jnp.exp(logits)
        slope = grown / (1.0 + grown)
    else:
        grown = jnp.exp(jnp.where(same, -logits, logits))
        share = grown / (1.0 + grown)
        slope = jnp.where(same, -share, share)
    quarter = left.shape[0] // 4
    a, b, c, d = (grown[k * quarter : (k + 1) * quarter, :] for k in range(4))
    ab = a + (b + a * b)
    cd = c + (d + c * d)
    sums = (fold(jnp.log1p(ab + (cd + ab * cd))), fold(slope * product), fold(slope))
    return (scale * slope).astype(jnp.bfloat16), sums


def write_sums(out, sums, before=None):
    for k in range(3):
        value = total([found[k] for found in sums])
        if before is not None:
            value = value + before[8 * k : 8 * k + 8, :]
        out[8 * k : 8 * k + 8, :] = value


tile = 256


def home_kernel(scales, spot, left, right, weights, sums_out, kept):
    kept[...] = right[...]
    rows, columns = left.shape[0], right.shape[0]
    sums = []
    for start in range(0, rows, tile):
        here = pl.ds(start, tile)
        row = lax.broadcasted_iota(jnp.int32, (tile, 1), 0) + (start - spot[0])
        row = jnp.where((row >= 0) & (row < piece), row, -1)
        column = lax.broadcasted_iota(jnp.int32, (1, columns), 1) - spot[1]
        same = row == jnp.where(column >= 0, column, -2)
        weights[here, :], found = pair_terms(
            left[here, :], right[...], scales[0], scales[1], same
        )
        sums.append(found)
    write_sums(sums_out, sums)


def own_kernel(scales, left, t0, t1, t2, t3, home, home_sums, back, weights, right, sums_out):
    rows, part = left.shape[0], t0.shape[0]
    for k, ref in enumerate((t0, t1, t2, t3)):
        right[k * part : (k + 1) * part, :] = ref[...]
    sums = []
    for start in range(0, rows, tile):
        here = pl.ds(start, tile)
        value, found = pair_terms(left[here, :], right[part:, :], scales[0], scales[1])
        weights[here, :part] = home[here, :]
        weights[here, part:] = value
        back[here, :] = jnp.dot(
            weights[here, :], right[...], preferred_element_type=jnp.float32
        ).astype(jnp.bfloat16)
        sums.append(found)
    write_sums(sums_out, sums, home_sums)


def other_kernel(
    scales, left, right, own_sums, own_weights, own_left, back, sums_out, b0, b1, b2, b3, weights
):
    sums = []
    for start in range(0, left.shape[0], tile):
        here = pl.ds(start, tile)
        value, found = pair_terms(left[here, :], right[...], scales[0], scales[1])
        weights[here, :] = value
        back[here, :] = jnp.dot(
            value, right[...], preferred_element_type=jnp.float32
        ).astype(jnp.bfloat16)
        sums.append(found)
    row = lax.broadcasted_iota(jnp.int32, (8, lanes), 0)
    value = jnp.zeros((8, lanes), jnp.float32)
    for k in range(3):
        found = total([s[k] for s in sums]) + own_sums[8 * k : 8 * k + 8, :]
        value = jnp.where(row == k, jnp.sum(found, axis=0, keepdims=True), value)
    for k in range(sums_out.shape[0]):
        sums_out[k] = value
    contract = (((0,), (0,)), ((), ()))
    part = b0.shape[0]
    value = lax.dot_general(
        own_weights[...], own_left[...], contract, preferred_element_type=jnp.float32
    ) + lax.dot_general(weights[...], left[...], contract, preferred_element_type=jnp.float32)
    for k, out in enumerate((b0, b1, b2, b3)):
        out[...] = value[k * part : (k + 1) * part].astype(jnp.bfloat16)


def three_parts(value):
    high = value.astype(jnp.bfloat16).astype(jnp.float32)
    middle = (value - high).astype(jnp.bfloat16).astype(jnp.float32)
    return high, middle, value - high - middle


def carry_of(value):
    parts = three_parts(jnp.sum(value, axis=1, keepdims=True))
    lane = lax.broadcasted_iota(jnp.int32, (8, lanes), 1)
    carry = jnp.zeros((8, lanes), jnp.float32)
    for k in range(3):
        carry = jnp.where(lane == k, parts[k], carry)
    return jnp.concatenate([carry, jnp.zeros((8, lanes), jnp.float32)], axis=0)


def combine_kernel(own, given, sums, out):
    count, all_rows, _ = out.shape
    block = own.shape[0] // count
    carry = carry_of(total([sums[k] for k in range(sums.shape[0])])).astype(jnp.bfloat16)
    for k in range(count):
        rows = pl.ds(k * block, block)
        for t in range(tiles):
            columns = pl.ds(t * lanes, lanes)
            value = wide(own, rows, columns) + wide(given, rows, columns)
            out[k, t * block : (t + 1) * block, :] = value.astype(jnp.bfloat16)
        out[k, tiles * block : all_rows, :] = carry


def grads_of(units, inverse, grads):
    along = jnp.sum(total([u * g for u, g in zip(units, grads)]), axis=1, keepdims=True)
    return [(g - u * along) * inverse for u, g in zip(units, grads)]


def image_finish_kernel(place, arrived, backs, out):
    group = lane_group()
    count = backs.shape[0]
    heads = arrived.shape[0] // strips
    block = heads * piece
    tail = pl.ds(tiles * block, carry_rows)
    carry = carry_of(total([wide(backs, k, tail, slice(None)) for k in range(count)])[:8])
    for h in range(heads):
        units, inverse = image_units(place, arrived, h, group)
        grads = []
        for t in range(tiles):
            rows = pl.ds(t * block + h * piece, piece)
            grads.append(total([wide(backs, k, rows, slice(None)) for k in range(count)]))
        final = grads_of(units, inverse, grads)
        for s in range(strips):
            last = jnp.zeros((8, lanes), jnp.float32)
            for g in range(4):
                turn = rest * (g - s) % lanes
                rows = final[tiles - 1][8 * g : 8 * g + 8]
                moved = pltpu.roll(rows, turn, 1) if turn else rows
                last = jnp.where(group == g, moved, last)
            chunk = jnp.concatenate([carry, final[2 * s], final[2 * s + 1], last], axis=0)
            out[h * strips + strip_at(place, s)] = chunk.astype(jnp.bfloat16)


def text_finish_kernel(p0, p1, p2, p3, b0, b1, b2, b3, *outs):
    units, inverse = text_units((p0, p1, p2, p3))
    grads = []
    for t in range(tiles):
        columns = pl.ds(t * lanes, lanes)
        grads.append(total([wide(b, slice(None), columns) for b in (b0, b1, b2, b3)]))
    final = grads_of(units, inverse, grads)
    last = final[tiles - 1].T.astype(jnp.bfloat16)
    for s, out in enumerate(outs):
        out[:lanes, :] = final[2 * s].T.astype(jnp.bfloat16)
        out[lanes : 2 * lanes, :] = final[2 * s + 1].T.astype(jnp.bfloat16)
        out[2 * lanes :, :] = last[s * rest : (s + 1) * rest]


def text_last_kernel(g0, g1, g2, g3, out):
    value = total([wide(g, slice(None)) for g in (g0, g1, g2, g3)])
    out[...] = value.astype(jnp.bfloat16)


def image_last_kernel(arrived, out, sums_out):
    values = [wide(arrived, d) for d in range(arrived.shape[0])]
    heads = len(values) // strips
    found = []
    for k in range(strips):
        chunk = total([values[h * strips + k][carry_rows:] for h in range(heads)])
        last = chunk[2 * piece :]
        groups = [last] + [pltpu.roll(last, lanes - rest * g, 1) for g in range(1, 4)]
        last = jnp.concatenate(groups, axis=0)
        found.append((chunk[:piece], chunk[piece : 2 * piece], last))
    for t in range(3):
        rows = jnp.concatenate([f[t] for f in found], axis=0).T
        count = lanes if t < 2 else rest
        out[t * lanes : t * lanes + count, :] = rows[:count].astype(jnp.bfloat16)
    sums = total([v[:8] for v in values])
    sums_out[...] = jnp.broadcast_to(jnp.sum(sums, axis=1, keepdims=True), sums.shape)


def swap_core(value):
    return lax.ppermute(value, "core", [(0, 1), (1, 0)])


def shift(value, axis, k):
    count = lax.axis_size(axis)
    return lax.ppermute(value, axis, [(i, (i + k) % count) for i in range(count)])


def shards(image, text, log_temp, bias):
    rows, strip = image.shape
    x_count, y_count, zh_count = (lax.axis_size(name) for name in ("x", "y", "zh"))
    z_count = zh_count * strips
    width = strip * strips
    block = zh_count * piece
    count = x_count * block
    zh, x, zl = (lax.axis_index(name).astype(jnp.int32) for name in ("zh", "x", "zl"))
    scale = jnp.exp(log_temp)
    scales = jnp.stack([scale, bias])
    place = zl.reshape(1)
    spot = jnp.stack([x * block + zh * piece, zl * piece])
    f32 = jnp.float32

    (packed,) = call(pack_kernel, [shape((z_count, chunk_rows, lanes))], "pack", [image.T])
    parts = [text.T] + [shift(text.T, "zl", k) for k in range(1, strips)]
    arrived = lax.all_to_all(packed, ("zh", "zl"), 0, 0)
    (home_text,) = call(text_unit_kernel, [shape((block, width))], "text_unit", parts)
    texts = [shift(home_text, "y", k) for k in range(1, y_count)]
    (units,) = call(
        image_unit_kernel,
        [shape((x_count, block, width))],
        "image_unit",
        [arrived],
        scalars=[place],
        after=[home_text],
    )
    image_rows = lax.all_to_all(units, "x", 0, 0).reshape(count, width)
    other_rows = swap_core(image_rows)

    columns = y_count * block
    area = count * columns
    home_weights, home_sums, home_text = call(
        home_kernel,
        [shape((count, block)), shape((24, lanes), f32), shape((block, width))],
        "home",
        [image_rows, home_text],
        scalars=[scales, spot],
        flops=200 * count * block * width,
    )
    own_back, own_weights, right, own_sums = call(
        own_kernel,
        [
            shape((count, width)),
            shape((count, columns)),
            shape((columns, width)),
            shape((24, lanes), f32),
        ],
        "own",
        [image_rows, home_text] + texts + [home_weights, home_sums],
        scalars=[scales],
        flops=4 * area * width,
        special=2 * area,
    )
    other_back, sums, *text_backs = call(
        other_kernel,
        [shape((count, width)), shape((y_count * 2, 8, lanes), f32)]
        + [shape((block, width))] * y_count,
        "other",
        [other_rows, right, own_sums, own_weights, image_rows],
        scalars=[scales],
        flops=8 * area * width,
        special=2 * area,
        scratch=[pltpu.VMEM((count, columns), jnp.bfloat16)],
    )
    given_back = swap_core(other_back)
    sums = lax.all_to_all(sums, ("y", "core"), 0, 0)
    (combined,) = call(
        combine_kernel,
        [shape((x_count, tiles * block + carry_rows, lanes))],
        "combine",
        [own_back, given_back, sums],
    )
    combined = lax.all_to_all(combined, "x", 0, 0)
    (finished,) = call(
        image_finish_kernel,
        [shape((z_count, sent_rows, lanes))],
        "image_finish",
        [arrived, combined],
        scalars=[place],
        flops=200 * count * block * width,
    )
    moved = [text_backs[0]] + [shift(text_backs[k], "y", -k) for k in range(1, y_count)]
    finished = hold(finished, moved[1:3])
    finished = lax.all_to_all(finished, ("zh", "zl"), 0, 0)
    text_parts = call(
        text_finish_kernel, [shape((strip, rows))] * strips, "text_finish", parts + moved
    )
    given = [text_parts[0]] + [shift(text_parts[k], "zl", -k) for k in range(1, strips)]
    (grad_text,) = call(text_last_kernel, [shape((strip, rows))], "text_last", given)
    grad_image, sums = call(
        image_last_kernel, [shape((strip, rows)), shape((8, lanes), f32)], "image_last", [finished]
    )
    pairs_count = rows * 4 * x_count * y_count * 2
    return (
        sums[0, 0] / pairs_count,
        grad_image.T,
        grad_text.T,
        scale * sums[1, 0] / pairs_count,
        sums[2, 0] / pairs_count,
    )


def solution(mesh):
    fine = Mesh(mesh.devices.reshape(4, 4, 4, 2, 4), ("zh", "x", "y", "core", "zl"))
    whole = P(("zh", "x", "y", "core"), "zl")
    return jax.shard_map(
        shards,
        mesh=fine,
        in_specs=(whole, whole, P(), P()),
        out_specs=(P(), whole, whole, P(), P()),
        check_vma=False,
    )
```

```python
import functools

import jax
import jax.numpy as jnp
from jax import lax
from jax.experimental import pallas as pl
from jax.experimental.pallas import tpu as pltpu
from jax.sharding import Mesh, PartitionSpec as P

epsilon = 1e-06
lanes = 128
piece = 32
strips = 4
rest = 32
chunk_rows = 72
carry_rows = 16
sent_rows = 80
tiles = 9
vmem = pl.BlockSpec(memory_space=pltpu.VMEM)
smem = pl.BlockSpec(memory_space=pltpu.SMEM)
anywhere = pl.BlockSpec(memory_space=pl.ANY)
limits = pltpu.CompilerParams(vmem_limit_bytes=16 * 1024 * 1024)


def shape(dims, dtype=jnp.bfloat16):
    return jax.ShapeDtypeStruct(tuple(dims), dtype)


def call(kernel, out_shape, name, operands, scalars=(), after=(), flops=0, special=0, scratch=()):
    out_shape = tuple(out_shape)
    scalars, operands, after = tuple(scalars), tuple(operands), tuple(after)
    inputs = len(scalars) + len(operands)
    moved = sum(a.size * a.dtype.itemsize for a in operands + out_shape)

    def body(*refs):
        kernel(*refs[:inputs], *refs[inputs + len(after) :])

    return pl.pallas_call(
        body,
        out_shape=out_shape,
        in_specs=[smem] * len(scalars) + [vmem] * len(operands) + [anywhere] * len(after),
        out_specs=(vmem,) * len(out_shape),
        scratch_shapes=list(scratch),
        compiler_params=limits,
        cost_estimate=pl.CostEstimate(flops=flops, bytes_accessed=moved, transcendentals=special),
        name=name,
    )(*scalars, *operands, *after)


def hold(value, after):
    def body(*refs):
        del refs

    return pl.pallas_call(
        body,
        out_shape=shape(value.shape, value.dtype),
        in_specs=[anywhere] * (1 + len(after)),
        out_specs=anywhere,
        input_output_aliases={0: 0},
        compiler_params=limits,
        name="hold",
    )(value, *after)


def total(values):
    return functools.reduce(lambda a, b: a + b, values)


def wide(ref, *index):
    return ref[index].astype(jnp.float32)


def lane_group():
    return lax.broadcasted_iota(jnp.int32, (8, lanes), 1) // rest


def pack_kernel(image, out):
    whole = wide(image, slice(None)).T
    for k in range(4):
        rows = whole[k * piece : (k + 1) * piece]
        last = rows[:, 2 * lanes :]
        last = jnp.concatenate([last[8 * g : 8 * g + 8] for g in range(4)], axis=1)
        chunk = jnp.concatenate([rows[:, :lanes], rows[:, lanes : 2 * lanes], last], axis=0)
        chunk = chunk.astype(jnp.bfloat16)
        for h in range(out.shape[0] // strips):
            out[h * strips + k] = chunk


def unpack_rows(chunks, group):
    found = []
    lasts = []
    for chunk in chunks:
        found += [chunk[:piece], chunk[piece : 2 * piece]]
        lasts.append(chunk[2 * piece :])
    last = []
    for g in range(4):
        value = jnp.zeros((8, lanes), jnp.float32)
        for s in range(strips):
            turn = rest * (s - g) % lanes
            moved = pltpu.roll(lasts[s], turn, 1) if turn else lasts[s]
            value = jnp.where(group == s, moved, value)
        last.append(value)
    found.append(jnp.concatenate(last, axis=0))
    return found


def units_of(found):
    inverse = lax.rsqrt(jnp.sum(total([t * t for t in found]), axis=1, keepdims=True) + epsilon)
    return [t * inverse for t in found], inverse


def strip_at(place, k):
    return lax.rem(place[0] + (strips - k), strips)


def image_units(place, arrived, h, group):
    chunks = [wide(arrived, h * strips + strip_at(place, k)) for k in range(strips)]
    return units_of(unpack_rows(chunks, group))


def image_unit_kernel(place, arrived, out):
    group = lane_group()
    for h in range(arrived.shape[0] // strips):
        units, _ = image_units(place, arrived, h, group)
        for t in range(tiles):
            value = units[t].astype(jnp.bfloat16)
            for k in range(out.shape[0]):
                out[k, h * piece : (h + 1) * piece, t * lanes : (t + 1) * lanes] = value


def text_units(parts):
    rows = [wide(p, slice(None)).T for p in parts]
    found = []
    for r in rows:
        found += [r[:, :lanes], r[:, lanes : 2 * lanes]]
    found.append(jnp.concatenate([r[:, 2 * lanes :] for r in rows], axis=1))
    return units_of(found)


def text_unit_kernel(p0, p1, p2, p3, out):
    units, _ = text_units((p0, p1, p2, p3))
    for t in range(tiles):
        out[:, t * lanes : (t + 1) * lanes] = units[t].astype(jnp.bfloat16)


def fold(values):
    rows, columns = values.shape
    part = jnp.sum(values.reshape(rows // 8, 8, columns), axis=0)
    return total([part[:, c : c + lanes] for c in range(0, columns, lanes)])


def pair_terms(left, right, scale, bias, same=None):
    product = lax.dot_general(
        left, right, (((1,), (1,)), ((), ())), preferred_element_type=jnp.float32
    )
    logits = scale * product + bias
    if same is None:
        grown = jnp.exp(logits)
        slope = grown / (1.0 + grown)
    else:
        grown = jnp.exp(jnp.where(same, -logits, logits))
        share = grown / (1.0 + grown)
        slope = jnp.where(same, -share, share)
    quarter = left.shape[0] // 4
    a, b, c, d = (grown[k * quarter : (k + 1) * quarter, :] for k in range(4))
    ab = a + (b + a * b)
    cd = c + (d + c * d)
    sums = (fold(jnp.log1p(ab + (cd + ab * cd))), fold(slope * product), fold(slope))
    return (scale * slope).astype(jnp.bfloat16), sums


def write_sums(out, sums, before=None):
    for k in range(3):
        value = total([found[k] for found in sums])
        if before is not None:
            value = value + before[8 * k : 8 * k + 8, :]
        out[8 * k : 8 * k + 8, :] = value


tile = 256


def home_kernel(scales, spot, left, right, weights, sums_out, kept):
    kept[...] = right[...]
    rows, columns = left.shape[0], right.shape[0]
    sums = []
    for start in range(0, rows, tile):
        here = pl.ds(start, tile)
        row = lax.broadcasted_iota(jnp.int32, (tile, 1), 0) + (start - spot[0])
        row = jnp.where((row >= 0) & (row < piece), row, -1)
        column = lax.broadcasted_iota(jnp.int32, (1, columns), 1) - spot[1]
        same = row == jnp.where(column >= 0, column, -2)
        weights[here, :], found = pair_terms(
            left[here, :], right[...], scales[0], scales[1], same
        )
        sums.append(found)
    write_sums(sums_out, sums)


def own_kernel(scales, left, t0, t1, t2, t3, home, home_sums, back, weights, right, sums_out):
    rows, part = left.shape[0], t0.shape[0]
    for k, ref in enumerate((t0, t1, t2, t3)):
        right[k * part : (k + 1) * part, :] = ref[...]
    sums = []
    for start in range(0, rows, tile):
        here = pl.ds(start, tile)
        value, found = pair_terms(left[here, :], right[part:, :], scales[0], scales[1])
        weights[here, :part] = home[here, :]
        weights[here, part:] = value
        back[here, :] = jnp.dot(
            weights[here, :], right[...], preferred_element_type=jnp.float32
        ).astype(jnp.bfloat16)
        sums.append(found)
    write_sums(sums_out, sums, home_sums)


def other_kernel(scales, left, right, own_sums, back, weights, sums_out):
    sums = []
    for start in range(0, left.shape[0], tile):
        here = pl.ds(start, tile)
        value, found = pair_terms(left[here, :], right[...], scales[0], scales[1])
        weights[here, :] = value
        back[here, :] = jnp.dot(
            value, right[...], preferred_element_type=jnp.float32
        ).astype(jnp.bfloat16)
        sums.append(found)
    row = lax.broadcasted_iota(jnp.int32, (8, lanes), 0)
    value = jnp.zeros((8, lanes), jnp.float32)
    for k in range(3):
        found = total([s[k] for s in sums]) + own_sums[8 * k : 8 * k + 8, :]
        value = jnp.where(row == k, jnp.sum(found, axis=0, keepdims=True), value)
    carry = carry_of(value)
    sums_out[...] = carry
    rows = left.shape[0]
    back[rows:, :lanes] = carry.astype(jnp.bfloat16)
    back[rows:, lanes:] = jnp.zeros((carry_rows, back.shape[1] - lanes), jnp.bfloat16)


def text_kernel(own_weights, other_weights, own_left, other_left, *backs):
    contract = (((0,), (0,)), ((), ()))
    part = backs[0].shape[0]
    value = lax.dot_general(
        own_weights[...], own_left[...], contract, preferred_element_type=jnp.float32
    ) + lax.dot_general(
        other_weights[...], other_left[...], contract, preferred_element_type=jnp.float32
    )
    for k, out in enumerate(backs):
        out[...] = value[k * part : (k + 1) * part].astype(jnp.bfloat16)


def three_parts(value):
    high = value.astype(jnp.bfloat16).astype(jnp.float32)
    middle = (value - high).astype(jnp.bfloat16).astype(jnp.float32)
    return high, middle, value - high - middle


def carry_of(value):
    parts = three_parts(jnp.sum(value, axis=1, keepdims=True))
    lane = lax.broadcasted_iota(jnp.int32, (8, lanes), 1)
    carry = jnp.zeros((8, lanes), jnp.float32)
    for k in range(3):
        carry = jnp.where(lane == k, parts[k], carry)
    return jnp.concatenate([carry, jnp.zeros((8, lanes), jnp.float32)], axis=0)


def combine_kernel(own, given, sums, out):
    count, all_rows, _ = out.shape
    block = own.shape[0] // count
    carry = sums[...] + wide(given, pl.ds(own.shape[0], carry_rows), pl.ds(0, lanes))
    carry = carry_of(carry[:8]).astype(jnp.bfloat16)
    for k in range(count):
        rows = pl.ds(k * block, block)
        for t in range(tiles):
            columns = pl.ds(t * lanes, lanes)
            value = wide(own, rows, columns) + wide(given, rows, columns)
            out[k, t * block : (t + 1) * block, :] = value.astype(jnp.bfloat16)
        out[k, tiles * block : all_rows, :] = carry


def grads_of(units, inverse, grads):
    along = jnp.sum(total([u * g for u, g in zip(units, grads)]), axis=1, keepdims=True)
    return [(g - u * along) * inverse for u, g in zip(units, grads)]


def image_finish_kernel(place, arrived, backs, out):
    group = lane_group()
    count = backs.shape[0]
    heads = arrived.shape[0] // strips
    block = heads * piece
    tail = pl.ds(tiles * block, carry_rows)
    carry = carry_of(total([wide(backs, k, tail, slice(None)) for k in range(count)])[:8])[:8]
    for h in range(heads):
        units, inverse = image_units(place, arrived, h, group)
        grads = []
        for t in range(tiles):
            rows = pl.ds(t * block + h * piece, piece)
            grads.append(total([wide(backs, k, rows, slice(None)) for k in range(count)]))
        final = grads_of(units, inverse, grads)
        for s in range(strips):
            last = jnp.zeros((8, lanes), jnp.float32)
            for g in range(4):
                turn = rest * (g - s) % lanes
                rows = final[tiles - 1][8 * g : 8 * g + 8]
                moved = pltpu.roll(rows, turn, 1) if turn else rows
                last = jnp.where(group == g, moved, last)
            chunk = jnp.concatenate([carry, final[2 * s], final[2 * s + 1], last], axis=0)
            out[h * strips + strip_at(place, s)] = chunk.astype(jnp.bfloat16)


def text_finish_kernel(p0, p1, p2, p3, b0, b1, b2, b3, *outs):
    units, inverse = text_units((p0, p1, p2, p3))
    grads = []
    for t in range(tiles):
        columns = pl.ds(t * lanes, lanes)
        grads.append(total([wide(b, slice(None), columns) for b in (b0, b1, b2, b3)]))
    final = grads_of(units, inverse, grads)
    last = final[tiles - 1].T.astype(jnp.bfloat16)
    for s, out in enumerate(outs):
        out[:lanes, :] = final[2 * s].T.astype(jnp.bfloat16)
        out[lanes : 2 * lanes, :] = final[2 * s + 1].T.astype(jnp.bfloat16)
        out[2 * lanes :, :] = last[s * rest : (s + 1) * rest]


def text_last_kernel(g0, g1, g2, g3, out):
    value = total([wide(g, slice(None)) for g in (g0, g1, g2, g3)])
    out[...] = value.astype(jnp.bfloat16)


def image_last_kernel(arrived, out, sums_out):
    values = [wide(arrived, d) for d in range(arrived.shape[0])]
    heads = len(values) // strips
    found = []
    for k in range(strips):
        chunk = total([values[h * strips + k][8:] for h in range(heads)])
        last = chunk[2 * piece :]
        groups = [last] + [pltpu.roll(last, lanes - rest * g, 1) for g in range(1, 4)]
        last = jnp.concatenate(groups, axis=0)
        found.append((chunk[:piece], chunk[piece : 2 * piece], last))
    for t in range(3):
        rows = jnp.concatenate([f[t] for f in found], axis=0).T
        count = lanes if t < 2 else rest
        out[t * lanes : t * lanes + count, :] = rows[:count].astype(jnp.bfloat16)
    sums = jnp.sum(total([v[:8] for v in values]), axis=1, keepdims=True)
    for k in range(sums_out.shape[0]):
        sums_out[k] = jnp.broadcast_to(sums, sums_out.shape[1:])


def swap_core(value):
    return lax.ppermute(value, "core", [(0, 1), (1, 0)])


def shift(value, axis, k):
    count = lax.axis_size(axis)
    return lax.ppermute(value, axis, [(i, (i + k) % count) for i in range(count)])


def shards(image, text, log_temp, bias):
    rows, strip = image.shape
    x_count, y_count, zh_count = (lax.axis_size(name) for name in ("x", "y", "zh"))
    z_count = zh_count * strips
    width = strip * strips
    block = zh_count * piece
    count = x_count * block
    zh, x, zl = (lax.axis_index(name).astype(jnp.int32) for name in ("zh", "x", "zl"))
    scale = jnp.exp(log_temp)
    scales = jnp.stack([scale, bias])
    place = zl.reshape(1)
    spot = jnp.stack([x * block + zh * piece, zl * piece])
    f32 = jnp.float32

    (packed,) = call(pack_kernel, [shape((z_count, chunk_rows, lanes))], "pack", [image.T])
    parts = [text.T] + [shift(text.T, "zl", k) for k in range(1, strips)]
    arrived = lax.all_to_all(packed, ("zh", "zl"), 0, 0)
    (home_text,) = call(text_unit_kernel, [shape((block, width))], "text_unit", parts)
    texts = [shift(home_text, "y", k) for k in range(1, y_count)]
    (units,) = call(
        image_unit_kernel,
        [shape((x_count, block, width))],
        "image_unit",
        [arrived],
        scalars=[place],
        after=parts[1:] + [scales, spot],
    )
    image_rows = lax.all_to_all(units, "x", 0, 0).reshape(count, width)
    other_rows = swap_core(image_rows)

    columns = y_count * block
    area = count * columns
    home_weights, home_sums, home_text = call(
        home_kernel,
        [shape((count, block)), shape((24, lanes), f32), shape((block, width))],
        "home",
        [image_rows, home_text],
        scalars=[scales, spot],
        flops=200 * count * block * width,
    )
    own_back, own_weights, right, own_sums = call(
        own_kernel,
        [
            shape((count, width)),
            shape((count, columns)),
            shape((columns, width)),
            shape((24, lanes), f32),
        ],
        "own",
        [image_rows, home_text] + texts + [home_weights, home_sums],
        scalars=[scales],
        flops=4 * area * width,
        special=2 * area,
    )
    other_back, other_weights, sums = call(
        other_kernel,
        [
            shape((count + carry_rows, width)),
            shape((count, columns)),
            shape((carry_rows, lanes), f32),
        ],
        "other",
        [other_rows, right, own_sums],
        scalars=[scales],
        flops=4 * area * width,
        special=2 * area,
    )
    given_back = swap_core(other_back)
    text_backs = call(
        text_kernel,
        [shape((block, width))] * y_count,
        "text_back",
        [own_weights, other_weights, image_rows, other_rows],
        flops=4 * area * width,
    )
    (combined,) = call(
        combine_kernel,
        [shape((x_count, tiles * block + carry_rows, lanes))],
        "combine",
        [own_back, given_back, sums],
        after=text_backs[:1],
    )
    combined = lax.all_to_all(combined, "x", 0, 0)
    (finished,) = call(
        image_finish_kernel,
        [shape((z_count, sent_rows, lanes))],
        "image_finish",
        [arrived, combined],
        scalars=[place],
        flops=200 * count * block * width,
    )
    moved = [text_backs[0]] + [shift(text_backs[k], "y", -k) for k in range(1, y_count)]
    finished = hold(finished, moved[1:3])
    finished = lax.all_to_all(finished, ("zh", "zl"), 0, 0)
    text_parts = call(
        text_finish_kernel, [shape((strip, rows))] * strips, "text_finish", parts + moved, flops=200 * count * block * width
    )
    given = [text_parts[0]] + [shift(text_parts[k], "zl", -k) for k in range(1, strips)]
    (grad_text,) = call(text_last_kernel, [shape((strip, rows))], "text_last", given)
    grad_image, sums = call(
        image_last_kernel,
        [shape((strip, rows)), shape((y_count, 8, lanes), f32)],
        "image_last",
        [finished],
    )
    sums = jnp.sum(lax.all_to_all(sums, "y", 0, 0), axis=0)
    pairs_count = rows * 4 * x_count * y_count * 2
    return (
        sums[0, 0] / pairs_count,
        grad_image.T,
        grad_text.T,
        scale * sums[1, 0] / pairs_count,
        sums[2, 0] / pairs_count,
    )


def solution(mesh):
    fine = Mesh(mesh.devices.reshape(4, 4, 4, 2, 4), ("zh", "x", "y", "core", "zl"))
    whole = P(("zh", "x", "y", "core"), "zl")
    return jax.shard_map(
        shards,
        mesh=fine,
        in_specs=(whole, whole, P(), P()),
        out_specs=(P(), whole, whole, P(), P()),
        check_vma=False,
    )
```

```python
import functools

import jax
import jax.numpy as jnp
from jax import lax
from jax.experimental import pallas as pl
from jax.experimental.pallas import tpu as pltpu
from jax.sharding import Mesh, PartitionSpec as P

epsilon = 1e-06
lanes = 128
piece = 32
strips = 4
rest = 32
chunk_rows = 72
carry_rows = 16
sent_rows = 80
tiles = 9
vmem = pl.BlockSpec(memory_space=pltpu.VMEM)
smem = pl.BlockSpec(memory_space=pltpu.SMEM)
anywhere = pl.BlockSpec(memory_space=pl.ANY)
limits = pltpu.CompilerParams(vmem_limit_bytes=16 * 1024 * 1024)


def shape(dims, dtype=jnp.bfloat16):
    return jax.ShapeDtypeStruct(tuple(dims), dtype)


def call(kernel, out_shape, name, operands, scalars=(), after=(), flops=0, special=0, scratch=()):
    out_shape = tuple(out_shape)
    scalars, operands, after = tuple(scalars), tuple(operands), tuple(after)
    inputs = len(scalars) + len(operands)
    moved = sum(a.size * a.dtype.itemsize for a in operands + out_shape)

    def body(*refs):
        kernel(*refs[:inputs], *refs[inputs + len(after) :])

    return pl.pallas_call(
        body,
        out_shape=out_shape,
        in_specs=[smem] * len(scalars) + [vmem] * len(operands) + [anywhere] * len(after),
        out_specs=(vmem,) * len(out_shape),
        scratch_shapes=list(scratch),
        compiler_params=limits,
        cost_estimate=pl.CostEstimate(flops=flops, bytes_accessed=moved, transcendentals=special),
        name=name,
    )(*scalars, *operands, *after)


def hold(value, after):
    def body(*refs):
        del refs

    return pl.pallas_call(
        body,
        out_shape=shape(value.shape, value.dtype),
        in_specs=[anywhere] * (1 + len(after)),
        out_specs=anywhere,
        input_output_aliases={0: 0},
        compiler_params=limits,
        name="hold",
    )(value, *after)


def total(values):
    return functools.reduce(lambda a, b: a + b, values)


def wide(ref, *index):
    return ref[index].astype(jnp.float32)


def lane_group():
    return lax.broadcasted_iota(jnp.int32, (8, lanes), 1) // rest


def pack_kernel(image, out):
    whole = wide(image, slice(None)).T
    for k in range(4):
        rows = whole[k * piece : (k + 1) * piece]
        last = rows[:, 2 * lanes :]
        last = jnp.concatenate([last[8 * g : 8 * g + 8] for g in range(4)], axis=1)
        chunk = jnp.concatenate([rows[:, :lanes], rows[:, lanes : 2 * lanes], last], axis=0)
        chunk = chunk.astype(jnp.bfloat16)
        for h in range(out.shape[0] // strips):
            out[h * strips + k] = chunk


def unpack_rows(chunks, group):
    found = []
    lasts = []
    for chunk in chunks:
        found += [chunk[:piece], chunk[piece : 2 * piece]]
        lasts.append(chunk[2 * piece :])
    last = []
    for g in range(4):
        value = jnp.zeros((8, lanes), jnp.float32)
        for s in range(strips):
            turn = rest * (s - g) % lanes
            moved = pltpu.roll(lasts[s], turn, 1) if turn else lasts[s]
            value = jnp.where(group == s, moved, value)
        last.append(value)
    found.append(jnp.concatenate(last, axis=0))
    return found


def units_of(found):
    inverse = lax.rsqrt(jnp.sum(total([t * t for t in found]), axis=1, keepdims=True) + epsilon)
    return [t * inverse for t in found], inverse


def strip_at(place, k):
    return lax.rem(place[0] + (strips - k), strips)


def image_units(place, arrived, h, group):
    chunks = [wide(arrived, h * strips + strip_at(place, k)) for k in range(strips)]
    return units_of(unpack_rows(chunks, group))


def image_unit_kernel(place, arrived, out):
    group = lane_group()
    for h in range(arrived.shape[0] // strips):
        units, _ = image_units(place, arrived, h, group)
        for t in range(tiles):
            value = units[t].astype(jnp.bfloat16)
            for k in range(out.shape[0]):
                out[k, h * piece : (h + 1) * piece, t * lanes : (t + 1) * lanes] = value


def text_units(parts):
    rows = [wide(p, slice(None)).T for p in parts]
    found = []
    for r in rows:
        found += [r[:, :lanes], r[:, lanes : 2 * lanes]]
    found.append(jnp.concatenate([r[:, 2 * lanes :] for r in rows], axis=1))
    return units_of(found)


def text_unit_kernel(p0, p1, p2, p3, out):
    units, _ = text_units((p0, p1, p2, p3))
    for t in range(tiles):
        out[:, t * lanes : (t + 1) * lanes] = units[t].astype(jnp.bfloat16)


def fold(values):
    rows, columns = values.shape
    part = jnp.sum(values.reshape(rows // 8, 8, columns), axis=0)
    return total([part[:, c : c + lanes] for c in range(0, columns, lanes)])


def pair_product(left, right):
    return lax.dot_general(
        left, right, (((1,), (1,)), ((), ())), preferred_element_type=jnp.float32
    )


def pair_terms(product, scale, bias, same=None):
    logits = scale * product + bias
    if same is None:
        grown = jnp.exp(logits)
        slope = grown / (1.0 + grown)
    else:
        grown = jnp.exp(jnp.where(same, -logits, logits))
        share = grown / (1.0 + grown)
        slope = jnp.where(same, -share, share)
    quarter = product.shape[0] // 4
    a, b, c, d = (grown[k * quarter : (k + 1) * quarter, :] for k in range(4))
    ab = a + (b + a * b)
    cd = c + (d + c * d)
    sums = (fold(jnp.log1p(ab + (cd + ab * cd))), fold(slope * product), fold(slope))
    return (scale * slope).astype(jnp.bfloat16), sums


def write_sums(out, sums, before=None):
    for k in range(3):
        value = total([found[k] for found in sums])
        if before is not None:
            value = value + before[8 * k : 8 * k + 8, :]
        out[8 * k : 8 * k + 8, :] = value


tile = 256


def home_kernel(scales, spot, left, right, weights, sums_out, kept):
    kept[...] = right[...]
    rows, columns = left.shape[0], right.shape[0]
    sums = []
    for start in range(0, rows, tile):
        here = pl.ds(start, tile)
        row = lax.broadcasted_iota(jnp.int32, (tile, 1), 0) + (start - spot[0])
        row = jnp.where((row >= 0) & (row < piece), row, -1)
        column = lax.broadcasted_iota(jnp.int32, (1, columns), 1) - spot[1]
        same = row == jnp.where(column >= 0, column, -2)
        product = pair_product(left[here, :], right[...])
        weights[here, :], found = pair_terms(product, scales[0], scales[1], same)
        sums.append(found)
    write_sums(sums_out, sums)


def own_kernel(scales, left, t0, t1, t2, t3, home, home_sums, back, weights, right, sums_out):
    rows, part = left.shape[0], t0.shape[0]
    for k, ref in enumerate((t0, t1, t2, t3)):
        right[k * part : (k + 1) * part, :] = ref[...]
    sums = []
    products = [pair_product(left[k : k + tile, :], right[part:, :]) for k in range(0, rows, tile)]
    for start in range(0, rows, tile):
        here = pl.ds(start, tile)
        value, found = pair_terms(products[start // tile], scales[0], scales[1])
        weights[here, :part] = home[here, :]
        weights[here, part:] = value
        back[here, :] = jnp.dot(
            weights[here, :], right[...], preferred_element_type=jnp.float32
        ).astype(jnp.bfloat16)
        sums.append(found)
    write_sums(sums_out, sums, home_sums)


def other_kernel(scales, left, right, own_sums, back, weights, sums_out):
    sums = []
    rows = left.shape[0]
    products = [pair_product(left[k : k + tile, :], right[...]) for k in range(0, rows, tile)]
    for start in range(0, rows, tile):
        here = pl.ds(start, tile)
        value, found = pair_terms(products[start // tile], scales[0], scales[1])
        weights[here, :] = value
        back[here, :] = jnp.dot(
            value, right[...], preferred_element_type=jnp.float32
        ).astype(jnp.bfloat16)
        sums.append(found)
    row = lax.broadcasted_iota(jnp.int32, (8, lanes), 0)
    value = jnp.zeros((8, lanes), jnp.float32)
    for k in range(3):
        found = total([s[k] for s in sums]) + own_sums[8 * k : 8 * k + 8, :]
        value = jnp.where(row == k, jnp.sum(found, axis=0, keepdims=True), value)
    carry = carry_of(value)
    sums_out[...] = carry
    back[rows:, :lanes] = carry.astype(jnp.bfloat16)
    back[rows:, lanes:] = jnp.zeros((carry_rows, back.shape[1] - lanes), jnp.bfloat16)


def text_kernel(own_weights, other_weights, own_left, other_left, *backs):
    contract = (((0,), (0,)), ((), ()))
    part = backs[0].shape[0]
    value = lax.dot_general(
        own_weights[...], own_left[...], contract, preferred_element_type=jnp.float32
    ) + lax.dot_general(
        other_weights[...], other_left[...], contract, preferred_element_type=jnp.float32
    )
    for k, out in enumerate(backs):
        out[...] = value[k * part : (k + 1) * part].astype(jnp.bfloat16)


def three_parts(value):
    high = value.astype(jnp.bfloat16).astype(jnp.float32)
    middle = (value - high).astype(jnp.bfloat16).astype(jnp.float32)
    return high, middle, value - high - middle


def carry_of(value):
    parts = three_parts(jnp.sum(value, axis=1, keepdims=True))
    lane = lax.broadcasted_iota(jnp.int32, (8, lanes), 1)
    carry = jnp.zeros((8, lanes), jnp.float32)
    for k in range(3):
        carry = jnp.where(lane == k, parts[k], carry)
    return jnp.concatenate([carry, jnp.zeros((8, lanes), jnp.float32)], axis=0)


def combine_kernel(own, given, sums, out):
    count, all_rows, _ = out.shape
    block = own.shape[0] // count
    carry = sums[...] + wide(given, pl.ds(own.shape[0], carry_rows), pl.ds(0, lanes))
    carry = carry_of(carry[:8]).astype(jnp.bfloat16)
    for k in range(count):
        rows = pl.ds(k * block, block)
        for t in range(tiles):
            columns = pl.ds(t * lanes, lanes)
            value = wide(own, rows, columns) + wide(given, rows, columns)
            out[k, t * block : (t + 1) * block, :] = value.astype(jnp.bfloat16)
        out[k, tiles * block : all_rows, :] = carry


def grads_of(units, inverse, grads):
    along = jnp.sum(total([u * g for u, g in zip(units, grads)]), axis=1, keepdims=True)
    return [(g - u * along) * inverse for u, g in zip(units, grads)]


def image_finish_kernel(place, arrived, backs, out):
    group = lane_group()
    count = backs.shape[0]
    heads = arrived.shape[0] // strips
    block = heads * piece
    tail = pl.ds(tiles * block, carry_rows)
    carry = carry_of(total([wide(backs, k, tail, slice(None)) for k in range(count)])[:8])[:8]
    for h in range(heads):
        units, inverse = image_units(place, arrived, h, group)
        grads = []
        for t in range(tiles):
            rows = pl.ds(t * block + h * piece, piece)
            grads.append(total([wide(backs, k, rows, slice(None)) for k in range(count)]))
        final = grads_of(units, inverse, grads)
        for s in range(strips):
            last = jnp.zeros((8, lanes), jnp.float32)
            for g in range(4):
                turn = rest * (g - s) % lanes
                rows = final[tiles - 1][8 * g : 8 * g + 8]
                moved = pltpu.roll(rows, turn, 1) if turn else rows
                last = jnp.where(group == g, moved, last)
            chunk = jnp.concatenate([carry, final[2 * s], final[2 * s + 1], last], axis=0)
            out[h * strips + strip_at(place, s)] = chunk.astype(jnp.bfloat16)


def text_finish_kernel(p0, p1, p2, p3, b0, b1, b2, b3, *outs):
    units, inverse = text_units((p0, p1, p2, p3))
    grads = []
    for t in range(tiles):
        columns = pl.ds(t * lanes, lanes)
        grads.append(total([wide(b, slice(None), columns) for b in (b0, b1, b2, b3)]))
    final = grads_of(units, inverse, grads)
    last = final[tiles - 1].T.astype(jnp.bfloat16)
    for s, out in enumerate(outs):
        out[:lanes, :] = final[2 * s].T.astype(jnp.bfloat16)
        out[lanes : 2 * lanes, :] = final[2 * s + 1].T.astype(jnp.bfloat16)
        out[2 * lanes :, :] = last[s * rest : (s + 1) * rest]


def text_last_kernel(g0, g1, g2, g3, out):
    value = total([wide(g, slice(None)) for g in (g0, g1, g2, g3)])
    out[...] = value.astype(jnp.bfloat16)


def image_last_kernel(arrived, out):
    values = [wide(arrived, d) for d in range(arrived.shape[0])]
    heads = len(values) // strips
    found = []
    for k in range(strips):
        chunk = total([values[h * strips + k][8:] for h in range(heads)])
        last = chunk[2 * piece :]
        groups = [last] + [pltpu.roll(last, lanes - rest * g, 1) for g in range(1, 4)]
        last = jnp.concatenate(groups, axis=0)
        found.append((chunk[:piece], chunk[piece : 2 * piece], last))
    for t in range(3):
        rows = jnp.concatenate([f[t] for f in found], axis=0).T
        count = lanes if t < 2 else rest
        out[t * lanes : t * lanes + count, :] = rows[:count].astype(jnp.bfloat16)


def sums_kernel(arrived, out):
    value = total([arrived[d].astype(jnp.float32)[:8] for d in range(arrived.shape[0])])
    value = jnp.sum(value, axis=1, keepdims=True)
    for k in range(out.shape[0]):
        out[k] = jnp.broadcast_to(value, out.shape[1:])


def swap_core(value):
    return lax.ppermute(value, "core", [(0, 1), (1, 0)])


def shift(value, axis, k):
    count = lax.axis_size(axis)
    return lax.ppermute(value, axis, [(i, (i + k) % count) for i in range(count)])


def shards(image, text, log_temp, bias):
    rows, strip = image.shape
    x_count, y_count, zh_count = (lax.axis_size(name) for name in ("x", "y", "zh"))
    z_count = zh_count * strips
    width = strip * strips
    block = zh_count * piece
    count = x_count * block
    zh, x, zl = (lax.axis_index(name).astype(jnp.int32) for name in ("zh", "x", "zl"))
    scale = jnp.exp(log_temp)
    scales = jnp.stack([scale, bias])
    place = zl.reshape(1)
    spot = jnp.stack([x * block + zh * piece, zl * piece])
    f32 = jnp.float32

    (packed,) = call(pack_kernel, [shape((z_count, chunk_rows, lanes))], "pack", [image.T])
    parts = [text.T] + [shift(text.T, "zl", k) for k in range(1, strips)]
    arrived = lax.all_to_all(packed, ("zh", "zl"), 0, 0)
    (home_text,) = call(text_unit_kernel, [shape((block, width))], "text_unit", parts, flops=400 * count * block * width)
    texts = [shift(home_text, "y", k) for k in range(1, y_count)]
    (units,) = call(
        image_unit_kernel,
        [shape((x_count, block, width))],
        "image_unit",
        [arrived],
        scalars=[place],
        after=[scales, spot],
    )
    image_rows = lax.all_to_all(units, "x", 0, 0).reshape(count, width)
    other_rows = swap_core(image_rows)

    columns = y_count * block
    area = count * columns
    home_weights, home_sums, home_text = call(
        home_kernel,
        [shape((count, block)), shape((24, lanes), f32), shape((block, width))],
        "home",
        [image_rows, home_text],
        scalars=[scales, spot],
        flops=200 * count * block * width,
    )
    own_back, own_weights, right, own_sums = call(
        own_kernel,
        [
            shape((count, width)),
            shape((count, columns)),
            shape((columns, width)),
            shape((24, lanes), f32),
        ],
        "own",
        [image_rows, home_text] + texts + [home_weights, home_sums],
        scalars=[scales],
        flops=4 * area * width,
        special=2 * area,
    )
    other_back, other_weights, sums = call(
        other_kernel,
        [
            shape((count + carry_rows, width)),
            shape((count, columns)),
            shape((carry_rows, lanes), f32),
        ],
        "other",
        [other_rows, right, own_sums],
        scalars=[scales],
        flops=4 * area * width,
        special=2 * area,
    )
    given_back = swap_core(other_back)
    text_backs = call(
        text_kernel,
        [shape((block, width))] * y_count,
        "text_back",
        [own_weights, other_weights, image_rows, other_rows],
        flops=4 * area * width,
    )
    (combined,) = call(
        combine_kernel,
        [shape((x_count, tiles * block + carry_rows, lanes))],
        "combine",
        [own_back, given_back, sums],
        after=text_backs[:1],
    )
    combined = lax.all_to_all(combined, "x", 0, 0)
    (finished,) = call(
        image_finish_kernel,
        [shape((z_count, sent_rows, lanes))],
        "image_finish",
        [arrived, combined],
        scalars=[place],
        flops=200 * count * block * width,
    )
    moved = [text_backs[0]] + [shift(text_backs[k], "y", -k) for k in range(1, y_count)]
    finished = lax.all_to_all(finished, ("zh", "zl"), 0, 0)
    text_parts = call(
        text_finish_kernel, [shape((strip, rows))] * strips, "text_finish", parts + moved, flops=200 * count * block * width
    )
    given = [text_parts[0]] + [shift(text_parts[k], "zl", -k) for k in range(1, strips)]
    (grad_text,) = call(text_last_kernel, [shape((strip, rows))], "text_last", given)
    (sums,) = call(sums_kernel, [shape((y_count, 8, lanes), f32)], "sums", [finished])
    (grad_image,) = call(image_last_kernel, [shape((strip, rows))], "image_last", [finished], after=[sums])
    sums = jnp.sum(lax.all_to_all(sums, "y", 0, 0), axis=0)
    pairs_count = rows * 4 * x_count * y_count * 2
    return (
        sums[0, 0] / pairs_count,
        grad_image.T,
        grad_text.T,
        scale * sums[1, 0] / pairs_count,
        sums[2, 0] / pairs_count,
    )


def solution(mesh):
    fine = Mesh(mesh.devices.reshape(4, 4, 4, 2, 4), ("zh", "x", "y", "core", "zl"))
    whole = P(("zh", "x", "y", "core"), "zl")
    return jax.shard_map(
        shards,
        mesh=fine,
        in_specs=(whole, whole, P(), P()),
        out_specs=(P(), whole, whole, P(), P()),
        check_vma=False,
    )
```

```python
import functools

import jax
import jax.numpy as jnp
from jax import lax
from jax.experimental import pallas as pl
from jax.experimental.pallas import tpu as pltpu
from jax.sharding import Mesh, PartitionSpec as P

epsilon = 1e-06
lanes = 128
piece = 32
strips = 4
rest = 32
chunk_rows = 72
carry_rows = 16
sent_rows = 80
tiles = 9
vmem = pl.BlockSpec(memory_space=pltpu.VMEM)
smem = pl.BlockSpec(memory_space=pltpu.SMEM)
anywhere = pl.BlockSpec(memory_space=pl.ANY)
limits = pltpu.CompilerParams(vmem_limit_bytes=16 * 1024 * 1024)


def shape(dims, dtype=jnp.bfloat16):
    return jax.ShapeDtypeStruct(tuple(dims), dtype)


def call(kernel, out_shape, name, operands, scalars=(), after=(), flops=0, special=0, scratch=()):
    out_shape = tuple(out_shape)
    scalars, operands, after = tuple(scalars), tuple(operands), tuple(after)
    inputs = len(scalars) + len(operands)
    moved = sum(a.size * a.dtype.itemsize for a in operands + out_shape)

    def body(*refs):
        kernel(*refs[:inputs], *refs[inputs + len(after) :])

    return pl.pallas_call(
        body,
        out_shape=out_shape,
        in_specs=[smem] * len(scalars) + [vmem] * len(operands) + [anywhere] * len(after),
        out_specs=(vmem,) * len(out_shape),
        scratch_shapes=list(scratch),
        compiler_params=limits,
        cost_estimate=pl.CostEstimate(flops=flops, bytes_accessed=moved, transcendentals=special),
        name=name,
    )(*scalars, *operands, *after)


def hold(value, after):
    def body(*refs):
        del refs

    return pl.pallas_call(
        body,
        out_shape=shape(value.shape, value.dtype),
        in_specs=[anywhere] * (1 + len(after)),
        out_specs=anywhere,
        input_output_aliases={0: 0},
        compiler_params=limits,
        name="hold",
    )(value, *after)


def total(values):
    return functools.reduce(lambda a, b: a + b, values)


def wide(ref, *index):
    return ref[index].astype(jnp.float32)


def lane_group():
    return lax.broadcasted_iota(jnp.int32, (8, lanes), 1) // rest


def pack_kernel(image, out):
    whole = wide(image, slice(None)).T
    for k in range(4):
        rows = whole[k * piece : (k + 1) * piece]
        last = rows[:, 2 * lanes :]
        last = jnp.concatenate([last[8 * g : 8 * g + 8] for g in range(4)], axis=1)
        chunk = jnp.concatenate([rows[:, :lanes], rows[:, lanes : 2 * lanes], last], axis=0)
        chunk = chunk.astype(jnp.bfloat16)
        for h in range(out.shape[0] // strips):
            out[h * strips + k] = chunk


def unpack_rows(chunks, group):
    found = []
    lasts = []
    for chunk in chunks:
        found += [chunk[:piece], chunk[piece : 2 * piece]]
        lasts.append(chunk[2 * piece :])
    last = []
    for g in range(4):
        value = jnp.zeros((8, lanes), jnp.float32)
        for s in range(strips):
            turn = rest * (s - g) % lanes
            moved = pltpu.roll(lasts[s], turn, 1) if turn else lasts[s]
            value = jnp.where(group == s, moved, value)
        last.append(value)
    found.append(jnp.concatenate(last, axis=0))
    return found


def units_of(found):
    inverse = lax.rsqrt(jnp.sum(total([t * t for t in found]), axis=1, keepdims=True) + epsilon)
    return [t * inverse for t in found], inverse


def strip_at(place, k):
    return lax.rem(place[0] + (strips - k), strips)


def image_units(place, arrived, h, group):
    chunks = [wide(arrived, h * strips + strip_at(place, k)) for k in range(strips)]
    return units_of(unpack_rows(chunks, group))


def image_unit_kernel(place, arrived, out):
    group = lane_group()
    for h in range(arrived.shape[0] // strips):
        units, _ = image_units(place, arrived, h, group)
        for t in range(tiles):
            value = units[t].astype(jnp.bfloat16)
            for k in range(out.shape[0]):
                out[k, h * piece : (h + 1) * piece, t * lanes : (t + 1) * lanes] = value


def text_units(parts):
    rows = [wide(p, slice(None)).T for p in parts]
    found = []
    for r in rows:
        found += [r[:, :lanes], r[:, lanes : 2 * lanes]]
    found.append(jnp.concatenate([r[:, 2 * lanes :] for r in rows], axis=1))
    return units_of(found)


def keep_kernel(strip, out):
    out[...] = strip[...]


def text_unit_kernel(p0, p1, p2, p3, out):
    units, _ = text_units((p0, p1, p2, p3))
    for t in range(tiles):
        out[:, t * lanes : (t + 1) * lanes] = units[t].astype(jnp.bfloat16)


def fold(values):
    rows, columns = values.shape
    part = jnp.sum(values.reshape(rows // 8, 8, columns), axis=0)
    return total([part[:, c : c + lanes] for c in range(0, columns, lanes)])


def pair_product(left, right):
    return lax.dot_general(
        left, right, (((1,), (1,)), ((), ())), preferred_element_type=jnp.float32
    )


def pair_terms(product, scale, bias, same=None):
    logits = scale * product + bias
    if same is None:
        grown = jnp.exp(logits)
        slope = grown / (1.0 + grown)
    else:
        grown = jnp.exp(jnp.where(same, -logits, logits))
        share = grown / (1.0 + grown)
        slope = jnp.where(same, -share, share)
    quarter = product.shape[0] // 4
    a, b, c, d = (grown[k * quarter : (k + 1) * quarter, :] for k in range(4))
    ab = a + (b + a * b)
    cd = c + (d + c * d)
    sums = (fold(jnp.log1p(ab + (cd + ab * cd))), fold(slope * product), fold(slope))
    return (scale * slope).astype(jnp.bfloat16), sums


def write_sums(out, sums, before=None):
    for k in range(3):
        value = total([found[k] for found in sums])
        if before is not None:
            value = value + before[8 * k : 8 * k + 8, :]
        out[8 * k : 8 * k + 8, :] = value


tile = 256


def home_kernel(scales, spot, left, right, weights, sums_out, kept):
    kept[...] = right[...]
    rows, columns = left.shape[0], right.shape[0]
    sums = []
    for start in range(0, rows, tile):
        here = pl.ds(start, tile)
        row = lax.broadcasted_iota(jnp.int32, (tile, 1), 0) + (start - spot[0])
        row = jnp.where((row >= 0) & (row < piece), row, -1)
        column = lax.broadcasted_iota(jnp.int32, (1, columns), 1) - spot[1]
        same = row == jnp.where(column >= 0, column, -2)
        product = pair_product(left[here, :], right[...])
        weights[here, :], found = pair_terms(product, scales[0], scales[1], same)
        sums.append(found)
    write_sums(sums_out, sums)


def own_kernel(scales, left, t0, t1, t2, t3, home, home_sums, back, weights, right, sums_out):
    rows, part = left.shape[0], t0.shape[0]
    for k, ref in enumerate((t0, t1, t2, t3)):
        right[k * part : (k + 1) * part, :] = ref[...]
    sums = []
    products = [pair_product(left[k : k + tile, :], right[part:, :]) for k in range(0, rows, tile)]
    for start in range(0, rows, tile):
        here = pl.ds(start, tile)
        value, found = pair_terms(products[start // tile], scales[0], scales[1])
        weights[here, :part] = home[here, :]
        weights[here, part:] = value
        back[here, :] = jnp.dot(
            weights[here, :], right[...], preferred_element_type=jnp.float32
        ).astype(jnp.bfloat16)
        sums.append(found)
    write_sums(sums_out, sums, home_sums)


def other_kernel(scales, left, right, own_sums, back, weights, sums_out):
    sums = []
    rows = left.shape[0]
    products = [pair_product(left[k : k + tile, :], right[...]) for k in range(0, rows, tile)]
    for start in range(0, rows, tile):
        here = pl.ds(start, tile)
        value, found = pair_terms(products[start // tile], scales[0], scales[1])
        weights[here, :] = value
        back[here, :] = jnp.dot(
            value, right[...], preferred_element_type=jnp.float32
        ).astype(jnp.bfloat16)
        sums.append(found)
    row = lax.broadcasted_iota(jnp.int32, (8, lanes), 0)
    value = jnp.zeros((8, lanes), jnp.float32)
    for k in range(3):
        found = total([s[k] for s in sums]) + own_sums[8 * k : 8 * k + 8, :]
        value = jnp.where(row == k, jnp.sum(found, axis=0, keepdims=True), value)
    carry = carry_of(value)
    sums_out[...] = carry
    back[rows:, :lanes] = carry.astype(jnp.bfloat16)
    back[rows:, lanes:] = jnp.zeros((carry_rows, back.shape[1] - lanes), jnp.bfloat16)


def text_kernel(own_weights, other_weights, own_left, other_left, *backs):
    contract = (((0,), (0,)), ((), ()))
    part = backs[0].shape[0]
    value = lax.dot_general(
        own_weights[...], own_left[...], contract, preferred_element_type=jnp.float32
    ) + lax.dot_general(
        other_weights[...], other_left[...], contract, preferred_element_type=jnp.float32
    )
    for k, out in enumerate(backs):
        out[...] = value[k * part : (k + 1) * part].astype(jnp.bfloat16)


def three_parts(value):
    high = value.astype(jnp.bfloat16).astype(jnp.float32)
    middle = (value - high).astype(jnp.bfloat16).astype(jnp.float32)
    return high, middle, value - high - middle


def carry_of(value):
    parts = three_parts(jnp.sum(value, axis=1, keepdims=True))
    lane = lax.broadcasted_iota(jnp.int32, (8, lanes), 1)
    carry = jnp.zeros((8, lanes), jnp.float32)
    for k in range(3):
        carry = jnp.where(lane == k, parts[k], carry)
    return jnp.concatenate([carry, jnp.zeros((8, lanes), jnp.float32)], axis=0)


def combine_kernel(own, given, sums, out):
    count, all_rows, _ = out.shape
    block = own.shape[0] // count
    carry = sums[...] + wide(given, pl.ds(own.shape[0], carry_rows), pl.ds(0, lanes))
    carry = carry_of(carry[:8]).astype(jnp.bfloat16)
    for k in range(count):
        rows = pl.ds(k * block, block)
        for t in range(tiles):
            columns = pl.ds(t * lanes, lanes)
            value = wide(own, rows, columns) + wide(given, rows, columns)
            out[k, t * block : (t + 1) * block, :] = value.astype(jnp.bfloat16)
        out[k, tiles * block : all_rows, :] = carry


def grads_of(units, inverse, grads):
    along = jnp.sum(total([u * g for u, g in zip(units, grads)]), axis=1, keepdims=True)
    return [(g - u * along) * inverse for u, g in zip(units, grads)]


def image_finish_kernel(place, arrived, backs, out):
    group = lane_group()
    count = backs.shape[0]
    heads = arrived.shape[0] // strips
    block = heads * piece
    tail = pl.ds(tiles * block, carry_rows)
    carry = carry_of(total([wide(backs, k, tail, slice(None)) for k in range(count)])[:8])[:8]
    for h in range(heads):
        units, inverse = image_units(place, arrived, h, group)
        grads = []
        for t in range(tiles):
            rows = pl.ds(t * block + h * piece, piece)
            grads.append(total([wide(backs, k, rows, slice(None)) for k in range(count)]))
        final = grads_of(units, inverse, grads)
        for s in range(strips):
            last = jnp.zeros((8, lanes), jnp.float32)
            for g in range(4):
                turn = rest * (g - s) % lanes
                rows = final[tiles - 1][8 * g : 8 * g + 8]
                moved = pltpu.roll(rows, turn, 1) if turn else rows
                last = jnp.where(group == g, moved, last)
            chunk = jnp.concatenate([carry, final[2 * s], final[2 * s + 1], last], axis=0)
            out[h * strips + strip_at(place, s)] = chunk.astype(jnp.bfloat16)


def text_finish_kernel(p0, p1, p2, p3, b0, b1, b2, b3, *outs):
    units, inverse = text_units((p0, p1, p2, p3))
    grads = []
    for t in range(tiles):
        columns = pl.ds(t * lanes, lanes)
        grads.append(total([wide(b, slice(None), columns) for b in (b0, b1, b2, b3)]))
    final = grads_of(units, inverse, grads)
    last = final[tiles - 1].T.astype(jnp.bfloat16)
    for s, out in enumerate(outs):
        out[:lanes, :] = final[2 * s].T.astype(jnp.bfloat16)
        out[lanes : 2 * lanes, :] = final[2 * s + 1].T.astype(jnp.bfloat16)
        out[2 * lanes :, :] = last[s * rest : (s + 1) * rest]


def text_last_kernel(g0, g1, g2, g3, out):
    value = total([wide(g, slice(None)) for g in (g0, g1, g2, g3)])
    out[...] = value.astype(jnp.bfloat16)


def image_last_kernel(arrived, out):
    values = [wide(arrived, d) for d in range(arrived.shape[0])]
    heads = len(values) // strips
    found = []
    for k in range(strips):
        chunk = total([values[h * strips + k][8:] for h in range(heads)])
        last = chunk[2 * piece :]
        groups = [last] + [pltpu.roll(last, lanes - rest * g, 1) for g in range(1, 4)]
        last = jnp.concatenate(groups, axis=0)
        found.append((chunk[:piece], chunk[piece : 2 * piece], last))
    for t in range(3):
        rows = jnp.concatenate([f[t] for f in found], axis=0).T
        count = lanes if t < 2 else rest
        out[t * lanes : t * lanes + count, :] = rows[:count].astype(jnp.bfloat16)


def sums_kernel(arrived, out):
    value = total([arrived[d].astype(jnp.float32)[:8] for d in range(arrived.shape[0])])
    value = jnp.sum(value, axis=1, keepdims=True)
    for k in range(out.shape[0]):
        out[k] = jnp.broadcast_to(value, out.shape[1:])


def swap_core(value):
    return lax.ppermute(value, "core", [(0, 1), (1, 0)])


def shift(value, axis, k):
    count = lax.axis_size(axis)
    return lax.ppermute(value, axis, [(i, (i + k) % count) for i in range(count)])


def shards(image, text, log_temp, bias):
    rows, strip = image.shape
    x_count, y_count, zh_count = (lax.axis_size(name) for name in ("x", "y", "zh"))
    z_count = zh_count * strips
    width = strip * strips
    block = zh_count * piece
    count = x_count * block
    zh, x, zl = (lax.axis_index(name).astype(jnp.int32) for name in ("zh", "x", "zl"))
    scale = jnp.exp(log_temp)
    scales = jnp.stack([scale, bias])
    place = zl.reshape(1)
    spot = jnp.stack([x * block + zh * piece, zl * piece])
    f32 = jnp.float32

    (packed,) = call(pack_kernel, [shape((z_count, chunk_rows, lanes))], "pack", [image.T])
    (kept,) = call(keep_kernel, [shape((strip, rows))], "keep", [text.T])
    parts = [kept] + [shift(text.T, "zl", k) for k in range(1, strips)]
    arrived = lax.all_to_all(packed, ("zh", "zl"), 0, 0)
    (home_text,) = call(text_unit_kernel, [shape((block, width))], "text_unit", parts, flops=400 * count * block * width)
    texts = [shift(home_text, "y", k) for k in range(1, y_count)]
    (units,) = call(
        image_unit_kernel,
        [shape((x_count, block, width))],
        "image_unit",
        [arrived],
        scalars=[place],
        after=[scales, spot, kept],
    )
    image_rows = lax.all_to_all(units, "x", 0, 0).reshape(count, width)
    other_rows = swap_core(image_rows)

    columns = y_count * block
    area = count * columns
    home_weights, home_sums, home_text = call(
        home_kernel,
        [shape((count, block)), shape((24, lanes), f32), shape((block, width))],
        "home",
        [image_rows, home_text],
        scalars=[scales, spot],
        flops=200 * count * block * width,
    )
    own_back, own_weights, right, own_sums = call(
        own_kernel,
        [
            shape((count, width)),
            shape((count, columns)),
            shape((columns, width)),
            shape((24, lanes), f32),
        ],
        "own",
        [image_rows, home_text] + texts + [home_weights, home_sums],
        scalars=[scales],
        flops=4 * area * width,
        special=2 * area,
    )
    other_back, other_weights, sums = call(
        other_kernel,
        [
            shape((count + carry_rows, width)),
            shape((count, columns)),
            shape((carry_rows, lanes), f32),
        ],
        "other",
        [other_rows, right, own_sums],
        scalars=[scales],
        flops=4 * area * width,
        special=2 * area,
    )
    given_back = swap_core(other_back)
    text_backs = call(
        text_kernel,
        [shape((block, width))] * y_count,
        "text_back",
        [own_weights, other_weights, image_rows, other_rows],
        flops=4 * area * width,
    )
    (combined,) = call(
        combine_kernel,
        [shape((x_count, tiles * block + carry_rows, lanes))],
        "combine",
        [own_back, given_back, sums],
        after=text_backs[:1],
    )
    combined = lax.all_to_all(combined, "x", 0, 0)
    (finished,) = call(
        image_finish_kernel,
        [shape((z_count, sent_rows, lanes))],
        "image_finish",
        [arrived, combined],
        scalars=[place],
        flops=200 * count * block * width,
    )
    moved = [text_backs[0]] + [shift(text_backs[k], "y", -k) for k in range(1, y_count)]
    finished = lax.all_to_all(finished, ("zh", "zl"), 0, 0)
    text_parts = call(
        text_finish_kernel, [shape((strip, rows))] * strips, "text_finish", parts + moved, flops=200 * count * block * width
    )
    given = [text_parts[0]] + [shift(text_parts[k], "zl", -k) for k in range(1, strips)]
    (grad_text,) = call(text_last_kernel, [shape((strip, rows))], "text_last", given)
    (sums,) = call(sums_kernel, [shape((y_count, 8, lanes), f32)], "sums", [finished])
    (grad_image,) = call(image_last_kernel, [shape((strip, rows))], "image_last", [finished], after=[sums])
    sums = jnp.sum(lax.all_to_all(sums, "y", 0, 0), axis=0)
    pairs_count = rows * 4 * x_count * y_count * 2
    return (
        sums[0, 0] / pairs_count,
        grad_image.T,
        grad_text.T,
        scale * sums[1, 0] / pairs_count,
        sums[2, 0] / pairs_count,
    )


def solution(mesh):
    fine = Mesh(mesh.devices.reshape(4, 4, 4, 2, 4), ("zh", "x", "y", "core", "zl"))
    whole = P(("zh", "x", "y", "core"), "zl")
    return jax.shard_map(
        shards,
        mesh=fine,
        in_specs=(whole, whole, P(), P()),
        out_specs=(P(), whole, whole, P(), P()),
        check_vma=False,
    )
```

```python
import functools

import jax
import jax.numpy as jnp
from jax import lax
from jax.experimental import pallas as pl
from jax.experimental.pallas import tpu as pltpu
from jax.sharding import Mesh, PartitionSpec as P

epsilon = 1e-06
lanes = 128
piece = 32
strips = 4
rest = 32
chunk_rows = 72
carry_rows = 16
sent_rows = 80
tiles = 9
vmem = pl.BlockSpec(memory_space=pltpu.VMEM)
smem = pl.BlockSpec(memory_space=pltpu.SMEM)
anywhere = pl.BlockSpec(memory_space=pl.ANY)
limits = pltpu.CompilerParams(vmem_limit_bytes=16 * 1024 * 1024)


def shape(dims, dtype=jnp.bfloat16):
    return jax.ShapeDtypeStruct(tuple(dims), dtype)


def call(kernel, out_shape, name, operands, scalars=(), after=(), flops=0, special=0, scratch=(), out_specs=None):
    out_shape = tuple(out_shape)
    scalars, operands, after = tuple(scalars), tuple(operands), tuple(after)
    inputs = len(scalars) + len(operands)
    moved = sum(a.size * a.dtype.itemsize for a in operands + out_shape)

    def body(*refs):
        kernel(*refs[:inputs], *refs[inputs + len(after) :])

    return pl.pallas_call(
        body,
        out_shape=out_shape,
        in_specs=[smem] * len(scalars) + [vmem] * len(operands) + [anywhere] * len(after),
        out_specs=out_specs or (vmem,) * len(out_shape),
        scratch_shapes=list(scratch),
        compiler_params=limits,
        cost_estimate=pl.CostEstimate(flops=flops, bytes_accessed=moved, transcendentals=special),
        name=name,
    )(*scalars, *operands, *after)


def hold(value, after):
    def body(*refs):
        del refs

    return pl.pallas_call(
        body,
        out_shape=shape(value.shape, value.dtype),
        in_specs=[anywhere] * (1 + len(after)),
        out_specs=anywhere,
        input_output_aliases={0: 0},
        compiler_params=limits,
        name="hold",
    )(value, *after)


def total(values):
    return functools.reduce(lambda a, b: a + b, values)


def wide(ref, *index):
    return ref[index].astype(jnp.float32)


def lane_group():
    return lax.broadcasted_iota(jnp.int32, (8, lanes), 1) // rest


def pack_kernel(image, out):
    whole = wide(image, slice(None)).T
    for k in range(4):
        rows = whole[k * piece : (k + 1) * piece]
        last = rows[:, 2 * lanes :]
        last = jnp.concatenate([last[8 * g : 8 * g + 8] for g in range(4)], axis=1)
        chunk = jnp.concatenate([rows[:, :lanes], rows[:, lanes : 2 * lanes], last], axis=0)
        chunk = chunk.astype(jnp.bfloat16)
        for h in range(out.shape[0] // strips):
            out[h * strips + k] = chunk


def unpack_rows(chunks, group):
    found = []
    lasts = []
    for chunk in chunks:
        found += [chunk[:piece], chunk[piece : 2 * piece]]
        lasts.append(chunk[2 * piece :])
    last = []
    for g in range(4):
        value = jnp.zeros((8, lanes), jnp.float32)
        for s in range(strips):
            turn = rest * (s - g) % lanes
            moved = pltpu.roll(lasts[s], turn, 1) if turn else lasts[s]
            value = jnp.where(group == s, moved, value)
        last.append(value)
    found.append(jnp.concatenate(last, axis=0))
    return found


def units_of(found):
    inverse = lax.rsqrt(jnp.sum(total([t * t for t in found]), axis=1, keepdims=True) + epsilon)
    return [t * inverse for t in found], inverse


def strip_at(place, k):
    return lax.rem(place[0] + (strips - k), strips)


def image_units(place, arrived, h, group):
    chunks = [wide(arrived, h * strips + strip_at(place, k)) for k in range(strips)]
    return units_of(unpack_rows(chunks, group))


def image_unit_kernel(place, arrived, out, buffer, semaphores):
    group = lane_group()
    copies = []
    for h in range(arrived.shape[0] // strips):
        units, _ = image_units(place, arrived, h, group)
        rows = pl.ds(h * piece, piece)
        for t in range(tiles):
            buffer[rows, t * lanes : (t + 1) * lanes] = units[t].astype(jnp.bfloat16)
        for k in range(out.shape[0]):
            copies.append(
                pltpu.make_async_copy(buffer.at[rows], out.at[k, rows], semaphores.at[h, k])
            )
            copies[-1].start()
    for copy in copies:
        copy.wait()


def text_units(parts):
    rows = [wide(p, slice(None)).T for p in parts]
    found = []
    for r in rows:
        found += [r[:, :lanes], r[:, lanes : 2 * lanes]]
    found.append(jnp.concatenate([r[:, 2 * lanes :] for r in rows], axis=1))
    return units_of(found)


def keep_kernel(strip, out):
    out[...] = strip[...]


def text_unit_kernel(p0, p1, p2, p3, out):
    units, _ = text_units((p0, p1, p2, p3))
    for t in range(tiles):
        out[:, t * lanes : (t + 1) * lanes] = units[t].astype(jnp.bfloat16)


def fold(values):
    rows, columns = values.shape
    part = jnp.sum(values.reshape(rows // 8, 8, columns), axis=0)
    return total([part[:, c : c + lanes] for c in range(0, columns, lanes)])


def pair_product(left, right):
    return lax.dot_general(
        left, right, (((1,), (1,)), ((), ())), preferred_element_type=jnp.float32
    )


def pair_terms(product, scale, bias, same=None):
    logits = scale * product + bias
    if same is None:
        grown = jnp.exp(logits)
        slope = grown / (1.0 + grown)
    else:
        grown = jnp.exp(jnp.where(same, -logits, logits))
        share = grown / (1.0 + grown)
        slope = jnp.where(same, -share, share)
    quarter = product.shape[0] // 4
    a, b, c, d = (grown[k * quarter : (k + 1) * quarter, :] for k in range(4))
    ab = a + (b + a * b)
    cd = c + (d + c * d)
    sums = (fold(jnp.log1p(ab + (cd + ab * cd))), fold(slope * product), fold(slope))
    return (scale * slope).astype(jnp.bfloat16), sums


def write_sums(out, sums, before=None):
    for k in range(3):
        value = total([found[k] for found in sums])
        if before is not None:
            value = value + before[8 * k : 8 * k + 8, :]
        out[8 * k : 8 * k + 8, :] = value


tile = 256


def home_kernel(scales, spot, left, right, weights, sums_out, kept):
    kept[...] = right[...]
    rows, columns = left.shape[0], right.shape[0]
    sums = []
    for start in range(0, rows, tile):
        here = pl.ds(start, tile)
        row = lax.broadcasted_iota(jnp.int32, (tile, 1), 0) + (start - spot[0])
        row = jnp.where((row >= 0) & (row < piece), row, -1)
        column = lax.broadcasted_iota(jnp.int32, (1, columns), 1) - spot[1]
        same = row == jnp.where(column >= 0, column, -2)
        product = pair_product(left[here, :], right[...])
        weights[here, :], found = pair_terms(product, scales[0], scales[1], same)
        sums.append(found)
    write_sums(sums_out, sums)


def own_kernel(scales, left, t0, t1, t2, t3, home, home_sums, back, weights, right, sums_out):
    rows, part = left.shape[0], t0.shape[0]
    for k, ref in enumerate((t0, t1, t2, t3)):
        right[k * part : (k + 1) * part, :] = ref[...]
    sums = []
    products = [pair_product(left[k : k + tile, :], right[part:, :]) for k in range(0, rows, tile)]
    for start in range(0, rows, tile):
        here = pl.ds(start, tile)
        value, found = pair_terms(products[start // tile], scales[0], scales[1])
        weights[here, :part] = home[here, :]
        weights[here, part:] = value
        back[here, :] = jnp.dot(
            weights[here, :], right[...], preferred_element_type=jnp.float32
        ).astype(jnp.bfloat16)
        sums.append(found)
    write_sums(sums_out, sums, home_sums)


def other_kernel(scales, left, right, own_sums, back, weights, sums_out):
    sums = []
    rows = left.shape[0]
    products = [pair_product(left[k : k + tile, :], right[...]) for k in range(0, rows, tile)]
    for start in range(0, rows, tile):
        here = pl.ds(start, tile)
        value, found = pair_terms(products[start // tile], scales[0], scales[1])
        weights[here, :] = value
        back[here, :] = jnp.dot(
            value, right[...], preferred_element_type=jnp.float32
        ).astype(jnp.bfloat16)
        sums.append(found)
    row = lax.broadcasted_iota(jnp.int32, (8, lanes), 0)
    value = jnp.zeros((8, lanes), jnp.float32)
    for k in range(3):
        found = total([s[k] for s in sums]) + own_sums[8 * k : 8 * k + 8, :]
        value = jnp.where(row == k, jnp.sum(found, axis=0, keepdims=True), value)
    carry = carry_of(value)
    sums_out[...] = carry
    back[rows:, :lanes] = carry.astype(jnp.bfloat16)
    back[rows:, lanes:] = jnp.zeros((carry_rows, back.shape[1] - lanes), jnp.bfloat16)


def text_kernel(own_weights, other_weights, own_left, other_left, *backs):
    contract = (((0,), (0,)), ((), ()))
    part = backs[0].shape[0]
    value = lax.dot_general(
        own_weights[...], own_left[...], contract, preferred_element_type=jnp.float32
    ) + lax.dot_general(
        other_weights[...], other_left[...], contract, preferred_element_type=jnp.float32
    )
    for k, out in enumerate(backs):
        out[...] = value[k * part : (k + 1) * part].astype(jnp.bfloat16)


def three_parts(value):
    high = value.astype(jnp.bfloat16).astype(jnp.float32)
    middle = (value - high).astype(jnp.bfloat16).astype(jnp.float32)
    return high, middle, value - high - middle


def carry_of(value):
    parts = three_parts(jnp.sum(value, axis=1, keepdims=True))
    lane = lax.broadcasted_iota(jnp.int32, (8, lanes), 1)
    carry = jnp.zeros((8, lanes), jnp.float32)
    for k in range(3):
        carry = jnp.where(lane == k, parts[k], carry)
    return jnp.concatenate([carry, jnp.zeros((8, lanes), jnp.float32)], axis=0)


def combine_kernel(own, given, sums, out, buffer, semaphores):
    copies = []
    count, all_rows, _ = out.shape
    block = own.shape[0] // count
    carry = sums[...] + wide(given, pl.ds(own.shape[0], carry_rows), pl.ds(0, lanes))
    carry = carry_of(carry[:8]).astype(jnp.bfloat16)
    for k in range(count):
        rows = pl.ds(k * block, block)
        for t in range(tiles):
            columns = pl.ds(t * lanes, lanes)
            value = wide(own, rows, columns) + wide(given, rows, columns)
            buffer[k, t * block : (t + 1) * block, :] = value.astype(jnp.bfloat16)
        buffer[k, tiles * block : all_rows, :] = carry
        copies.append(pltpu.make_async_copy(buffer.at[k], out.at[k], semaphores.at[k]))
        copies[-1].start()
    for copy in copies:
        copy.wait()


def grads_of(units, inverse, grads):
    along = jnp.sum(total([u * g for u, g in zip(units, grads)]), axis=1, keepdims=True)
    return [(g - u * along) * inverse for u, g in zip(units, grads)]


def image_finish_kernel(place, arrived, backs, out):
    group = lane_group()
    count = backs.shape[0]
    heads = arrived.shape[0] // strips
    block = heads * piece
    tail = pl.ds(tiles * block, carry_rows)
    carry = carry_of(total([wide(backs, k, tail, slice(None)) for k in range(count)])[:8])[:8]
    for h in range(heads):
        units, inverse = image_units(place, arrived, h, group)
        grads = []
        for t in range(tiles):
            rows = pl.ds(t * block + h * piece, piece)
            grads.append(total([wide(backs, k, rows, slice(None)) for k in range(count)]))
        final = grads_of(units, inverse, grads)
        for s in range(strips):
            last = jnp.zeros((8, lanes), jnp.float32)
            for g in range(4):
                turn = rest * (g - s) % lanes
                rows = final[tiles - 1][8 * g : 8 * g + 8]
                moved = pltpu.roll(rows, turn, 1) if turn else rows
                last = jnp.where(group == g, moved, last)
            chunk = jnp.concatenate([carry, final[2 * s], final[2 * s + 1], last], axis=0)
            out[h * strips + strip_at(place, s)] = chunk.astype(jnp.bfloat16)


def text_finish_kernel(p0, p1, p2, p3, b0, b1, b2, b3, *outs):
    units, inverse = text_units((p0, p1, p2, p3))
    grads = []
    for t in range(tiles):
        columns = pl.ds(t * lanes, lanes)
        grads.append(total([wide(b, slice(None), columns) for b in (b0, b1, b2, b3)]))
    final = grads_of(units, inverse, grads)
    last = final[tiles - 1].T.astype(jnp.bfloat16)
    for s, out in enumerate(outs):
        out[:lanes, :] = final[2 * s].T.astype(jnp.bfloat16)
        out[lanes : 2 * lanes, :] = final[2 * s + 1].T.astype(jnp.bfloat16)
        out[2 * lanes :, :] = last[s * rest : (s + 1) * rest]


def text_last_kernel(g0, g1, g2, g3, out):
    value = total([wide(g, slice(None)) for g in (g0, g1, g2, g3)])
    out[...] = value.astype(jnp.bfloat16)


def image_last_kernel(arrived, out):
    values = [wide(arrived, d) for d in range(arrived.shape[0])]
    heads = len(values) // strips
    found = []
    for k in range(strips):
        chunk = total([values[h * strips + k][8:] for h in range(heads)])
        last = chunk[2 * piece :]
        groups = [last] + [pltpu.roll(last, lanes - rest * g, 1) for g in range(1, 4)]
        last = jnp.concatenate(groups, axis=0)
        found.append((chunk[:piece], chunk[piece : 2 * piece], last))
    for t in range(3):
        rows = jnp.concatenate([f[t] for f in found], axis=0).T
        count = lanes if t < 2 else rest
        out[t * lanes : t * lanes + count, :] = rows[:count].astype(jnp.bfloat16)


def sums_kernel(arrived, out):
    value = total([arrived[d].astype(jnp.float32)[:8] for d in range(arrived.shape[0])])
    value = jnp.sum(value, axis=1, keepdims=True)
    for k in range(out.shape[0]):
        out[k] = jnp.broadcast_to(value, out.shape[1:])


def swap_core(value):
    return lax.ppermute(value, "core", [(0, 1), (1, 0)])


def shift(value, axis, k):
    count = lax.axis_size(axis)
    return lax.ppermute(value, axis, [(i, (i + k) % count) for i in range(count)])


def shards(image, text, log_temp, bias):
    rows, strip = image.shape
    x_count, y_count, zh_count = (lax.axis_size(name) for name in ("x", "y", "zh"))
    z_count = zh_count * strips
    width = strip * strips
    block = zh_count * piece
    count = x_count * block
    zh, x, zl = (lax.axis_index(name).astype(jnp.int32) for name in ("zh", "x", "zl"))
    scale = jnp.exp(log_temp)
    scales = jnp.stack([scale, bias])
    place = zl.reshape(1)
    spot = jnp.stack([x * block + zh * piece, zl * piece])
    f32 = jnp.float32

    (packed,) = call(pack_kernel, [shape((z_count, chunk_rows, lanes))], "pack", [image.T])
    (kept,) = call(keep_kernel, [shape((strip, rows))], "keep", [text.T])
    parts = [kept] + [shift(text.T, "zl", k) for k in range(1, strips)]
    arrived = lax.all_to_all(packed, ("zh", "zl"), 0, 0)
    (home_text,) = call(text_unit_kernel, [shape((block, width))], "text_unit", parts, flops=400 * count * block * width)
    texts = [shift(home_text, "y", k) for k in range(1, y_count)]
    (units,) = call(
        image_unit_kernel,
        [shape((x_count, block, width))],
        "image_unit",
        [arrived],
        scalars=[place],
        after=[scales, spot, kept],
        scratch=[
            pltpu.VMEM((block, width), jnp.bfloat16),
            pltpu.SemaphoreType.DMA((zh_count, x_count)),
        ],
        out_specs=(anywhere,),
    )
    image_rows = lax.all_to_all(units, "x", 0, 0).reshape(count, width)
    other_rows = swap_core(image_rows)

    columns = y_count * block
    area = count * columns
    home_weights, home_sums, home_text = call(
        home_kernel,
        [shape((count, block)), shape((24, lanes), f32), shape((block, width))],
        "home",
        [image_rows, home_text],
        scalars=[scales, spot],
        flops=200 * count * block * width,
    )
    own_back, own_weights, right, own_sums = call(
        own_kernel,
        [
            shape((count, width)),
            shape((count, columns)),
            shape((columns, width)),
            shape((24, lanes), f32),
        ],
        "own",
        [image_rows, home_text] + texts + [home_weights, home_sums],
        scalars=[scales],
        flops=4 * area * width,
        special=2 * area,
    )
    other_back, other_weights, sums = call(
        other_kernel,
        [
            shape((count + carry_rows, width)),
            shape((count, columns)),
            shape((carry_rows, lanes), f32),
        ],
        "other",
        [other_rows, right, own_sums],
        scalars=[scales],
        flops=4 * area * width,
        special=2 * area,
    )
    given_back = swap_core(other_back)
    text_backs = call(
        text_kernel,
        [shape((block, width))] * y_count,
        "text_back",
        [own_weights, other_weights, image_rows, other_rows],
        flops=4 * area * width,
    )
    (combined,) = call(
        combine_kernel,
        [shape((x_count, tiles * block + carry_rows, lanes))],
        "combine",
        [own_back, given_back, sums],
        after=text_backs[:1],
        scratch=[
            pltpu.VMEM((x_count, tiles * block + carry_rows, lanes), jnp.bfloat16),
            pltpu.SemaphoreType.DMA((x_count,)),
        ],
        out_specs=(anywhere,),
    )
    combined = lax.all_to_all(combined, "x", 0, 0)
    (finished,) = call(
        image_finish_kernel,
        [shape((z_count, sent_rows, lanes))],
        "image_finish",
        [arrived, combined],
        scalars=[place],
        flops=200 * count * block * width,
    )
    moved = [text_backs[0]] + [shift(text_backs[k], "y", -k) for k in range(1, y_count)]
    finished = lax.all_to_all(finished, ("zh", "zl"), 0, 0)
    text_parts = call(
        text_finish_kernel, [shape((strip, rows))] * strips, "text_finish", parts + moved, flops=200 * count * block * width
    )
    given = [text_parts[0]] + [shift(text_parts[k], "zl", -k) for k in range(1, strips)]
    (grad_text,) = call(text_last_kernel, [shape((strip, rows))], "text_last", given)
    (sums,) = call(sums_kernel, [shape((y_count, 8, lanes), f32)], "sums", [finished])
    (grad_image,) = call(image_last_kernel, [shape((strip, rows))], "image_last", [finished], after=[sums])
    sums = jnp.sum(lax.all_to_all(sums, "y", 0, 0), axis=0)
    pairs_count = rows * 4 * x_count * y_count * 2
    return (
        sums[0, 0] / pairs_count,
        grad_image.T,
        grad_text.T,
        scale * sums[1, 0] / pairs_count,
        sums[2, 0] / pairs_count,
    )


def solution(mesh):
    fine = Mesh(mesh.devices.reshape(4, 4, 4, 2, 4), ("zh", "x", "y", "core", "zl"))
    whole = P(("zh", "x", "y", "core"), "zl")
    return jax.shard_map(
        shards,
        mesh=fine,
        in_specs=(whole, whole, P(), P()),
        out_specs=(P(), whole, whole, P(), P()),
        check_vma=False,
    )
```
